32 devices in a mesh: groups: 2 (over y), space: 4 (over z), wave: 4 (over x, core).
Axes of the slice: x: 2, y: 2, z: 4, core: 2. Of those that a mesh axis runs over, the one named last changes fastest.
Arguments:
- density: float32 [512, 16, 128], P(('groups', 'space')), parts along dimension 0, may hold values from -6 to 6
- even_taps: float32 [15], replicated, may hold values from -1.5 to 1.5
- odd_taps: float32 [15], replicated, may hold values from -1.5 to 1.5
- low_taps: float32 [15], replicated, may hold values from -1.5 to 1.5
- wavelets: int32 [40, 2], replicated, may hold values from 0 to 2, as said below
- pairs: int32 [32, 2], replicated, may hold values from -1 to 39, as said below
Outputs:
- second: float32 [32, 256, 8, 64], P('wave', ('groups', 'space')), parts along dimension 1
The draws below stay inside these ranges and needn't reach their ends.
There are 2 independent parts, one for each index of `groups`. The reference program is written for one: setup_inputs(seed, part) draws one part's arguments, and reference() takes and returns one part's arrays. A program takes and returns all parts, laid end to end along the dimension named above; an argument that names none is the same for every part. Nothing has to cross between parts.
Inputs may be any that keep to these rules, and one draw needn't show every extreme that they name: `wavelets`: column 0 is a dilation level below 3, column 1 an orientation 0, 1 or 2. Rows below 5 have levels below 2; the last row has level 2. `pairs`: the slots form aligned blocks of 8 rows, one block for each index of wave. In every block the live rows come first and at least one is live; some block has all 8 rows live. A live row holds a first-order field below 5 and a wavelet row of 5 or more whose level is above that field's level; a dead row is (-1, 0).
All inputs are finite; a program needn't handle non-finite values.
Results may differ from the reference program's by a relative error of at most 0.0003.
Values sent between devices are 32-bit elements; how exact they have to be, the bound alone decides.
No kernel may reach another device: no remote copies, remote signals or barrier semaphores. Data moves between devices by JAX's collectives and lax.ppermute only.
A program may use at most 64 MiB of HBM per device.

```python
import jax
import jax.numpy as jnp
from jax import lax

NY = 16
NZ = 128
PAIR_DEV = 8
NFIRST = 5
NWAVE = 40
TAPS = 15
LEVELS = 3
REACH = 28
NX = 256
PAIRS = 32


def wavelet_table(key):
    first_levels = jax.random.randint(jax.random.fold_in(key, 11), (NWAVE,), 0, LEVELS - 1)
    other_levels = jax.random.randint(jax.random.fold_in(key, 16), (NWAVE,), 0, LEVELS)
    rows = jnp.arange(NWAVE)
    level_draw = jnp.where(rows < NFIRST, first_levels, other_levels)
    orient_draw = jax.random.randint(jax.random.fold_in(key, 12), (NWAVE,), 0, 3)
    level_draw = level_draw.at[NWAVE - 1].set(LEVELS - 1)
    orient_draw = orient_draw.at[0].set(2)
    return jnp.stack([level_draw, orient_draw], axis=1).astype(jnp.int32)


def draw_wavelets(key, part):
    return wavelet_table(key)


def draw_pairs(key, part):
    table = wavelet_table(key)
    levels = table[:, 0]
    block_count = PAIRS // PAIR_DEV
    ranking = jax.random.permutation(jax.random.fold_in(key, 13), block_count)
    heights = ranking + 1
    squared = block_count * block_count
    live_counts = jnp.maximum(1, (PAIR_DEV * heights * heights + squared - 1) // squared)
    positions = jnp.arange(PAIRS)
    slot_in_block = positions % PAIR_DEV
    block_of = positions // PAIR_DEV
    live_flags = slot_in_block < live_counts[block_of]
    field_draw = jax.random.randint(jax.random.fold_in(key, 14), (PAIRS,), 0, NFIRST)
    field_levels = levels[field_draw]
    rows = jnp.arange(NWAVE)
    eligible = (rows[None, :] >= NFIRST) & (levels[None, :] > field_levels[:, None])
    scores = jax.random.randint(jax.random.fold_in(key, 15), (PAIRS, NWAVE), 0, 1 << 20) * 64 + rows[None, :]
    scores = jnp.where(eligible, scores, -1)
    wave_draw = jnp.argmax(scores, axis=1).astype(jnp.int32)
    busiest = (ranking[block_of] == block_count - 1) & (slot_in_block == 0)
    wave_draw = jnp.where(busiest, NWAVE - 1, wave_draw)
    first_col = jnp.where(live_flags, field_draw, -1)
    second_col = jnp.where(live_flags, wave_draw, 0)
    return jnp.stack([first_col, second_col], axis=1).astype(jnp.int32)


def block_scale(key, shape, pieces, low, high):
    gain = 1.0
    for dim, shards_of in pieces:
        steps = jax.random.uniform(jax.random.fold_in(jax.random.fold_in(key, 6), dim), (shards_of,), jnp.float32, low / len(pieces), high / len(pieces))
        gain = gain * jnp.repeat(jnp.exp(steps), shape[dim] // shards_of).reshape((-1,) + (1,) * (len(shape) - 1 - dim))
    return gain


def centred(key, shape, scale, reach, shards=(), kind=jnp.bfloat16):
    result = scale * jax.random.normal(key, shape, jnp.float32)
    if shards:
        result = result * block_scale(key, shape, shards, -0.22, 0.18)
    return jnp.clip(result, -reach, reach).astype(kind)


def setup_inputs(seed: int = 0, part: int = 0) -> dict:
    key_of = jax.random.split(jax.random.key(seed), 7)
    own_keys = jax.random.split(jax.random.fold_in(key_of[6], part), 7)
    density = centred(own_keys[0], (NX, NY, NZ), 1.0, 6.0, ((0, 4),), jnp.float32)
    even_taps = centred(key_of[1], (TAPS,), TAPS ** -0.5, 1.5, (), jnp.float32)
    odd_taps = centred(key_of[2], (TAPS,), TAPS ** -0.5, 1.5, (), jnp.float32)
    low_taps = centred(key_of[3], (TAPS,), TAPS ** -0.5, 1.5, (), jnp.float32)
    wavelets = draw_wavelets(jax.random.fold_in(key_of[6], 71), part)
    pairs = draw_pairs(jax.random.fold_in(key_of[6], 71), part)
    return {"density": density, "even_taps": even_taps, "odd_taps": odd_taps, "low_taps": low_taps, "wavelets": wavelets, "pairs": pairs}


def widen(values_in, direction, margin):
    widths = [(0, 0)] * values_in.ndim
    widths[direction] = (margin, margin)
    return jnp.pad(values_in, widths)

def along(values_in, weights, dilation, direction, length_out):
    centre = weights.shape[0] // 2
    accumulated = None
    for tap_index in range(weights.shape[0]):
        offset = REACH + (tap_index - centre) * dilation
        shifted = lax.dynamic_slice_in_dim(values_in, offset, length_out, direction)
        weighted = weights[tap_index] * shifted
        accumulated = weighted if accumulated is None else accumulated + weighted
    return accumulated

def respond(values_in, level_index, orient, filters, length_out):
    even_taps, odd_taps, low_taps = filters
    dilation = jnp.left_shift(jnp.int32(1), level_index.astype(jnp.int32))

    def make_branch(band):

        def respond_oriented(source):
            signals = (source,)
            for direction in range(3):
                if direction == 0:
                    extent = length_out
                    prepared = signals
                else:
                    extent = source.shape[direction]
                    prepared = tuple((widen(signal, direction, REACH) for signal in signals))
                if direction == band:
                    signals = (along(prepared[0], even_taps, dilation, direction, extent), along(prepared[0], odd_taps, dilation, direction, extent))
                else:
                    signals = tuple((along(signal, low_taps, dilation, direction, extent) for signal in prepared))
            real_part, imag_part = signals
            return jnp.sqrt(real_part * real_part + imag_part * imag_part + 1e-06)
        return respond_oriented
    return lax.switch(orient.astype(jnp.int32), [make_branch(0), make_branch(1), make_branch(2)], values_in)

def reference(density, even_taps, odd_taps, low_taps, wavelets, pairs):
    filters = (even_taps, odd_taps, low_taps)
    wide_density = widen(density, 0, REACH)
    firsts = jnp.stack([respond(wide_density, wavelets[field_index, 0], wavelets[field_index, 1], filters, NX) for field_index in range(NFIRST)])
    first_wide = widen(firsts, 1, REACH)

    def one_pair(pair_row):
        source = lax.dynamic_index_in_dim(first_wide, jnp.maximum(pair_row[0], 0), 0, keepdims=False)

        def work_pair(values_in):
            level_index = wavelets[pair_row[1], 0]
            orient = wavelets[pair_row[1], 1]
            return respond(values_in, level_index, orient, filters, NX)[::2, ::2, ::2]

        def skip_pair(values_in):
            return jnp.zeros((NX // 2, NY // 2, NZ // 2), values_in.dtype)
        return lax.cond(pair_row[0] >= 0, work_pair, skip_pair, source)
    return lax.map(one_pair, pairs)
```

```python
import functools

import jax
import jax.numpy as jnp
from jax import lax
from jax.experimental import pallas as pl
from jax.experimental.pallas import tpu as pltpu
from jax.sharding import PartitionSpec as P

NFIRST = 5
TAPS = 15
HALF = 7
HALO = 42
ROWS = 64
EPS = 1e-6
F32 = jnp.float32
BF16 = jnp.bfloat16
LOW, EVEN, ODD, BOTH = 0, 1, 2, 3


def split(value):
    high = value.astype(BF16)
    return high, (value - high.astype(F32)).astype(BF16)


def dot(a, b):
    return jnp.dot(a, b, preferred_element_type=F32)


def lanes(shape):
    return lax.broadcasted_iota(jnp.int32, shape, 1)


def modulus(value):
    squares = value * value
    return jnp.sqrt(squares + pltpu.roll(squares, 64, 1) + EPS)


def banded(taps_ref, height, numerator, dilation):
    offset = numerator((height, 128))
    low = jnp.zeros((height, 128), F32)
    both = jnp.zeros((height, 128), F32)
    for t in range(TAPS):
        here = offset == (t - HALF) * dilation
        low = jnp.where(here, taps_ref[LOW, t][0:1], low)
        both = jnp.where(here, taps_ref[BOTH, t][0:1], both)
    return low, both


def body(
    even_s, odd_s, low_s, wave_s, pairs_s, before_ref, own_ref, after_ref, out_ref,
    grid_ref, taps_ref, w_first, w_zero, w_second, lhs_low, lhs_both, z_ref, lhs_second, z2_ref, sems,
):
    tile_rows = own_ref.shape[0]
    rank = lax.axis_index("space")
    total = lax.axis_size("space") * tile_rows
    base = lax.axis_index("wave") * out_ref.shape[0]
    slots = out_ref.shape[0]
    places = ((before_ref, 0), (own_ref, HALO), (after_ref, HALO + tile_rows))
    copies = []
    for n, (source, start) in enumerate(places):
        copies.append(pltpu.make_async_copy(source, grid_ref.at[pl.ds(start, source.shape[0])], sems.at[n]))
    for copy in copies:
        copy.start()

    tile = (8, 128)
    left = lanes(tile) < 64
    for t in range(TAPS):
        even = jnp.full(tile, even_s[t], F32)
        odd = jnp.full(tile, odd_s[t], F32)
        taps_ref[LOW, t] = jnp.full(tile, low_s[t], F32)
        taps_ref[EVEN, t] = even
        taps_ref[ODD, t] = odd
        taps_ref[BOTH, t] = jnp.where(left, even, odd)

    def row(shape):
        return lax.broadcasted_iota(jnp.int32, shape, 0)

    for level in range(2):
        low, both = banded(taps_ref, 128, lambda s: row(s) - 2 * (lanes(s) % 64), 1 << level)
        for kind, matrix in enumerate((low, both)):
            high, rest = split(matrix)
            w_first[level, kind, 0:128, 0:128] = high
            w_first[level, kind, 128:256, 0:128] = high
            w_first[level, kind, 0:128, 128:256] = rest
            w_first[level, kind, 128:256, 128:256] = jnp.zeros((128, 128), BF16)
        inner = lanes((128, 128)) < 64
        for part, keep in enumerate((inner, ~inner)):
            high, rest = split(jnp.where(keep, low, 0.0))
            first = 256 * part
            w_zero[level, first:first + 128, 0:128] = high
            w_zero[level, first + 128:first + 256, 0:128] = high
            w_zero[level, first:first + 128, 128:256] = rest
            w_zero[level, first + 128:first + 256, 128:256] = jnp.zeros((128, 128), BF16)
        low, both = banded(taps_ref, 64, lambda s: row(s) - lanes(s) % 64, 1 << level)
        for kind, matrix in enumerate((low, both)):
            high, rest = split(matrix)
            w_second[2 * level + kind, 0:64] = high
            w_second[2 * level + kind, 64:128] = high
            w_second[2 * level + kind, 128:192] = rest
            w_second[2 * level + kind, 192:256] = jnp.zeros((64, 128), BF16)

    need = [[False] * 3 for _ in range(2)]
    for p in range(slots):
        field = pairs_s[base + p, 0]
        safe = jnp.maximum(field, 0)
        level, orient = wave_s[safe, 0], wave_s[safe, 1]
        for a in range(2):
            for b in range(3):
                need[a][b] = need[a][b] | ((field >= 0) & (level == a) & (orient == b))

    for copy in copies:
        copy.wait()

    flat = grid_ref.reshape(grid_ref.shape[0] * 16, 128)

    def x_pass(level, kind, store):
        def step(c, carry):
            taps = [taps_ref[kind, t] for t in range(TAPS)]
            halves = []
            for h in range(2 if level == 0 else 1):
                sums = [None] * 16
                if level == 0:
                    first, reach = c * 32 + HALF, 2 * 15 + TAPS
                else:
                    first, reach = c * 32, 16 + TAPS - 1
                for r in range(reach):
                    if level == 0:
                        value = flat[pl.ds(pl.multiple_of((first + r) * 16 + 8 * h, 8), 8), :]
                    else:
                        value = flat[pl.ds(pl.multiple_of((first + 2 * r) * 16, 8), 8, stride=2), :]
                    for i in range(16):
                        t = r - 2 * i if level == 0 else r - i
                        if 0 <= t < TAPS:
                            term = taps[t] * value
                            sums[i] = term if sums[i] is None else sums[i] + term
                halves.append(sums)
            for i in range(16 if level == 0 else 8):
                if level == 0:
                    joined = jnp.concatenate([halves[0][i], halves[1][i]], axis=0)
                else:
                    joined = jnp.concatenate([halves[0][2 * i], halves[0][2 * i + 1]], axis=0)
                per = 256 if level == 0 else 128
                store(pl.multiple_of(c * per + i * 16, 16), *split(joined))
            return carry

        lax.fori_loop(0, 4, step, 0)

    def to_low(at, high, rest):
        lhs_low[pl.ds(at, 16), 0:128] = high
        lhs_low[pl.ds(at, 16), 128:256] = rest

    def to_even(at, high, rest):
        lhs_both[pl.ds(at, 16), 0:128] = high
        lhs_both[pl.ds(at, 16), 128:256] = rest

    def to_odd(at, high, rest):
        lhs_both[pl.ds(at, 16), 256:384] = high
        lhs_both[pl.ds(at, 16), 384:512] = rest

    sub = lax.broadcasted_iota(jnp.int32, tile, 0)

    def finish(level, orient):
        height = 16 if level == 0 else 8
        per = 16 * height
        if orient == 0:
            weights = w_zero[level]
        else:
            weights = w_first[level, orient - 1]
        source = lhs_both if orient == 0 else lhs_low
        taps = taps_ref.at[BOTH if orient == 1 else LOW]
        slot = level * 3 + orient
        for c in range(4):
            both = dot(source[c * per:(c + 1) * per, :], weights)
            z_ref[c * per:(c + 1) * per, :] = both[:, 0:128] + both[:, 128:256]
        for c in range(4):
            parts = []
            for h in range(2):
                values = [z_ref[pl.ds(c * per + h * 8 * height + y, 8, stride=height), :] for y in range(height)]
                i = c * 16 + h * 8 + sub
                x = rank * tile_rows - 28 + 2 * i
                inside = (x >= 0) & (x < total) & (i < 60)
                outs = []
                for j in range(8):
                    acc = None
                    for y in range(height):
                        t = y - (2 * j if level == 0 else j) + HALF
                        if 0 <= t < TAPS:
                            term = taps[t] * values[y]
                            acc = term if acc is None else acc + term
                    outs.append(jnp.where(inside, modulus(acc), 0.0))
                parts.append(outs)
            for j in range(8):
                joined = jnp.concatenate([parts[0][j], parts[1][j]], axis=0)
                high = joined.astype(BF16)
                wide = high.astype(F32)
                pair = jnp.where(lanes((16, 128)) < 64, wide, joined - wide).astype(BF16)
                lhs_second[slot, j * 64 + c * 16:j * 64 + c * 16 + 16, 0:128] = pair
                lhs_second[slot, j * 64 + c * 16:j * 64 + c * 16 + 16, 128:256] = high

    for level in range(2):
        @pl.when(need[level][0])
        def _():
            x_pass(level, EVEN, to_even)
            x_pass(level, ODD, to_odd)
            finish(level, 0)

        @pl.when(need[level][1] | need[level][2])
        def _():
            x_pass(level, LOW, to_low)

        for orient in (1, 2):
            @pl.when(need[level][orient])
            def _():
                finish(level, orient)

    def second(p, dilation, orient, slot):
        weights = w_second[(dilation - 1) * 2 + (orient == 2).astype(jnp.int32)]
        z2_ref[...] = dot(lhs_second[slot], weights)
        x_taps = taps_ref.at[jnp.where(orient == 0, BOTH, LOW)]
        y_taps = taps_ref.at[jnp.where(orient == 1, BOTH, LOW)]
        out = out_ref.at[p].reshape(out_ref.shape[1] * 8, 64)
        for c in range(4):
            rows = []
            for j in range(8):
                acc = None
                for t in range(TAPS):
                    start = j * 64 + c * 8 + 14 + (t - HALF) * dilation
                    term = x_taps[t] * z2_ref[start:start + 8, :]
                    acc = term if acc is None else acc + term
                rows.append(acc)
            for j in range(8):
                acc = None
                for y in range(8):
                    if (y - j) % dilation == 0 and abs(y - j) <= HALF * dilation:
                        term = y_taps[(y - j) // dilation + HALF] * rows[y]
                        acc = term if acc is None else acc + term
                out[pl.ds(c * 64 + j, 8, stride=8), :] = modulus(acc)[:, 0:64]

    def one_pair(p, carry):
        field, wavelet = pairs_s[base + p, 0], pairs_s[base + p, 1]
        live = field >= 0
        safe = jnp.maximum(field, 0)
        slot = wave_s[safe, 0] * 3 + wave_s[safe, 1]
        level, orient = wave_s[wavelet, 0], wave_s[wavelet, 1]
        for dilation in (1, 2):
            @pl.when(live & (level == dilation))
            def _():
                second(p, dilation, orient, slot)

        @pl.when(jnp.logical_not(live))
        def _():
            out_ref[p] = jnp.zeros(out_ref.shape[1:], F32)

        return carry

    lax.fori_loop(0, slots, one_pair, 0)


def shards(density, even_taps, odd_taps, low_taps, wavelets, pairs):
    tile_rows, ny, nz = density.shape
    count = lax.axis_size("space")
    up = [(i, i + 1) for i in range(count - 1)]
    down = [(j, i) for i, j in up]
    before = lax.ppermute(density[tile_rows - HALO:], "space", up)
    after = lax.ppermute(density[:HALO], "space", down)
    per_dev = pairs.shape[0] // lax.axis_size("wave")
    smem = pl.BlockSpec(memory_space=pltpu.SMEM)
    anywhere = pl.BlockSpec(memory_space=pl.ANY)
    return pl.pallas_call(
        body,
        out_shape=jax.ShapeDtypeStruct((per_dev, tile_rows // 2, ny // 2, nz // 2), F32),
        in_specs=[smem] * 5 + [anywhere] * 3,
        out_specs=pl.BlockSpec(memory_space=pltpu.VMEM),
        scratch_shapes=[
            pltpu.VMEM((160, 16, 128), F32),
            pltpu.VMEM((4, 16, 8, 128), F32),
            pltpu.VMEM((2, 2, 256, 256), BF16),
            pltpu.VMEM((2, 512, 256), BF16),
            pltpu.VMEM((4, 256, 128), BF16),
            pltpu.VMEM((1024, 256), BF16),
            pltpu.VMEM((1024, 512), BF16),
            pltpu.VMEM((1024, 128), F32),
            pltpu.VMEM((6, 512, 256), BF16),
            pltpu.VMEM((512, 128), F32),
            pltpu.SemaphoreType.DMA((3,)),
        ],
        compiler_params=pltpu.CompilerParams(vmem_limit_bytes=24 * 1024 * 1024),
    )(even_taps, odd_taps, low_taps, wavelets, pairs, before, density, after)


def solution(mesh):
    placed = (P(("groups", "space"), None, None), P(), P(), P(), P(), P())
    return jax.shard_map(
        shards,
        mesh=mesh,
        in_specs=placed,
        out_specs=P("wave", ("groups", "space"), None, None),
        check_vma=False,
    )
```

```python
import functools

import jax
import jax.numpy as jnp
from jax import lax
from jax.experimental import pallas as pl
from jax.experimental.pallas import tpu as pltpu
from jax.sharding import PartitionSpec as P

NFIRST = 5
TAPS = 15
HALF = 7
HALO = 42
ROWS = 64
EPS = 1e-6
F32 = jnp.float32
BF16 = jnp.bfloat16
LOW, EVEN, ODD, BOTH = 0, 1, 2, 3


def split(value):
    high = value.astype(BF16)
    return high, (value - high.astype(F32)).astype(BF16)


def dot(a, b):
    return jnp.dot(a, b, preferred_element_type=F32)


def lanes(shape):
    return lax.broadcasted_iota(jnp.int32, shape, 1)


def modulus(value):
    squares = value * value
    return jnp.sqrt(squares + pltpu.roll(squares, 64, 1) + EPS)


def banded(taps_ref, height, numerator, dilation):
    offset = numerator((height, 128))
    low = jnp.zeros((height, 128), F32)
    both = jnp.zeros((height, 128), F32)
    for t in range(TAPS):
        here = offset == (t - HALF) * dilation
        low = jnp.where(here, taps_ref[LOW, t][0:1], low)
        both = jnp.where(here, taps_ref[BOTH, t][0:1], both)
    return low, both


def body(
    even_s, odd_s, low_s, wave_s, pairs_s, got_ref, own_ref, other_ref, out_ref,
    grid_ref, taps_ref, w_first, w_zero, w_second, lhs_low, lhs_both, z_ref, lhs_second, z2_ref, sems,
):
    tile_rows = own_ref.shape[0]
    rank = lax.axis_index("space")
    total = lax.axis_size("space") * tile_rows
    base = lax.axis_index("wave") * out_ref.shape[0]
    slots = out_ref.shape[0]
    upper = lax.axis_index("wave") % 2
    far = HALO + tile_rows
    places = ((got_ref, (1 - upper) * far), (own_ref, HALO), (other_ref, upper * far))
    copies = []
    for n, (source, start) in enumerate(places):
        copies.append(pltpu.make_async_copy(source, grid_ref.at[pl.ds(start, source.shape[0])], sems.at[n]))
    for copy in copies:
        copy.start()

    tile = (8, 128)
    left = lanes(tile) < 64
    for t in range(TAPS):
        even = jnp.full(tile, even_s[t], F32)
        odd = jnp.full(tile, odd_s[t], F32)
        taps_ref[LOW, t] = jnp.full(tile, low_s[t], F32)
        taps_ref[EVEN, t] = even
        taps_ref[ODD, t] = odd
        taps_ref[BOTH, t] = jnp.where(left, even, odd)

    def row(shape):
        return lax.broadcasted_iota(jnp.int32, shape, 0)

    for level in range(2):
        low, both = banded(taps_ref, 128, lambda s: row(s) - 2 * (lanes(s) % 64), 1 << level)
        for kind, matrix in enumerate((low, both)):
            high, rest = split(matrix)
            w_first[level, kind, 0:128, 0:128] = high
            w_first[level, kind, 128:256, 0:128] = high
            w_first[level, kind, 0:128, 128:256] = rest
            w_first[level, kind, 128:256, 128:256] = jnp.zeros((128, 128), BF16)
        inner = lanes((128, 128)) < 64
        for part, keep in enumerate((inner, ~inner)):
            high, rest = split(jnp.where(keep, low, 0.0))
            first = 256 * part
            w_zero[level, first:first + 128, 0:128] = high
            w_zero[level, first + 128:first + 256, 0:128] = high
            w_zero[level, first:first + 128, 128:256] = rest
            w_zero[level, first + 128:first + 256, 128:256] = jnp.zeros((128, 128), BF16)
        low, both = banded(taps_ref, 64, lambda s: row(s) - lanes(s) % 64, 1 << level)
        for kind, matrix in enumerate((low, both)):
            high, rest = split(matrix)
            w_second[2 * level + kind, 0:64] = high
            w_second[2 * level + kind, 64:128] = high
            w_second[2 * level + kind, 128:192] = rest
            w_second[2 * level + kind, 192:256] = jnp.zeros((64, 128), BF16)

    need = [[False] * 3 for _ in range(2)]
    for p in range(slots):
        field = pairs_s[base + p, 0]
        safe = jnp.maximum(field, 0)
        level, orient = wave_s[safe, 0], wave_s[safe, 1]
        for a in range(2):
            for b in range(3):
                need[a][b] = need[a][b] | ((field >= 0) & (level == a) & (orient == b))

    for copy in copies:
        copy.wait()

    flat = grid_ref.reshape(grid_ref.shape[0] * 16, 128)

    def x_pass(level, kind, store):
        def step(c, carry):
            taps = [taps_ref[kind, t] for t in range(TAPS)]
            halves = []
            for h in range(2 if level == 0 else 1):
                sums = [None] * 16
                if level == 0:
                    first, reach = c * 32 + HALF, 2 * 15 + TAPS
                else:
                    first, reach = c * 32, 16 + TAPS - 1
                for r in range(reach):
                    if level == 0:
                        value = flat[pl.ds(pl.multiple_of((first + r) * 16 + 8 * h, 8), 8), :]
                    else:
                        value = flat[pl.ds(pl.multiple_of((first + 2 * r) * 16, 8), 8, stride=2), :]
                    for i in range(16):
                        t = r - 2 * i if level == 0 else r - i
                        if 0 <= t < TAPS:
                            term = taps[t] * value
                            sums[i] = term if sums[i] is None else sums[i] + term
                halves.append(sums)
            for i in range(16 if level == 0 else 8):
                if level == 0:
                    joined = jnp.concatenate([halves[0][i], halves[1][i]], axis=0)
                else:
                    joined = jnp.concatenate([halves[0][2 * i], halves[0][2 * i + 1]], axis=0)
                per = 256 if level == 0 else 128
                store(pl.multiple_of(c * per + i * 16, 16), *split(joined))
            return carry

        lax.fori_loop(0, 4, step, 0)

    def to_low(at, high, rest):
        lhs_low[pl.ds(at, 16), 0:128] = high
        lhs_low[pl.ds(at, 16), 128:256] = rest

    def to_even(at, high, rest):
        lhs_both[pl.ds(at, 16), 0:128] = high
        lhs_both[pl.ds(at, 16), 128:256] = rest

    def to_odd(at, high, rest):
        lhs_both[pl.ds(at, 16), 256:384] = high
        lhs_both[pl.ds(at, 16), 384:512] = rest

    sub = lax.broadcasted_iota(jnp.int32, tile, 0)

    def finish(level, orient):
        height = 16 if level == 0 else 8
        per = 16 * height
        if orient == 0:
            weights = w_zero[level]
        else:
            weights = w_first[level, orient - 1]
        source = lhs_both if orient == 0 else lhs_low
        taps = taps_ref.at[BOTH if orient == 1 else LOW]
        slot = level * 3 + orient
        for c in range(4):
            both = dot(source[c * per:(c + 1) * per, :], weights)
            z_ref[c * per:(c + 1) * per, :] = both[:, 0:128] + both[:, 128:256]
        for c in range(4):
            parts = []
            for h in range(2):
                values = [z_ref[pl.ds(c * per + h * 8 * height + y, 8, stride=height), :] for y in range(height)]
                i = c * 16 + h * 8 + sub
                x = rank * tile_rows - 28 + 2 * i
                inside = (x >= 0) & (x < total) & (i < 60)
                outs = []
                for j in range(8):
                    acc = None
                    for y in range(height):
                        t = y - (2 * j if level == 0 else j) + HALF
                        if 0 <= t < TAPS:
                            term = taps[t] * values[y]
                            acc = term if acc is None else acc + term
                    outs.append(jnp.where(inside, modulus(acc), 0.0))
                parts.append(outs)
            for j in range(8):
                joined = jnp.concatenate([parts[0][j], parts[1][j]], axis=0)
                high = joined.astype(BF16)
                wide = high.astype(F32)
                pair = jnp.where(lanes((16, 128)) < 64, wide, joined - wide).astype(BF16)
                lhs_second[slot, j * 64 + c * 16:j * 64 + c * 16 + 16, 0:128] = pair
                lhs_second[slot, j * 64 + c * 16:j * 64 + c * 16 + 16, 128:256] = high

    for level in range(2):
        @pl.when(need[level][0])
        def _():
            x_pass(level, EVEN, to_even)
            x_pass(level, ODD, to_odd)
            finish(level, 0)

        @pl.when(need[level][1] | need[level][2])
        def _():
            x_pass(level, LOW, to_low)

        for orient in (1, 2):
            @pl.when(need[level][orient])
            def _():
                finish(level, orient)

    def second(p, dilation, orient, slot):
        weights = w_second[(dilation - 1) * 2 + (orient == 2).astype(jnp.int32)]
        z2_ref[...] = dot(lhs_second[slot], weights)
        x_taps = taps_ref.at[jnp.where(orient == 0, BOTH, LOW)]
        y_taps = taps_ref.at[jnp.where(orient == 1, BOTH, LOW)]
        out = out_ref.at[p].reshape(out_ref.shape[1] * 8, 64)
        for c in range(4):
            rows = []
            for j in range(8):
                acc = None
                for t in range(TAPS):
                    start = j * 64 + c * 8 + 14 + (t - HALF) * dilation
                    term = x_taps[t] * z2_ref[start:start + 8, :]
                    acc = term if acc is None else acc + term
                rows.append(acc)
            for j in range(8):
                acc = None
                for y in range(8):
                    if (y - j) % dilation == 0 and abs(y - j) <= HALF * dilation:
                        term = y_taps[(y - j) // dilation + HALF] * rows[y]
                        acc = term if acc is None else acc + term
                out[pl.ds(c * 64 + j, 8, stride=8), :] = modulus(acc)[:, 0:64]

    def one_pair(p, carry):
        field, wavelet = pairs_s[base + p, 0], pairs_s[base + p, 1]
        live = field >= 0
        safe = jnp.maximum(field, 0)
        slot = wave_s[safe, 0] * 3 + wave_s[safe, 1]
        level, orient = wave_s[wavelet, 0], wave_s[wavelet, 1]
        for dilation in (1, 2):
            @pl.when(live & (level == dilation))
            def _():
                second(p, dilation, orient, slot)

        @pl.when(jnp.logical_not(live))
        def _():
            out_ref[p] = jnp.zeros(out_ref.shape[1:], F32)

        return carry

    lax.fori_loop(0, slots, one_pair, 0)


def shards(density, even_taps, odd_taps, low_taps, wavelets, pairs):
    tile_rows, ny, nz = density.shape
    count, waves = lax.axis_size("space"), lax.axis_size("wave")
    upper = lax.axis_index("wave") % 2
    halo = lax.dynamic_slice_in_dim(density, upper * (tile_rows - HALO), HALO, 0)
    step = (-1, 1)
    moves = [
        (z * waves + w, (z + step[w % 2]) * waves + w)
        for z in range(count)
        for w in range(waves)
        if 0 <= z + step[w % 2] < count
    ]
    got = lax.ppermute(halo, ("space", "wave"), moves)
    other = lax.ppermute(got, "wave", [(w, w ^ 1) for w in range(waves)])
    per_dev = pairs.shape[0] // lax.axis_size("wave")
    smem = pl.BlockSpec(memory_space=pltpu.SMEM)
    anywhere = pl.BlockSpec(memory_space=pl.ANY)
    return pl.pallas_call(
        body,
        out_shape=jax.ShapeDtypeStruct((per_dev, tile_rows // 2, ny // 2, nz // 2), F32),
        in_specs=[smem] * 5 + [anywhere] * 3,
        out_specs=pl.BlockSpec(memory_space=pltpu.VMEM),
        scratch_shapes=[
            pltpu.VMEM((160, 16, 128), F32),
            pltpu.VMEM((4, 16, 8, 128), F32),
            pltpu.VMEM((2, 2, 256, 256), BF16),
            pltpu.VMEM((2, 512, 256), BF16),
            pltpu.VMEM((4, 256, 128), BF16),
            pltpu.VMEM((1024, 256), BF16),
            pltpu.VMEM((1024, 512), BF16),
            pltpu.VMEM((1024, 128), F32),
            pltpu.VMEM((6, 512, 256), BF16),
            pltpu.VMEM((512, 128), F32),
            pltpu.SemaphoreType.DMA((3,)),
        ],
        compiler_params=pltpu.CompilerParams(vmem_limit_bytes=24 * 1024 * 1024),
    )(even_taps, odd_taps, low_taps, wavelets, pairs, got, density, other)


def solution(mesh):
    placed = (P(("groups", "space"), None, None), P(), P(), P(), P(), P())
    return jax.shard_map(
        shards,
        mesh=mesh,
        in_specs=placed,
        out_specs=P("wave", ("groups", "space"), None, None),
        check_vma=False,
    )
```

```python
import functools

import jax
import jax.numpy as jnp
from jax import lax
from jax.experimental import pallas as pl
from jax.experimental.pallas import tpu as pltpu
from jax.sharding import PartitionSpec as P

TAPS = 15
HALF = 7
HALO = 42
FRONT = 8
WINDOW = 160
KEPT = 60
STORED = 72
SHIFT = (6, 3)
INNER = ((18, 26, 34), (21, 29))
BEFORE = ((-6, 2, 10), (-3, 5, 13))
AFTER = ((42, 50, 58), (37, 45, 53))
EPS = 1e-6
F32 = jnp.float32
BF16 = jnp.bfloat16
LOW, EVEN, ODD, BOTH = 0, 1, 2, 3
TILE = (8, 128)


def split(value):
    high = value.astype(BF16)
    return high, (value - high.astype(F32)).astype(BF16)


def dot(a, b):
    return jnp.dot(a, b, preferred_element_type=F32)


def rows(shape):
    return lax.broadcasted_iota(jnp.int32, shape, 0)


def lanes(shape):
    return lax.broadcasted_iota(jnp.int32, shape, 1)


def modulus(value):
    squares = value * value
    total = squares + pltpu.roll(squares, 64, 1) + EPS
    return total * lax.rsqrt(total)


def weigh(taps, values, pairs):
    acc = None
    for t, v in pairs:
        term = taps[t] * values[v]
        acc = term if acc is None else acc + term
    return acc


def banded(taps_ref, offset, dilation):
    low = both = jnp.zeros(offset.shape, F32)
    for t in range(TAPS):
        here = offset == (t - HALF) * dilation
        low = jnp.where(here, taps_ref[LOW, t][0:1], low)
        both = jnp.where(here, taps_ref[BOTH, t][0:1], both)
    return low, both


def make_filters(even_s, odd_s, low_s, taps_ref, w_first, w_zero, w_second):
    left = lanes(TILE) < 64
    for t in range(TAPS):
        even = jnp.full(TILE, even_s[t], F32)
        odd = jnp.full(TILE, odd_s[t], F32)
        taps_ref[LOW, t] = jnp.full(TILE, low_s[t], F32)
        taps_ref[EVEN, t] = even
        taps_ref[ODD, t] = odd
        taps_ref[BOTH, t] = jnp.where(left, even, odd)
    wide = (128, 128)
    none = jnp.zeros(wide, BF16)
    for level in range(2):
        low, both = banded(taps_ref, rows(wide) - 2 * (lanes(wide) % 64), 1 << level)
        for kind, matrix in enumerate((low, both)):
            high, rest = split(matrix)
            column = 256 * kind
            w_first[level, 0:128, column:column + 128] = high
            w_first[level, 128:256, column:column + 128] = high
            w_first[level, 0:128, column + 128:column + 256] = rest
            w_first[level, 128:256, column + 128:column + 256] = none
        inner = lanes(wide) < 64
        for part, keep in enumerate((inner, ~inner)):
            high, rest = split(jnp.where(keep, low, 0.0))
            row = 256 * part
            w_zero[level, row:row + 128, 0:128] = high
            w_zero[level, row + 128:row + 256, 0:128] = high
            w_zero[level, row:row + 128, 128:256] = rest
            w_zero[level, row + 128:row + 256, 128:256] = none
        half = (64, 128)
        low, both = banded(taps_ref, rows(half) - lanes(half) % 64, 1 << level)
        for kind, matrix in enumerate((low, both)):
            high, rest = split(matrix)
            w_second[2 * level + kind, 0:64] = high
            w_second[2 * level + kind, 64:128] = high
            w_second[2 * level + kind, 128:192] = rest
            w_second[2 * level + kind, 192:256] = jnp.zeros(half, BF16)


def needed(wave_s, pairs_s, base, slots):
    need = [[False] * 3 for _ in range(2)]
    for p in range(slots):
        field = pairs_s[base + p, 0]
        safe = jnp.maximum(field, 0)
        level, orient = wave_s[safe, 0], wave_s[safe, 1]
        for a in range(2):
            for b in range(3):
                need[a][b] = need[a][b] | ((field >= 0) & (level == a) & (orient == b))
    return need


def first_rows(need, starts, tile_rows, taps_ref, w_first, w_zero, grid_ref, m_ref, lhs_ref, z_ref):
    rank = lax.axis_index("space")
    total = lax.axis_size("space") * tile_rows

    def x_pass(level, kind, start):
        taps = [taps_ref[kind, t] for t in range(TAPS)]
        parts = []
        for h in range(2 - level):
            sums = [None] * 8
            for r in range((29, 22)[level]):
                if level == 0:
                    value = grid_ref[2 * start + HALF + FRONT + r, 8 * h:8 * h + 8, :]
                else:
                    value = grid_ref[2 * (start + r) + FRONT, pl.ds(0, 8, stride=2), :]
                for i in range(8):
                    t = r - (2 - level) * i
                    if 0 <= t < TAPS:
                        term = taps[t] * value
                        sums[i] = term if sums[i] is None else sums[i] + term
            parts.append(sums)
        if level == 0:
            return [jnp.concatenate([parts[0][i], parts[1][i]], axis=0) for i in range(8)]
        return [jnp.concatenate([parts[0][i], parts[0][i + 1]], axis=0) for i in range(0, 8, 2)]

    def put(level, kind, n, start, column):
        for i, value in enumerate(x_pass(level, kind, start)):
            high, rest = split(value)
            at = n * 128 + i * 16
            lhs_ref[at:at + 16, column:column + 128] = high
            lhs_ref[at:at + 16, column + 128:column + 256] = rest

    def finish(level, orient):
        height = 16 >> level
        taps = taps_ref.at[BOTH if orient == 1 else LOW]
        for n, start in enumerate(starts[level]):
            values = [z_ref[orient, pl.ds(n * 128 + y, 8, stride=height), :] for y in range(height)]
            i = start + rows(TILE)
            x = rank * tile_rows - 28 + 2 * i
            inside = (x >= 0) & (x < total) & (i >= 0) & (i < KEPT)
            place = pl.multiple_of(start + SHIFT[level], 8)
            for j in range(8):
                terms = [(y - (2 - level) * j + HALF, y) for y in range(height)]
                out = modulus(weigh(taps, values, [(t, y) for t, y in terms if 0 <= t < TAPS]))
                m_ref[level * 3 + orient, j, pl.ds(place, 8), :] = jnp.where(inside, out, 0.0)

    for level in range(2):
        size = 128 >> level

        @pl.when(need[level][1] | need[level][2])
        def _():
            for n, start in enumerate(starts[level]):
                put(level, LOW, n, start, 0)
                at = n * 128
                z = dot(lhs_ref[at:at + size, 0:256], w_first[level])
                z_ref[1, at:at + size, :] = z[:, 0:128] + z[:, 128:256]
                z_ref[2, at:at + size, :] = z[:, 256:384] + z[:, 384:512]

        for orient in (1, 2):
            @pl.when(need[level][orient])
            def _():
                finish(level, orient)

        @pl.when(need[level][0])
        def _():
            for n, start in enumerate(starts[level]):
                put(level, EVEN, n, start, 0)
                put(level, ODD, n, start, 256)
                at = n * 128
                z = dot(lhs_ref[at:at + size, :], w_zero[level])
                z_ref[0, at:at + size, :] = z[:, 0:128] + z[:, 128:256]
            finish(level, 0)


def second_order(need, base, slots, wave_s, pairs_s, taps_ref, w_second, m_ref, out_ref, lhs_second, z2_ref, done_ref, sems):
    left = lanes((16, 128)) < 64
    for level in range(2):
        for orient in range(3):
            @pl.when(need[level][orient])
            def _():
                slot = level * 3 + orient
                for j in range(8):
                    for k in range(0, 64, 16):
                        value = m_ref[slot, j, k + SHIFT[level]:k + SHIFT[level] + 16, :]
                        high = value.astype(BF16)
                        wide = high.astype(F32)
                        pair = jnp.where(left, wide, value - wide).astype(BF16)
                        lhs_second[slot, j * 64 + k:j * 64 + k + 16, 0:128] = pair
                        lhs_second[slot, j * 64 + k:j * 64 + k + 16, 128:256] = high

    def read(p):
        field, wavelet = pairs_s[base + p, 0], pairs_s[base + p, 1]
        safe = jnp.maximum(field, 0)
        slot = wave_s[safe, 0] * 3 + wave_s[safe, 1]
        return field >= 0, slot, wave_s[wavelet, 0], wave_s[wavelet, 1]

    def z_pass(p, buffer):
        live, slot, level, orient = read(p)
        kind = 2 * jnp.maximum(level - 1, 0) + (orient == 2).astype(jnp.int32)
        z2_ref[buffer] = dot(lhs_second[slot], w_second[kind])

    def copy(p):
        return pltpu.make_async_copy(done_ref.at[p], out_ref.at[p], sems.at[p])

    def one_pair(p, carry):
        live, _, level, orient = read(p)
        buffer = p % 2

        def work(dilation):
            z_pass(jnp.minimum(p + 1, slots - 1), 1 - buffer)
            x_taps = taps_ref.at[jnp.where(orient == 0, BOTH, LOW)]
            y_taps = taps_ref.at[jnp.where(orient == 1, BOTH, LOW)]
            place = done_ref.at[p].reshape(done_ref.shape[1] * 8, 64)
            for c in range(4):
                lines = []
                for j in range(8):
                    at = j * 64 + c * 8 + 14
                    lines.append(weigh(
                        x_taps,
                        [z2_ref[buffer, at + s * dilation:at + s * dilation + 8, :] for s in range(-HALF, HALF + 1)],
                        [(t, t) for t in range(TAPS)],
                    ))
                for j in range(8):
                    terms = [((y - j) // dilation + HALF, y) for y in range(8) if (y - j) % dilation == 0]
                    out = modulus(weigh(y_taps, lines, terms))
                    place[pl.ds(c * 64 + j, 8, stride=8), :] = out[:, 0:64]

        for dilation in (1, 2):
            @pl.when(live & (level == dilation))
            def _():
                work(dilation)

        @pl.when(jnp.logical_not(live))
        def _():
            done_ref[p] = jnp.zeros(done_ref.shape[1:], F32)

        copy(p).start()
        return carry

    z_pass(0, 0)
    lax.fori_loop(0, slots, one_pair, 0)
    for p in range(slots):
        copy(p).wait()


def inner_body(
    even_s, odd_s, low_s, wave_s, pairs_s, own_ref,
    taps_ref, w_first, w_zero, w_second, grid_ref, m_ref, lhs_ref, z_ref, sem, *, slots,
):
    tile_rows = own_ref.shape[0]
    copy = pltpu.make_async_copy(own_ref, grid_ref.at[pl.ds(FRONT + HALO, tile_rows)], sem)
    copy.start()
    make_filters(even_s, odd_s, low_s, taps_ref, w_first, w_zero, w_second)
    need = needed(wave_s, pairs_s, lax.axis_index("wave") * slots, slots)
    copy.wait()
    first_rows(need, INNER, tile_rows, taps_ref, w_first, w_zero, grid_ref, m_ref, lhs_ref, z_ref)


def side_body(
    wave_s, pairs_s, got_ref, taps_ref, w_first, w_zero, grid_in, m_in,
    grid_ref, m_ref, lhs_ref, z_ref, *, slots, tile_rows,
):
    side = lax.axis_index("wave") % 2
    add_side(side, wave_s, pairs_s, got_ref, taps_ref, w_first, w_zero, grid_ref, m_ref, lhs_ref, z_ref, slots, tile_rows)


def add_side(side, wave_s, pairs_s, halo_ref, taps_ref, w_first, w_zero, grid_ref, m_ref, lhs_ref, z_ref, slots, tile_rows):
    place = FRONT + (1 - side) * (HALO + tile_rows)
    for r in range(HALO):
        grid_ref[place + r] = halo_ref[r]
    need = needed(wave_s, pairs_s, lax.axis_index("wave") * slots, slots)
    starts = [[jnp.where(side == 1, b, a) for b, a in zip(*pair)] for pair in zip(BEFORE, AFTER)]
    first_rows(need, starts, tile_rows, taps_ref, w_first, w_zero, grid_ref, m_ref, lhs_ref, z_ref)
    return need


def last_body(
    wave_s, pairs_s, other_ref, taps_ref, w_first, w_zero, w_second, grid_in, m_in,
    out_ref, grid_ref, m_ref, lhs_ref, z_ref, lhs_second, z2_ref, done_ref, sems, *, slots, tile_rows,
):
    side = 1 - lax.axis_index("wave") % 2
    need = add_side(side, wave_s, pairs_s, other_ref, taps_ref, w_first, w_zero, grid_ref, m_ref, lhs_ref, z_ref, slots, tile_rows)
    base = lax.axis_index("wave") * slots
    second_order(need, base, slots, wave_s, pairs_s, taps_ref, w_second, m_ref, out_ref, lhs_second, z2_ref, done_ref, sems)


def shards(density, even_taps, odd_taps, low_taps, wavelets, pairs):
    tile_rows, ny, nz = density.shape
    count, waves = lax.axis_size("space"), lax.axis_size("wave")
    slots = pairs.shape[0] // waves
    upper = lax.axis_index("wave") % 2
    halo = lax.dynamic_slice_in_dim(density, upper * (tile_rows - HALO), HALO, 0)
    step = (-1, 1)
    moves = [
        (z * waves + w, (z + step[w % 2]) * waves + w)
        for z in range(count)
        for w in range(waves)
        if 0 <= z + step[w % 2] < count
    ]
    got = lax.ppermute(halo, ("space", "wave"), moves)

    smem = pl.BlockSpec(memory_space=pltpu.SMEM)
    vmem = pl.BlockSpec(memory_space=pltpu.VMEM)
    anywhere = pl.BlockSpec(memory_space=pl.ANY)
    params = pltpu.CompilerParams(vmem_limit_bytes=24 * 1024 * 1024)
    held = lambda value: pltpu.with_memory_space_constraint(value, pltpu.VMEM)
    grid_type = pltpu.VMEM((WINDOW, ny, nz), F32)
    m_type = pltpu.VMEM((6, 8, STORED, 128), F32)
    scratch = [pltpu.VMEM((384, 512), BF16), pltpu.VMEM((3, 384, 128), F32)]

    def cost(us):
        return pl.CostEstimate(flops=us * 1000000000, bytes_accessed=us * 2500000, transcendentals=0)

    taps, w_first, w_zero, w_second, grid, m = pl.pallas_call(
        functools.partial(inner_body, slots=slots),
        out_shape=[
            pltpu.VMEM((4, 16, 8, 128), F32),
            pltpu.VMEM((2, 256, 512), BF16),
            pltpu.VMEM((2, 512, 256), BF16),
            pltpu.VMEM((4, 256, 128), BF16),
            grid_type,
            m_type,
        ],
        in_specs=[smem] * 5 + [anywhere],
        out_specs=[vmem] * 6,
        scratch_shapes=scratch + [pltpu.SemaphoreType.DMA],
        compiler_params=params,
        cost_estimate=cost(3),
        name="inner_rows",
    )(even_taps, odd_taps, low_taps, wavelets, pairs, density)
    got, grid = lax.optimization_barrier((got, grid))
    other = lax.ppermute(got, "wave", [(w, w ^ 1) for w in range(waves)])
    taps, w_first, w_zero, w_second, grid, m = map(held, (taps, w_first, w_zero, w_second, grid, m))
    grid, m = pl.pallas_call(
        functools.partial(side_body, slots=slots, tile_rows=tile_rows),
        out_shape=[grid_type, m_type],
        in_specs=[smem] * 2 + [vmem] * 6,
        out_specs=[vmem] * 2,
        input_output_aliases={6: 0, 7: 1},
        scratch_shapes=scratch,
        compiler_params=params,
        cost_estimate=cost(2),
        name="side_rows",
    )(wavelets, pairs, held(got), taps, w_first, w_zero, grid, m)
    grid, m = map(held, (grid, m))
    second, _, _ = pl.pallas_call(
        functools.partial(last_body, slots=slots, tile_rows=tile_rows),
        out_shape=[jax.ShapeDtypeStruct((slots, tile_rows // 2, ny // 2, nz // 2), F32), grid_type, m_type],
        in_specs=[smem] * 2 + [vmem] * 7,
        out_specs=[anywhere, vmem, vmem],
        input_output_aliases={7: 1, 8: 2},
        scratch_shapes=scratch + [
            pltpu.VMEM((6, 512, 256), BF16),
            pltpu.VMEM((2, 512, 128), F32),
            pltpu.VMEM((slots, tile_rows // 2, ny // 2, nz // 2), F32),
            pltpu.SemaphoreType.DMA((slots,)),
        ],
        compiler_params=params,
        cost_estimate=cost(5),
        name="second_order",
    )(wavelets, pairs, held(other), taps, w_first, w_zero, w_second, grid, m)
    return second


def solution(mesh):
    placed = (P(("groups", "space"), None, None), P(), P(), P(), P(), P())
    return jax.shard_map(
        shards,
        mesh=mesh,
        in_specs=placed,
        out_specs=P("wave", ("groups", "space"), None, None),
        check_vma=False,
    )
```

```python
import functools

import jax
import jax.numpy as jnp
from jax import lax
from jax.experimental import pallas as pl
from jax.experimental.pallas import tpu as pltpu
from jax.sharding import PartitionSpec as P

TAPS = 15
HALF = 7
HALO = 42
FRONT = 8
WINDOW = 160
KEPT = 60
STORED = 72
SHIFT = 6
INNER = ((18, 26, 34), (21, 29))
BEFORE = ((-6, 2, 10), (-3, 5, 13))
AFTER = ((42, 50, 58), (37, 45, 53))
EPS = 1e-6
F32 = jnp.float32
BF16 = jnp.bfloat16
LOW, EVEN, ODD, BOTH = 0, 1, 2, 3
TILE = (8, 128)


def split(value):
    high = value.astype(BF16)
    return high, (value - high.astype(F32)).astype(BF16)


def dot(a, b):
    return jnp.dot(a, b, preferred_element_type=F32)


def rows(shape):
    return lax.broadcasted_iota(jnp.int32, shape, 0)


def lanes(shape):
    return lax.broadcasted_iota(jnp.int32, shape, 1)


def modulus(value):
    squares = value * value
    total = squares + pltpu.roll(squares, 64, 1) + EPS
    return total * lax.rsqrt(total)


def weigh(taps, values, pairs):
    acc = None
    for t, v in pairs:
        term = taps[t] * values[v]
        acc = term if acc is None else acc + term
    return acc


def banded(taps_ref, offset, dilation):
    low = both = jnp.zeros(offset.shape, F32)
    for t in range(TAPS):
        here = offset == (t - HALF) * dilation
        low = jnp.where(here, taps_ref[LOW, t][0:1], low)
        both = jnp.where(here, taps_ref[BOTH, t][0:1], both)
    return low, both


def make_filters(even_s, odd_s, low_s, taps_ref, w_first, w_zero, w_second):
    left = lanes(TILE) < 64
    for t in range(TAPS):
        even = jnp.full(TILE, even_s[t], F32)
        odd = jnp.full(TILE, odd_s[t], F32)
        taps_ref[LOW, t] = jnp.full(TILE, low_s[t], F32)
        taps_ref[EVEN, t] = even
        taps_ref[ODD, t] = odd
        taps_ref[BOTH, t] = jnp.where(left, even, odd)
    wide = (128, 128)
    none = jnp.zeros(wide, BF16)
    for level in range(2):
        low, both = banded(taps_ref, rows(wide) - 2 * (lanes(wide) % 64), 1 << level)
        for kind, matrix in enumerate((low, both)):
            high, rest = split(matrix)
            column = 256 * kind
            w_first[level, 0:128, column:column + 128] = high
            w_first[level, 128:256, column:column + 128] = high
            w_first[level, 0:128, column + 128:column + 256] = rest
            w_first[level, 128:256, column + 128:column + 256] = none
        inner = lanes(wide) < 64
        for part, keep in enumerate((inner, ~inner)):
            high, rest = split(jnp.where(keep, low, 0.0))
            row = 256 * part
            w_zero[level, row:row + 128, 0:128] = high
            w_zero[level, row + 128:row + 256, 0:128] = high
            w_zero[level, row:row + 128, 128:256] = rest
            w_zero[level, row + 128:row + 256, 128:256] = none
        half = (64, 128)
        low, both = banded(taps_ref, rows(half) - lanes(half) % 64, 1 << level)
        for kind, matrix in enumerate((low, both)):
            high, rest = split(matrix)
            w_second[2 * level + kind, 0:64] = high
            w_second[2 * level + kind, 64:128] = high
            w_second[2 * level + kind, 128:192] = rest
            w_second[2 * level + kind, 192:256] = jnp.zeros(half, BF16)


def read_tables(wave_s, pairs_s, base, slots, info_s):
    found = []
    need = [False] * 6
    for p in range(slots):
        field, wavelet = pairs_s[0, base + p], pairs_s[1, base + p]
        safe = jnp.maximum(field, 0)
        live = field >= 0
        source = wave_s[0, safe] * 3 + wave_s[1, safe]
        level, orient = wave_s[0, wavelet], wave_s[1, wavelet]
        key = jnp.where(live, (source * 4 + level) * 4 + orient, -1)
        twin = jnp.int32(-1)
        for q in range(p - 1, -1, -1):
            twin = jnp.where(found[q] == key, q, twin)
        found.append(key)
        info_s[p] = jnp.where(live, jnp.where(twin >= 0, 3, level), 0)
        info_s[slots + p] = source
        info_s[2 * slots + p] = orient
        info_s[3 * slots + p] = jnp.maximum(twin, 0)
        for k in range(6):
            need[k] = need[k] | (live & (source == k))
    for k in range(6):
        info_s[4 * slots + k] = need[k].astype(jnp.int32)


def needed(info_s, slots):
    return [[info_s[4 * slots + level * 3 + orient] > 0 for orient in range(3)] for level in range(2)]


def first_rows(need, starts, tile_rows, taps_ref, w_first, w_zero, grid_ref, m_ref, lhs_ref, z_ref):
    rank = lax.axis_index("space")
    total = lax.axis_size("space") * tile_rows

    def x_pass(level, kind, start):
        taps = [taps_ref[kind, t] for t in range(TAPS)]
        parts = []
        for h in range(2 - level):
            sums = [None] * 8
            for r in range((29, 22)[level]):
                if level == 0:
                    value = grid_ref[2 * start + HALF + FRONT + r, 8 * h:8 * h + 8, :]
                else:
                    value = grid_ref[2 * (start + r) + FRONT, pl.ds(0, 8, stride=2), :]
                for i in range(8):
                    t = r - (2 - level) * i
                    if 0 <= t < TAPS:
                        term = taps[t] * value
                        sums[i] = term if sums[i] is None else sums[i] + term
            parts.append(sums)
        if level == 0:
            return [jnp.concatenate([parts[0][i], parts[1][i]], axis=0) for i in range(8)]
        return [jnp.concatenate([parts[0][i], parts[0][i + 1]], axis=0) for i in range(0, 8, 2)]

    def put(level, kind, n, start, column):
        for i, value in enumerate(x_pass(level, kind, start)):
            high, rest = split(value)
            at = n * 128 + i * 16
            lhs_ref[at:at + 16, column:column + 128] = high
            lhs_ref[at:at + 16, column + 128:column + 256] = rest

    def finish(level, orient):
        height = 16 >> level
        taps = taps_ref.at[BOTH if orient == 1 else LOW]
        for n, start in enumerate(starts[level]):
            values = [z_ref[orient, pl.ds(n * 128 + y, 8, stride=height), :] for y in range(height)]
            i = start + rows(TILE)
            x = rank * tile_rows - 28 + 2 * i
            inside = (x >= 0) & (x < total) & (i >= 0) & (i < KEPT)
            place = m_ref.at[level * 3 + orient].reshape(STORED * 8, 128)
            for j in range(8):
                terms = [(y - (2 - level) * j + HALF, y) for y in range(height)]
                out = modulus(weigh(taps, values, [(t, y) for t, y in terms if 0 <= t < TAPS]))
                place[pl.ds((start + SHIFT) * 8 + j, 8, stride=8), :] = jnp.where(inside, out, 0.0)

    for level in range(2):
        size = 128 >> level

        @pl.when(need[level][1] | need[level][2])
        def _():
            for n, start in enumerate(starts[level]):
                put(level, LOW, n, start, 0)
                at = n * 128
                z = dot(lhs_ref[at:at + size, 0:256], w_first[level])
                z_ref[1, at:at + size, :] = z[:, 0:128] + z[:, 128:256]
                z_ref[2, at:at + size, :] = z[:, 256:384] + z[:, 384:512]

        for orient in (1, 2):
            @pl.when(need[level][orient])
            def _():
                finish(level, orient)

        @pl.when(need[level][0])
        def _():
            for n, start in enumerate(starts[level]):
                put(level, EVEN, n, start, 0)
                put(level, ODD, n, start, 256)
                at = n * 128
                z = dot(lhs_ref[at:at + size, :], w_zero[level])
                z_ref[0, at:at + size, :] = z[:, 0:128] + z[:, 128:256]
            finish(level, 0)


def second_order(need, slots, info_s, taps_ref, w_second, m_ref, out_ref, lhs_second, z2_ref, line_ref, done_ref, sems):
    left = lanes((16, 128)) < 64
    for level in range(2):
        for orient in range(3):
            @pl.when(need[level][orient])
            def _():
                source = level * 3 + orient
                for i in range(0, KEPT, 2):
                    value = jnp.concatenate([m_ref[source, i + SHIFT], m_ref[source, i + 1 + SHIFT]], axis=0)
                    high = value.astype(BF16)
                    wide = high.astype(F32)
                    pair = jnp.where(left, wide, value - wide).astype(BF16)
                    lhs_second[source, i * 8:i * 8 + 16, 0:128] = pair
                    lhs_second[source, i * 8:i * 8 + 16, 128:256] = high

    def z_pass(p, buffer):
        kind = 2 * (info_s[p] == 2).astype(jnp.int32) + (info_s[2 * slots + p] == 2).astype(jnp.int32)
        z2_ref[buffer] = dot(lhs_second[info_s[slots + p]], w_second[kind]).reshape(KEPT, 8, 128)

    def copy(p):
        return pltpu.make_async_copy(done_ref.at[p], out_ref.at[p], sems.at[p])

    def one_pair(p, carry):
        mode, orient = info_s[p], info_s[2 * slots + p]
        buffer = p % 2
        following = jnp.minimum(p + 1, slots - 1)

        def work(dilation):
            z_pass(following, 1 - buffer)
            x_taps = taps_ref.at[jnp.where(orient == 0, BOTH, LOW)]
            y_taps = taps_ref.at[jnp.where(orient == 1, BOTH, LOW)]
            place = done_ref.at[p].reshape(done_ref.shape[1] * 8, 64)
            for c in range(0, 32, 16):
                taps = [x_taps[t] for t in range(TAPS)]
                sums = [None] * 16
                first = c + 14 - HALF * dilation
                for r in range(15 + 14 * dilation + 1):
                    value = z2_ref[buffer, first + r]
                    for i in range(16):
                        if (r - i) % dilation == 0 and 0 <= (r - i) // dilation < TAPS:
                            term = taps[(r - i) // dilation] * value
                            sums[i] = term if sums[i] is None else sums[i] + term
                for i in range(16):
                    line_ref[(c + i) * 8:(c + i) * 8 + 8, :] = sums[i]
            for c in range(4):
                lines = [line_ref[pl.ds(c * 64 + y, 8, stride=8), :] for y in range(8)]
                for j in range(8):
                    terms = [((y - j) // dilation + HALF, y) for y in range(8) if (y - j) % dilation == 0]
                    out = modulus(weigh(y_taps, lines, terms))
                    place[pl.ds(c * 64 + j, 8, stride=8), :] = out[:, 0:64]

        for dilation in (1, 2):
            @pl.when(mode == dilation)
            def _():
                work(dilation)

        @pl.when(mode == 3)
        def _():
            z_pass(following, 1 - buffer)
            done_ref[p] = done_ref[info_s[3 * slots + p]]

        @pl.when(mode == 0)
        def _():
            done_ref[p] = jnp.zeros(done_ref.shape[1:], F32)

        copy(p).start()
        return carry

    z_pass(0, 0)
    lax.fori_loop(0, slots, one_pair, 0)
    for p in range(slots):
        copy(p).wait()


def inner_body(
    even_ref, odd_ref, low_ref, wave_ref, pairs_ref, own_ref,
    taps_ref, w_first, w_zero, w_second, grid_ref, m_ref, info_s,
    even_s, odd_s, low_s, wave_s, pairs_s, lhs_ref, z_ref, sems, *, slots,
):
    tile_rows = own_ref.shape[0]
    moves = (
        (even_ref, even_s), (odd_ref, odd_s), (low_ref, low_s), (wave_ref, wave_s), (pairs_ref, pairs_s),
        (own_ref, grid_ref.at[pl.ds(FRONT + HALO, tile_rows)]),
    )
    copies = [pltpu.make_async_copy(source, place, sems.at[n]) for n, (source, place) in enumerate(moves)]
    for copy in copies:
        copy.start()
    for copy in copies[:-1]:
        copy.wait()
    make_filters(even_s, odd_s, low_s, taps_ref, w_first, w_zero, w_second)
    read_tables(wave_s, pairs_s, lax.axis_index("wave") * slots, slots, info_s)
    copies[-1].wait()
    first_rows(needed(info_s, slots), INNER, tile_rows, taps_ref, w_first, w_zero, grid_ref, m_ref, lhs_ref, z_ref)


def outer_body(
    info_s, got_ref, other_ref, taps_ref, w_first, w_zero, w_second, grid_in, m_in,
    out_ref, grid_ref, m_ref, lhs_ref, z_ref, lhs_second, z2_ref, line_ref, done_ref, sems, *, slots, tile_rows,
):
    upper = lax.axis_index("wave") % 2
    far = HALO + tile_rows
    for r in range(HALO):
        grid_ref[FRONT + (1 - upper) * far + r] = got_ref[r]
        grid_ref[FRONT + upper * far + r] = other_ref[r]
    need = needed(info_s, slots)
    starts = [a + b for a, b in zip(BEFORE, AFTER)]
    first_rows(need, starts, tile_rows, taps_ref, w_first, w_zero, grid_ref, m_ref, lhs_ref, z_ref)
    second_order(need, slots, info_s, taps_ref, w_second, m_ref, out_ref, lhs_second, z2_ref, line_ref, done_ref, sems)


def shards(density, even_taps, odd_taps, low_taps, wavelets, pairs):
    tile_rows, ny, nz = density.shape
    count, waves = lax.axis_size("space"), lax.axis_size("wave")
    slots = pairs.shape[0] // waves
    upper = lax.axis_index("wave") % 2
    halo = lax.dynamic_slice_in_dim(density, upper * (tile_rows - HALO), HALO, 0)
    step = (-1, 1)
    moves = [
        (z * waves + w, (z + step[w % 2]) * waves + w)
        for z in range(count)
        for w in range(waves)
        if 0 <= z + step[w % 2] < count
    ]
    got = lax.ppermute(halo, ("space", "wave"), moves)

    smem = pl.BlockSpec(memory_space=pltpu.SMEM)
    vmem = pl.BlockSpec(memory_space=pltpu.VMEM)
    anywhere = pl.BlockSpec(memory_space=pl.ANY)
    params = pltpu.CompilerParams(vmem_limit_bytes=24 * 1024 * 1024)

    def held(value):
        return pltpu.with_memory_space_constraint(value, pltpu.VMEM)

    def far(value):
        return pltpu.with_memory_space_constraint(value, pltpu.HBM)

    def cost(us):
        return pl.CostEstimate(flops=us * 1000000000, bytes_accessed=us * 2500000, transcendentals=0)

    grid_type = pltpu.VMEM((WINDOW, ny, nz), F32)
    m_type = pltpu.VMEM((6, STORED, 8, 128), F32)
    out_shape = (slots, tile_rows // 2, ny // 2, nz // 2)
    scratch = [pltpu.VMEM((768, 512), BF16), pltpu.VMEM((3, 768, 128), F32)]
    taps, w_first, w_zero, w_second, grid, m, info = pl.pallas_call(
        functools.partial(inner_body, slots=slots),
        out_shape=[
            pltpu.VMEM((4, 16, 8, 128), F32),
            pltpu.VMEM((2, 256, 512), BF16),
            pltpu.VMEM((2, 512, 256), BF16),
            pltpu.VMEM((4, 256, 128), BF16),
            grid_type,
            m_type,
            pltpu.SMEM((4 * slots + 8,), jnp.int32),
        ],
        in_specs=[anywhere] * 6,
        out_specs=[vmem] * 6 + [smem],
        scratch_shapes=[
            pltpu.SMEM((TAPS,), F32),
            pltpu.SMEM((TAPS,), F32),
            pltpu.SMEM((TAPS,), F32),
            pltpu.SMEM(wavelets.shape[::-1], jnp.int32),
            pltpu.SMEM(pairs.shape[::-1], jnp.int32),
            *scratch,
            pltpu.SemaphoreType.DMA((6,)),
        ],
        compiler_params=params,
        cost_estimate=cost(3),
        name="inner_rows",
    )(*map(far, (even_taps, odd_taps, low_taps, wavelets.T, pairs.T, density)))
    got, grid = lax.optimization_barrier((got, grid))
    other = lax.ppermute(got, "wave", [(w, w ^ 1) for w in range(waves)])
    taps, w_first, w_zero, w_second, grid, m = map(held, (taps, w_first, w_zero, w_second, grid, m))
    info = pltpu.with_memory_space_constraint(info, pltpu.SMEM)
    second, _, _ = pl.pallas_call(
        functools.partial(outer_body, slots=slots, tile_rows=tile_rows),
        out_shape=[jax.ShapeDtypeStruct(out_shape, F32), grid_type, m_type],
        in_specs=[smem] + [vmem] * 8,
        out_specs=[anywhere, vmem, vmem],
        input_output_aliases={7: 1, 8: 2},
        scratch_shapes=scratch + [
            pltpu.VMEM((6, KEPT * 8, 256), BF16),
            pltpu.VMEM((2, KEPT, 8, 128), F32),
            pltpu.VMEM((256, 128), F32),
            pltpu.VMEM(out_shape, F32),
            pltpu.SemaphoreType.DMA((slots,)),
        ],
        compiler_params=params,
        cost_estimate=cost(5),
        name="outer_rows_and_pairs",
    )(info, held(got), held(other), taps, w_first, w_zero, w_second, grid, m)
    return second


def solution(mesh):
    placed = (P(("groups", "space"), None, None), P(), P(), P(), P(), P())
    return jax.shard_map(
        shards,
        mesh=mesh,
        in_specs=placed,
        out_specs=P("wave", ("groups", "space"), None, None),
        check_vma=False,
    )
```

```python
import functools

import jax
import jax.numpy as jnp
from jax import lax
from jax.experimental import pallas as pl
from jax.experimental.pallas import tpu as pltpu
from jax.sharding import PartitionSpec as P

TAPS = 15
HALF = 7
HALO = 42
FRONT = 8
WINDOW = 160
KEPT = 60
STORED = 72
SHIFT = 6
INNER = ((18, 26, 34), (21, 29))
BEFORE = ((-6, 2, 10), (-3, 5, 13))
AFTER = ((42, 50, 58), (37, 45, 53))
EPS = 1e-6
F32 = jnp.float32
BF16 = jnp.bfloat16
LOW, EVEN, ODD, BOTH = 0, 1, 2, 3
TILE = (8, 128)


def split(value):
    high = value.astype(BF16)
    return high, (value - high.astype(F32)).astype(BF16)


def dot(a, b):
    return jnp.dot(a, b, preferred_element_type=F32)


def rows(shape):
    return lax.broadcasted_iota(jnp.int32, shape, 0)


def lanes(shape):
    return lax.broadcasted_iota(jnp.int32, shape, 1)


def modulus(value):
    squares = value * value
    total = squares + pltpu.roll(squares, 64, 1) + EPS
    return total * lax.rsqrt(total)


def weigh(taps, values, pairs):
    acc = None
    for t, v in pairs:
        term = taps[t] * values[v]
        acc = term if acc is None else acc + term
    return acc


def banded(taps_ref, offset, dilation):
    low = both = jnp.zeros(offset.shape, F32)
    for t in range(TAPS):
        here = offset == (t - HALF) * dilation
        low = jnp.where(here, taps_ref[LOW, t][0:1], low)
        both = jnp.where(here, taps_ref[BOTH, t][0:1], both)
    return low, both


def make_filters(even_s, odd_s, low_s, taps_ref, w_first, w_zero, w_second):
    left = lanes(TILE) < 64
    for t in range(TAPS):
        even = jnp.full(TILE, even_s[t], F32)
        odd = jnp.full(TILE, odd_s[t], F32)
        taps_ref[LOW, t] = jnp.full(TILE, low_s[t], F32)
        taps_ref[EVEN, t] = even
        taps_ref[ODD, t] = odd
        taps_ref[BOTH, t] = jnp.where(left, even, odd)
    wide = (128, 128)
    none = jnp.zeros(wide, BF16)
    for level in range(2):
        low, both = banded(taps_ref, rows(wide) - 2 * (lanes(wide) % 64), 1 << level)
        for kind, matrix in enumerate((low, both)):
            high, rest = split(matrix)
            column = 256 * kind
            w_first[level, 0:128, column:column + 128] = high
            w_first[level, 128:256, column:column + 128] = high
            w_first[level, 0:128, column + 128:column + 256] = rest
            w_first[level, 128:256, column + 128:column + 256] = none
        inner = lanes(wide) < 64
        for part, keep in enumerate((inner, ~inner)):
            high, rest = split(jnp.where(keep, low, 0.0))
            row = 256 * part
            w_zero[level, row:row + 128, 0:128] = high
            w_zero[level, row + 128:row + 256, 0:128] = high
            w_zero[level, row:row + 128, 128:256] = rest
            w_zero[level, row + 128:row + 256, 128:256] = none
        half = (64, 128)
        low, both = banded(taps_ref, rows(half) - lanes(half) % 64, 1 << level)
        for kind, matrix in enumerate((low, both)):
            high, rest = split(matrix)
            w_second[2 * level + kind, 0:64] = high
            w_second[2 * level + kind, 64:128] = high
            w_second[2 * level + kind, 128:192] = rest
            w_second[2 * level + kind, 192:256] = jnp.zeros(half, BF16)


def read_tables(wave_s, pairs_s, base, slots, info_s):
    found = []
    need = [False] * 6
    for p in range(slots):
        field, wavelet = pairs_s[0, base + p], pairs_s[1, base + p]
        safe = jnp.maximum(field, 0)
        live = field >= 0
        source = wave_s[0, safe] * 3 + wave_s[1, safe]
        level, orient = wave_s[0, wavelet], wave_s[1, wavelet]
        key = jnp.where(live, (source * 4 + level) * 4 + orient, -1)
        twin = jnp.int32(-1)
        for q in range(p - 1, -1, -1):
            twin = jnp.where(found[q] == key, q, twin)
        found.append(key)
        info_s[p] = jnp.where(live, jnp.where(twin >= 0, 3, level), 0)
        info_s[slots + p] = source
        info_s[2 * slots + p] = orient
        info_s[3 * slots + p] = jnp.maximum(twin, 0)
        for k in range(6):
            need[k] = need[k] | (live & (source == k))
    for k in range(6):
        info_s[4 * slots + k] = need[k].astype(jnp.int32)


def needed(info_s, slots):
    return [[info_s[4 * slots + level * 3 + orient] > 0 for orient in range(3)] for level in range(2)]


def first_rows(need, starts, tile_rows, taps_ref, w_first, w_zero, grid_ref, m_ref, low_lhs, both_lhs, z_ref):
    rank = lax.axis_index("space")
    total = lax.axis_size("space") * tile_rows

    def x_pass(level, kind, start):
        taps = [taps_ref[kind, t] for t in range(TAPS)]
        parts = []
        for h in range(2 - level):
            sums = [None] * 8
            for r in range((29, 22)[level]):
                if level == 0:
                    value = grid_ref[2 * start + HALF + FRONT + r, 8 * h:8 * h + 8, :]
                else:
                    value = grid_ref[2 * (start + r) + FRONT, pl.ds(0, 8, stride=2), :]
                for i in range(8):
                    t = r - (2 - level) * i
                    if 0 <= t < TAPS:
                        term = taps[t] * value
                        sums[i] = term if sums[i] is None else sums[i] + term
            parts.append(sums)
        if level == 0:
            return [jnp.concatenate([parts[0][i], parts[1][i]], axis=0) for i in range(8)]
        return [jnp.concatenate([parts[0][i], parts[0][i + 1]], axis=0) for i in range(0, 8, 2)]

    def put(level, kind, n, start, lhs_ref, column):
        for i, value in enumerate(x_pass(level, kind, start)):
            high, rest = split(value)
            at = n * (128 >> level) + i * 16
            lhs_ref[at:at + 16, column:column + 128] = high
            lhs_ref[at:at + 16, column + 128:column + 256] = rest

    def finish(level, orient):
        height = 16 >> level
        taps = taps_ref.at[BOTH if orient == 1 else LOW]
        for n, start in enumerate(starts[level]):
            values = [z_ref[pl.ds(n * 8 * height + y, 8, stride=height), :] for y in range(height)]
            i = start + rows(TILE)
            x = rank * tile_rows - 28 + 2 * i
            inside = (x >= 0) & (x < total) & (i >= 0) & (i < KEPT)
            place = m_ref.at[level * 3 + orient].reshape(STORED * 8, 128)
            for j in range(8):
                terms = [(y - (2 - level) * j + HALF, y) for y in range(height)]
                out = modulus(weigh(taps, values, [(t, y) for t, y in terms if 0 <= t < TAPS]))
                place[pl.ds((start + SHIFT) * 8 + j, 8, stride=8), :] = jnp.where(inside, out, 0.0)

    for level in range(2):
        per = 128 >> level
        size = per * len(starts[level])

        @pl.when(need[level][1] | need[level][2])
        def _():
            for n, start in enumerate(starts[level]):
                put(level, LOW, n, start, low_lhs, 0)

        for orient in (1, 2):
            @pl.when(need[level][orient])
            def _():
                z = dot(low_lhs[0:size, :], w_first[level, :, 256 * (orient - 1):256 * orient])
                z_ref[0:size, :] = z[:, 0:128] + z[:, 128:256]
                finish(level, orient)

        @pl.when(need[level][0])
        def _():
            for n, start in enumerate(starts[level]):
                put(level, EVEN, n, start, both_lhs, 0)
                put(level, ODD, n, start, both_lhs, 256)
            z = dot(both_lhs[0:size, :], w_zero[level])
            z_ref[0:size, :] = z[:, 0:128] + z[:, 128:256]
            finish(level, 0)


def second_order(need, slots, info_s, taps_ref, w_second, m_ref, out_ref, lhs_second, z2_ref, line_ref, done_ref, sems):
    left = lanes((16, 128)) < 64
    for level in range(2):
        for orient in range(3):
            @pl.when(need[level][orient])
            def _():
                source = level * 3 + orient
                for i in range(0, KEPT, 2):
                    value = jnp.concatenate([m_ref[source, i + SHIFT], m_ref[source, i + 1 + SHIFT]], axis=0)
                    high = value.astype(BF16)
                    wide = high.astype(F32)
                    pair = jnp.where(left, wide, value - wide).astype(BF16)
                    lhs_second[source, i * 8:i * 8 + 16, 0:128] = pair
                    lhs_second[source, i * 8:i * 8 + 16, 128:256] = high

    def z_pass(p, buffer):
        kind = 2 * (info_s[p] == 2).astype(jnp.int32) + (info_s[2 * slots + p] == 2).astype(jnp.int32)
        z2_ref[buffer] = dot(lhs_second[info_s[slots + p]], w_second[kind]).reshape(KEPT, 8, 128)

    def copy(p):
        return pltpu.make_async_copy(done_ref.at[p], out_ref.at[p], sems.at[p])

    def one_pair(p, carry):
        mode, orient = info_s[p], info_s[2 * slots + p]
        buffer = p % 2
        following = jnp.minimum(p + 1, slots - 1)

        def work(dilation):
            z_pass(following, 1 - buffer)
            x_taps = taps_ref.at[jnp.where(orient == 0, BOTH, LOW)]
            y_taps = taps_ref.at[jnp.where(orient == 1, BOTH, LOW)]
            place = done_ref.at[p].reshape(done_ref.shape[1] * 8, 64)
            for c in range(0, 32, 16):
                taps = [x_taps[t] for t in range(TAPS)]
                sums = [None] * 16
                first = c + 14 - HALF * dilation
                for r in range(15 + 14 * dilation + 1):
                    value = z2_ref[buffer, first + r]
                    for i in range(16):
                        if (r - i) % dilation == 0 and 0 <= (r - i) // dilation < TAPS:
                            term = taps[(r - i) // dilation] * value
                            sums[i] = term if sums[i] is None else sums[i] + term
                for i in range(16):
                    line_ref[(c + i) * 8:(c + i) * 8 + 8, :] = sums[i]
            for c in range(4):
                lines = [line_ref[pl.ds(c * 64 + y, 8, stride=8), :] for y in range(8)]
                for j in range(8):
                    terms = [((y - j) // dilation + HALF, y) for y in range(8) if (y - j) % dilation == 0]
                    out = modulus(weigh(y_taps, lines, terms))
                    place[pl.ds(c * 64 + j, 8, stride=8), :] = out[:, 0:64]

        for dilation in (1, 2):
            @pl.when(mode == dilation)
            def _():
                work(dilation)

        @pl.when(mode == 3)
        def _():
            z_pass(following, 1 - buffer)
            done_ref[p] = done_ref[info_s[3 * slots + p]]

        @pl.when(mode == 0)
        def _():
            done_ref[p] = jnp.zeros(done_ref.shape[1:], F32)

        copy(p).start()
        return carry

    z_pass(0, 0)
    lax.fori_loop(0, slots, one_pair, 0)
    for p in range(slots):
        copy(p).wait()


def inner_body(
    even_ref, odd_ref, low_ref, wave_ref, pairs_ref, own_ref,
    taps_ref, w_first, w_zero, w_second, grid_ref, m_ref, info_s,
    even_s, odd_s, low_s, wave_s, pairs_s, low_lhs, both_lhs, z_ref, sems, *, slots,
):
    tile_rows = own_ref.shape[0]
    moves = (
        (even_ref, even_s), (odd_ref, odd_s), (low_ref, low_s), (wave_ref, wave_s), (pairs_ref, pairs_s),
        (own_ref, grid_ref.at[pl.ds(FRONT + HALO, tile_rows)]),
    )
    copies = [pltpu.make_async_copy(source, place, sems.at[n]) for n, (source, place) in enumerate(moves)]
    for copy in copies:
        copy.start()
    for copy in copies[:-1]:
        copy.wait()
    make_filters(even_s, odd_s, low_s, taps_ref, w_first, w_zero, w_second)
    read_tables(wave_s, pairs_s, lax.axis_index("wave") * slots, slots, info_s)
    copies[-1].wait()
    first_rows(needed(info_s, slots), INNER, tile_rows, taps_ref, w_first, w_zero, grid_ref, m_ref, low_lhs, both_lhs, z_ref)


def outer_body(
    info_s, got_ref, other_ref, taps_ref, w_first, w_zero, w_second, grid_in, m_in,
    out_ref, grid_ref, m_ref, low_lhs, both_lhs, z_ref, lhs_second, z2_ref, line_ref, done_ref, sems, *, slots, tile_rows,
):
    upper = lax.axis_index("wave") % 2
    far = HALO + tile_rows
    for r in range(HALO):
        grid_ref[FRONT + (1 - upper) * far + r] = got_ref[r]
        grid_ref[FRONT + upper * far + r] = other_ref[r]
    need = needed(info_s, slots)
    starts = [a + b for a, b in zip(BEFORE, AFTER)]
    first_rows(need, starts, tile_rows, taps_ref, w_first, w_zero, grid_ref, m_ref, low_lhs, both_lhs, z_ref)
    second_order(need, slots, info_s, taps_ref, w_second, m_ref, out_ref, lhs_second, z2_ref, line_ref, done_ref, sems)


def shards(density, even_taps, odd_taps, low_taps, wavelets, pairs):
    tile_rows, ny, nz = density.shape
    count, waves = lax.axis_size("space"), lax.axis_size("wave")
    slots = pairs.shape[0] // waves
    upper = lax.axis_index("wave") % 2
    halo = lax.dynamic_slice_in_dim(density, upper * (tile_rows - HALO), HALO, 0)
    step = (-1, 1)
    moves = [
        (z * waves + w, (z + step[w % 2]) * waves + w)
        for z in range(count)
        for w in range(waves)
        if 0 <= z + step[w % 2] < count
    ]
    got = lax.ppermute(halo, ("space", "wave"), moves)

    smem = pl.BlockSpec(memory_space=pltpu.SMEM)
    vmem = pl.BlockSpec(memory_space=pltpu.VMEM)
    anywhere = pl.BlockSpec(memory_space=pl.ANY)
    params = pltpu.CompilerParams(vmem_limit_bytes=24 * 1024 * 1024)

    def held(value):
        return pltpu.with_memory_space_constraint(value, pltpu.VMEM)

    def far(value):
        return pltpu.with_memory_space_constraint(value, pltpu.HBM)

    def cost(us):
        return pl.CostEstimate(flops=us * 1000000000, bytes_accessed=us * 2500000, transcendentals=0)

    grid_type = pltpu.VMEM((WINDOW, ny, nz), F32)
    m_type = pltpu.VMEM((6, STORED, 8, 128), F32)
    out_shape = (slots, tile_rows // 2, ny // 2, nz // 2)
    scratch = [pltpu.VMEM((768, 256), BF16), pltpu.VMEM((768, 512), BF16), pltpu.VMEM((768, 128), F32)]
    taps, w_first, w_zero, w_second, grid, m, info = pl.pallas_call(
        functools.partial(inner_body, slots=slots),
        out_shape=[
            pltpu.VMEM((4, 16, 8, 128), F32),
            pltpu.VMEM((2, 256, 512), BF16),
            pltpu.VMEM((2, 512, 256), BF16),
            pltpu.VMEM((4, 256, 128), BF16),
            grid_type,
            m_type,
            pltpu.SMEM((4 * slots + 8,), jnp.int32),
        ],
        in_specs=[anywhere] * 6,
        out_specs=[vmem] * 6 + [smem],
        scratch_shapes=[
            pltpu.SMEM((TAPS,), F32),
            pltpu.SMEM((TAPS,), F32),
            pltpu.SMEM((TAPS,), F32),
            pltpu.SMEM(wavelets.shape[::-1], jnp.int32),
            pltpu.SMEM(pairs.shape[::-1], jnp.int32),
            *scratch,
            pltpu.SemaphoreType.DMA((6,)),
        ],
        compiler_params=params,
        cost_estimate=cost(3),
        name="inner_rows",
    )(*map(far, (even_taps, odd_taps, low_taps, wavelets.T, pairs.T, density)))
    got, grid = lax.optimization_barrier((got, grid))
    other = lax.ppermute(got, "wave", [(w, w ^ 1) for w in range(waves)])
    taps, w_first, w_zero, w_second, grid, m = map(held, (taps, w_first, w_zero, w_second, grid, m))
    info = pltpu.with_memory_space_constraint(info, pltpu.SMEM)
    second, _, _ = pl.pallas_call(
        functools.partial(outer_body, slots=slots, tile_rows=tile_rows),
        out_shape=[jax.ShapeDtypeStruct(out_shape, F32), grid_type, m_type],
        in_specs=[smem] + [vmem] * 8,
        out_specs=[anywhere, vmem, vmem],
        input_output_aliases={7: 1, 8: 2},
        scratch_shapes=scratch + [
            pltpu.VMEM((6, KEPT * 8, 256), BF16),
            pltpu.VMEM((2, KEPT, 8, 128), F32),
            pltpu.VMEM((256, 128), F32),
            pltpu.VMEM(out_shape, F32),
            pltpu.SemaphoreType.DMA((slots,)),
        ],
        compiler_params=params,
        cost_estimate=cost(5),
        name="outer_rows_and_pairs",
    )(info, held(got), held(other), taps, w_first, w_zero, w_second, grid, m)
    return second


def solution(mesh):
    placed = (P(("groups", "space"), None, None), P(), P(), P(), P(), P())
    return jax.shard_map(
        shards,
        mesh=mesh,
        in_specs=placed,
        out_specs=P("wave", ("groups", "space"), None, None),
        check_vma=False,
    )
```

```python
import functools

import jax
import jax.numpy as jnp
from jax import lax
from jax.experimental import pallas as pl
from jax.experimental.pallas import tpu as pltpu
from jax.sharding import PartitionSpec as P

TAPS = 15
HALF = 7
HALO = 42
FRONT = 8
WINDOW = 160
KEPT = 60
STORED = 72
SHIFT = 6
INNER = ((18, 26, 34), (21, 29))
BEFORE = ((-6, 2, 10), (-3, 5, 13))
AFTER = ((52, 42, 50), (36, 44, 52))
EDGE = (6, 0)
EPS = 1e-6
F32 = jnp.float32
BF16 = jnp.bfloat16
LOW, EVEN, ODD, BOTH = 0, 1, 2, 3
TILE = (8, 128)


def split(value):
    high = value.astype(BF16)
    return high, (value - high.astype(F32)).astype(BF16)


def dot(a, b):
    return jnp.dot(a, b, preferred_element_type=F32)


def rows(shape):
    return lax.broadcasted_iota(jnp.int32, shape, 0)


def lanes(shape):
    return lax.broadcasted_iota(jnp.int32, shape, 1)


def modulus(value):
    squares = value * value
    total = squares + pltpu.roll(squares, 64, 1) + EPS
    return total * lax.rsqrt(total)


def weigh(taps, values, pairs):
    acc = None
    for t, v in pairs:
        term = taps[t] * values[v]
        acc = term if acc is None else acc + term
    return acc


def banded(taps_ref, offset, dilation):
    low = both = jnp.zeros(offset.shape, F32)
    for t in range(TAPS):
        here = offset == (t - HALF) * dilation
        low = jnp.where(here, taps_ref[LOW, t][0:1], low)
        both = jnp.where(here, taps_ref[BOTH, t][0:1], both)
    return low, both


def make_filters(even_s, odd_s, low_s, taps_ref, w_first, w_second):
    left = lanes(TILE) < 64
    for t in range(TAPS):
        even = jnp.full(TILE, even_s[t], F32)
        odd = jnp.full(TILE, odd_s[t], F32)
        taps_ref[LOW, t] = jnp.full(TILE, low_s[t], F32)
        taps_ref[EVEN, t] = even
        taps_ref[ODD, t] = odd
        taps_ref[BOTH, t] = jnp.where(left, even, odd)
    wide = (128, 128)
    none = jnp.zeros(wide, BF16)
    for level in range(2):
        low, both = banded(taps_ref, rows(wide) - 2 * (lanes(wide) % 64), 1 << level)
        for kind, matrix in enumerate((low, both)):
            high, rest = split(matrix)
            column = 256 * kind
            w_first[level, 0:128, column:column + 128] = high
            w_first[level, 128:256, column:column + 128] = high
            w_first[level, 0:128, column + 128:column + 256] = rest
            w_first[level, 128:256, column + 128:column + 256] = none
        half = (64, 128)
        low, both = banded(taps_ref, rows(half) - lanes(half) % 64, 1 << level)
        for kind, matrix in enumerate((low, both)):
            high, rest = split(matrix)
            w_second[2 * level + kind, 0:64] = high
            w_second[2 * level + kind, 64:128] = high
            w_second[2 * level + kind, 128:192] = rest
            w_second[2 * level + kind, 192:256] = jnp.zeros(half, BF16)


def read_tables(wave_s, pairs_s, base, slots, info_s):
    found = []
    need = [False] * 6
    for p in range(slots):
        field, wavelet = pairs_s[0, base + p], pairs_s[1, base + p]
        safe = jnp.maximum(field, 0)
        live = field >= 0
        source = wave_s[0, safe] * 3 + wave_s[1, safe]
        level, orient = wave_s[0, wavelet], wave_s[1, wavelet]
        key = jnp.where(live, (source * 4 + level) * 4 + orient, -1)
        twin = jnp.int32(-1)
        for q in range(p - 1, -1, -1):
            twin = jnp.where(found[q] == key, q, twin)
        found.append(key)
        info_s[p] = jnp.where(live, jnp.where(twin >= 0, 3, level), 0)
        info_s[slots + p] = source
        info_s[2 * slots + p] = orient
        info_s[3 * slots + p] = jnp.maximum(twin, 0)
        for k in range(6):
            need[k] = need[k] | (live & (source == k))
    for k in range(6):
        info_s[4 * slots + k] = need[k].astype(jnp.int32)


def needed(info_s, slots):
    return [[info_s[4 * slots + level * 3 + orient] > 0 for orient in range(3)] for level in range(2)]


def filter_rows(need, place, count, w_first, grid_ref, low_refs, low_lhs):
    @pl.when(need[0][0])
    def _():
        for r in range(count):
            high, rest = split(grid_ref[place + r])
            low_lhs[r * 16:r * 16 + 16, 0:128] = high
            low_lhs[r * 16:r * 16 + 16, 128:256] = rest
        z = dot(low_lhs[0:count * 16, :], w_first[0, :, 0:256])
        low_refs[0][pl.ds(place, count)] = (z[:, 0:128] + z[:, 128:256]).reshape(count, 16, 128)

    @pl.when(need[1][0])
    def _():
        pairs = (count + 3) // 4
        for r in range(pairs):
            even = [grid_ref[place + 4 * r + n, pl.ds(0, 8, stride=2), :] for n in (0, 2)]
            high, rest = split(jnp.concatenate(even, axis=0))
            low_lhs[r * 16:r * 16 + 16, 0:128] = high
            low_lhs[r * 16:r * 16 + 16, 128:256] = rest
        z = dot(low_lhs[0:pairs * 16, :], w_first[1, :, 0:256])
        low_refs[1][pl.ds(place // 2, 2 * pairs)] = (z[:, 0:128] + z[:, 128:256]).reshape(2 * pairs, 8, 128)


def first_rows(need, starts, edge, tile_rows, taps_ref, w_first, grid_ref, low_refs, m_ref, low_lhs, z_ref):
    rank = lax.axis_index("space")
    total = lax.axis_size("space") * tile_rows

    def x_pass(level, kind, n, start):
        taps = [taps_ref[kind, t] for t in range(TAPS)]
        skip = edge[level] if n == 0 else 0
        stride = 2 - level
        parts = []
        for h in range(2 - level):
            sums = [None] * 8
            for r in range(stride * skip, stride * 7 + TAPS):
                if level == 0:
                    ref = low_refs[0] if kind == BOTH else grid_ref
                    value = ref[2 * start + HALF + FRONT + r, 8 * h:8 * h + 8, :]
                elif kind == BOTH:
                    value = low_refs[1][start + r + FRONT // 2]
                else:
                    value = grid_ref[2 * (start + r) + FRONT, pl.ds(0, 8, stride=2), :]
                for i in range(skip, 8):
                    t = r - stride * i
                    if 0 <= t < TAPS:
                        term = taps[t] * value
                        sums[i] = term if sums[i] is None else sums[i] + term
            parts.append(sums)
        if level == 0:
            return [(i * 16, jnp.concatenate([parts[0][i], parts[1][i]], axis=0)) for i in range(skip, 8)]
        return [(i * 8, jnp.concatenate([parts[0][i], parts[0][i + 1]], axis=0)) for i in range(skip, 8, 2)]

    def finish(level, orient):
        height = 16 >> level
        taps = taps_ref.at[BOTH if orient == 1 else LOW]
        place = m_ref.at[level * 3 + orient].reshape(STORED * 8, 128)
        for n, start in enumerate(starts[level]):
            values = [z_ref[pl.ds(n * 8 * height + y, 8, stride=height), :] for y in range(height)]
            i = start + rows(TILE)
            x = rank * tile_rows - 28 + 2 * i
            inside = (x >= 0) & (x < total) & (i >= 0) & (i < KEPT)
            for j in range(8):
                terms = [(y - (2 - level) * j + HALF, y) for y in range(height)]
                out = modulus(weigh(taps, values, [(t, y) for t, y in terms if 0 <= t < TAPS]))
                place[pl.ds((start + SHIFT) * 8 + j, 8, stride=8), :] = jnp.where(inside, out, 0.0)

    for level in range(2):
        per = 128 >> level
        first, size = edge[level] * (16 >> level), per * len(starts[level])

        @pl.when(need[level][1] | need[level][2])
        def _():
            for n, start in enumerate(starts[level]):
                for at, value in x_pass(level, LOW, n, start):
                    high, rest = split(value)
                    at += n * per
                    low_lhs[at:at + 16, 0:128] = high
                    low_lhs[at:at + 16, 128:256] = rest

        for orient in (1, 2):
            @pl.when(need[level][orient])
            def _():
                z = dot(low_lhs[first:size, :], w_first[level, :, 256 * (orient - 1):256 * orient])
                z_ref[first:size, :] = z[:, 0:128] + z[:, 128:256]
                finish(level, orient)

        @pl.when(need[level][0])
        def _():
            for n, start in enumerate(starts[level]):
                for at, value in x_pass(level, BOTH, n, start):
                    at += n * per
                    z_ref[at:at + 16, :] = value
            finish(level, 0)


def second_order(need, slots, info_s, taps_ref, w_second, m_ref, out_ref, lhs_second, z2_ref, line_ref, done_ref, sems):
    left = lanes((16, 128)) < 64
    for level in range(2):
        for orient in range(3):
            @pl.when(need[level][orient])
            def _():
                source = level * 3 + orient
                for i in range(0, KEPT, 2):
                    value = jnp.concatenate([m_ref[source, i + SHIFT], m_ref[source, i + 1 + SHIFT]], axis=0)
                    high = value.astype(BF16)
                    wide = high.astype(F32)
                    pair = jnp.where(left, wide, value - wide).astype(BF16)
                    lhs_second[source, i * 8:i * 8 + 16, 0:128] = pair
                    lhs_second[source, i * 8:i * 8 + 16, 128:256] = high

    def z_pass(p, buffer):
        kind = 2 * (info_s[p] == 2).astype(jnp.int32) + (info_s[2 * slots + p] == 2).astype(jnp.int32)
        z2_ref[buffer] = dot(lhs_second[info_s[slots + p]], w_second[kind]).reshape(KEPT, 8, 128)

    def copy(p):
        return pltpu.make_async_copy(done_ref.at[p], out_ref.at[p], sems.at[p])

    def one_pair(p, carry):
        mode, orient = info_s[p], info_s[2 * slots + p]
        buffer = p % 2
        following = jnp.minimum(p + 1, slots - 1)

        def work(dilation):
            z_pass(following, 1 - buffer)
            x_taps = taps_ref.at[jnp.where(orient == 0, BOTH, LOW)]
            y_taps = taps_ref.at[jnp.where(orient == 1, BOTH, LOW)]
            place = done_ref.at[p].reshape(done_ref.shape[1] * 8, 64)
            for c in range(0, 32, 16):
                taps = [x_taps[t] for t in range(TAPS)]
                sums = [None] * 16
                first = c + 14 - HALF * dilation
                for r in range(15 + 14 * dilation + 1):
                    value = z2_ref[buffer, first + r]
                    for i in range(16):
                        if (r - i) % dilation == 0 and 0 <= (r - i) // dilation < TAPS:
                            term = taps[(r - i) // dilation] * value
                            sums[i] = term if sums[i] is None else sums[i] + term
                for i in range(16):
                    line_ref[(c + i) * 8:(c + i) * 8 + 8, :] = sums[i]
            for c in range(4):
                lines = [line_ref[pl.ds(c * 64 + y, 8, stride=8), :] for y in range(8)]
                for j in range(8):
                    terms = [((y - j) // dilation + HALF, y) for y in range(8) if (y - j) % dilation == 0]
                    out = modulus(weigh(y_taps, lines, terms))
                    place[pl.ds(c * 64 + j, 8, stride=8), :] = out[:, 0:64]

        for dilation in (1, 2):
            @pl.when(mode == dilation)
            def _():
                work(dilation)

        @pl.when(mode == 3)
        def _():
            z_pass(following, 1 - buffer)
            done_ref[p] = done_ref[info_s[3 * slots + p]]

        @pl.when(mode == 0)
        def _():
            done_ref[p] = jnp.zeros(done_ref.shape[1:], F32)

        copy(p).start()
        return carry

    z_pass(0, 0)
    lax.fori_loop(0, slots, one_pair, 0)
    for p in range(slots):
        copy(p).wait()


def inner_body(
    even_ref, odd_ref, low_ref, wave_ref, pairs_ref, own_ref,
    taps_ref, w_first, w_second, grid_ref, low_zero, low_one, m_ref, info_s,
    even_s, odd_s, low_s, wave_s, pairs_s, low_lhs, z_ref, sems, *, slots,
):
    tile_rows = own_ref.shape[0]
    moves = (
        (even_ref, even_s), (odd_ref, odd_s), (low_ref, low_s), (wave_ref, wave_s), (pairs_ref, pairs_s),
        (own_ref, grid_ref.at[pl.ds(FRONT + HALO, tile_rows)]),
    )
    copies = [pltpu.make_async_copy(source, place, sems.at[n]) for n, (source, place) in enumerate(moves)]
    for copy in copies:
        copy.start()
    for copy in copies[:-1]:
        copy.wait()
    make_filters(even_s, odd_s, low_s, taps_ref, w_first, w_second)
    read_tables(wave_s, pairs_s, lax.axis_index("wave") * slots, slots, info_s)
    copies[-1].wait()
    need = needed(info_s, slots)
    low_refs = (low_zero, low_one)
    filter_rows(need, FRONT + HALO, tile_rows, w_first, grid_ref, low_refs, low_lhs)
    first_rows(need, INNER, (0, 0), tile_rows, taps_ref, w_first, grid_ref, low_refs, m_ref, low_lhs, z_ref)


def add_side(side, info_s, halo_ref, taps_ref, w_first, grid_ref, low_refs, m_ref, low_lhs, z_ref, slots, tile_rows):
    place = FRONT + (1 - side) * (HALO + tile_rows)
    for r in range(HALO):
        grid_ref[place + r] = halo_ref[r]
    need = needed(info_s, slots)
    filter_rows(need, place, HALO, w_first, grid_ref, low_refs, low_lhs)
    starts = [[jnp.where(side == 1, x, y) for x, y in zip(*both)] for both in zip(BEFORE, AFTER)]
    first_rows(need, starts, EDGE, tile_rows, taps_ref, w_first, grid_ref, low_refs, m_ref, low_lhs, z_ref)
    return need


def side_body(
    info_s, got_ref, taps_ref, w_first, grid_in, zero_in, one_in, m_in,
    grid_ref, low_zero, low_one, m_ref, low_lhs, z_ref, *, slots, tile_rows,
):
    side = lax.axis_index("wave") % 2
    add_side(side, info_s, got_ref, taps_ref, w_first, grid_ref, (low_zero, low_one), m_ref, low_lhs, z_ref, slots, tile_rows)


def last_body(
    info_s, other_ref, taps_ref, w_first, grid_in, zero_in, one_in, m_in, w_second,
    out_ref, grid_ref, low_zero, low_one, m_ref, low_lhs, z_ref, lhs_second, z2_ref, line_ref, done_ref, sems,
    *, slots, tile_rows,
):
    side = 1 - lax.axis_index("wave") % 2
    need = add_side(side, info_s, other_ref, taps_ref, w_first, grid_ref, (low_zero, low_one), m_ref, low_lhs, z_ref, slots, tile_rows)
    second_order(need, slots, info_s, taps_ref, w_second, m_ref, out_ref, lhs_second, z2_ref, line_ref, done_ref, sems)


def shards(density, even_taps, odd_taps, low_taps, wavelets, pairs):
    tile_rows, ny, nz = density.shape
    count, waves = lax.axis_size("space"), lax.axis_size("wave")
    slots = pairs.shape[0] // waves
    upper = lax.axis_index("wave") % 2
    halo = lax.dynamic_slice_in_dim(density, upper * (tile_rows - HALO), HALO, 0)
    step = (-1, 1)
    moves = [
        (z * waves + w, (z + step[w % 2]) * waves + w)
        for z in range(count)
        for w in range(waves)
        if 0 <= z + step[w % 2] < count
    ]
    got = lax.ppermute(halo, ("space", "wave"), moves)

    smem = pl.BlockSpec(memory_space=pltpu.SMEM)
    vmem = pl.BlockSpec(memory_space=pltpu.VMEM)
    anywhere = pl.BlockSpec(memory_space=pl.ANY)
    params = pltpu.CompilerParams(vmem_limit_bytes=24 * 1024 * 1024)

    def held(value):
        return pltpu.with_memory_space_constraint(value, pltpu.VMEM)

    def far(value):
        return pltpu.with_memory_space_constraint(value, pltpu.HBM)

    def cost(us):
        return pl.CostEstimate(flops=us * 1000000000, bytes_accessed=us * 2500000, transcendentals=0)

    state_types = [
        pltpu.VMEM((WINDOW, ny, nz), F32),
        pltpu.VMEM((WINDOW, ny, nz), F32),
        pltpu.VMEM((WINDOW // 2, ny // 2, nz), F32),
        pltpu.VMEM((6, STORED, 8, 128), F32),
    ]
    out_shape = (slots, tile_rows // 2, ny // 2, nz // 2)
    scratch = [pltpu.VMEM((1024, 256), BF16), pltpu.VMEM((384, 128), F32)]
    taps, w_first, w_second, *state, info = pl.pallas_call(
        functools.partial(inner_body, slots=slots),
        out_shape=[
            pltpu.VMEM((4, 16, 8, 128), F32),
            pltpu.VMEM((2, 256, 512), BF16),
            pltpu.VMEM((4, 256, 128), BF16),
            *state_types,
            pltpu.SMEM((4 * slots + 8,), jnp.int32),
        ],
        in_specs=[anywhere] * 6,
        out_specs=[vmem] * 7 + [smem],
        scratch_shapes=[
            pltpu.SMEM((TAPS,), F32),
            pltpu.SMEM((TAPS,), F32),
            pltpu.SMEM((TAPS,), F32),
            pltpu.SMEM(wavelets.shape[::-1], jnp.int32),
            pltpu.SMEM(pairs.shape[::-1], jnp.int32),
            *scratch,
            pltpu.SemaphoreType.DMA((6,)),
        ],
        compiler_params=params,
        cost_estimate=cost(3),
        name="inner_rows",
    )(*map(far, (even_taps, odd_taps, low_taps, wavelets.T, pairs.T, density)))
    got, state[0] = lax.optimization_barrier((got, state[0]))
    other = lax.ppermute(got, "wave", [(w, w ^ 1) for w in range(waves)])
    taps, w_first, w_second = map(held, (taps, w_first, w_second))
    info = pltpu.with_memory_space_constraint(info, pltpu.SMEM)
    state = pl.pallas_call(
        functools.partial(side_body, slots=slots, tile_rows=tile_rows),
        out_shape=state_types,
        in_specs=[smem] + [vmem] * 7,
        out_specs=[vmem] * 4,
        input_output_aliases={4: 0, 5: 1, 6: 2, 7: 3},
        scratch_shapes=scratch,
        compiler_params=params,
        cost_estimate=cost(2),
        name="side_rows",
    )(info, held(got), taps, w_first, *map(held, state))
    second, *_ = pl.pallas_call(
        functools.partial(last_body, slots=slots, tile_rows=tile_rows),
        out_shape=[jax.ShapeDtypeStruct(out_shape, F32), *state_types],
        in_specs=[smem] + [vmem] * 8,
        out_specs=[anywhere] + [vmem] * 4,
        input_output_aliases={4: 1, 5: 2, 6: 3, 7: 4},
        scratch_shapes=scratch + [
            pltpu.VMEM((6, KEPT * 8, 256), BF16),
            pltpu.VMEM((2, KEPT, 8, 128), F32),
            pltpu.VMEM((256, 128), F32),
            pltpu.VMEM(out_shape, F32),
            pltpu.SemaphoreType.DMA((slots,)),
        ],
        compiler_params=params,
        cost_estimate=cost(5),
        name="side_rows_and_pairs",
    )(info, held(other), taps, w_first, *map(held, state), w_second)
    return second


def solution(mesh):
    placed = (P(("groups", "space"), None, None), P(), P(), P(), P(), P())
    return jax.shard_map(
        shards,
        mesh=mesh,
        in_specs=placed,
        out_specs=P("wave", ("groups", "space"), None, None),
        check_vma=False,
    )
```

```python
import functools

import jax
import jax.numpy as jnp
from jax import lax
from jax.experimental import pallas as pl
from jax.experimental.pallas import tpu as pltpu
from jax.sharding import PartitionSpec as P

TAPS = 15
HALF = 7
HALO = 42
FRONT = 8
WINDOW = 160
KEPT = 60
STORED = 72
SHIFT = 6
INNER = ((18, 26, 34), (21, 29))
BEFORE = ((-6, 2, 10), (-3, 5, 13))
AFTER = ((52, 42, 50), (36, 44, 52))
EDGE = (6, 0)
EPS = 1e-6
F32 = jnp.float32
BF16 = jnp.bfloat16
LOW, EVEN, ODD, BOTH = 0, 1, 2, 3
TILE = (8, 128)


def split(value):
    high = value.astype(BF16)
    return high, (value - high.astype(F32)).astype(BF16)


def dot(a, b):
    return jnp.dot(a, b, preferred_element_type=F32)


def rows(shape):
    return lax.broadcasted_iota(jnp.int32, shape, 0)


def lanes(shape):
    return lax.broadcasted_iota(jnp.int32, shape, 1)


def modulus(value):
    squares = value * value
    total = squares + pltpu.roll(squares, 64, 1) + EPS
    return total * lax.rsqrt(total)


def weigh(taps, values, pairs):
    acc = None
    for t, v in pairs:
        term = taps[t] * values[v]
        acc = term if acc is None else acc + term
    return acc


def banded(taps_ref, offset, dilation):
    low = both = jnp.zeros(offset.shape, F32)
    for t in range(TAPS):
        here = offset == (t - HALF) * dilation
        low = jnp.where(here, taps_ref[LOW, t][0:1], low)
        both = jnp.where(here, taps_ref[BOTH, t][0:1], both)
    return low, both


def make_filters(even_s, odd_s, low_s, taps_ref, w_first, w_second):
    left = lanes(TILE) < 64
    for t in range(TAPS):
        even = jnp.full(TILE, even_s[t], F32)
        odd = jnp.full(TILE, odd_s[t], F32)
        taps_ref[LOW, t] = jnp.full(TILE, low_s[t], F32)
        taps_ref[EVEN, t] = even
        taps_ref[ODD, t] = odd
        taps_ref[BOTH, t] = jnp.where(left, even, odd)
    wide = (128, 128)
    none = jnp.zeros(wide, BF16)
    for level in range(2):
        low, both = banded(taps_ref, rows(wide) - 2 * (lanes(wide) % 64), 1 << level)
        for kind, matrix in enumerate((low, both)):
            high, rest = split(matrix)
            column = 256 * kind
            w_first[level, 0:128, column:column + 128] = high
            w_first[level, 128:256, column:column + 128] = high
            w_first[level, 0:128, column + 128:column + 256] = rest
            w_first[level, 128:256, column + 128:column + 256] = none
        half = (64, 128)
        low, both = banded(taps_ref, rows(half) - lanes(half) % 64, 1 << level)
        for kind, matrix in enumerate((low, both)):
            high, rest = split(matrix)
            w_second[2 * level + kind, 0:64] = high
            w_second[2 * level + kind, 64:128] = high
            w_second[2 * level + kind, 128:192] = rest
            w_second[2 * level + kind, 192:256] = jnp.zeros(half, BF16)


def read_tables(wave_s, pairs_s, base, slots, info_s):
    found = []
    need = [False] * 6
    for p in range(slots):
        field, wavelet = pairs_s[0, base + p], pairs_s[1, base + p]
        safe = jnp.maximum(field, 0)
        live = field >= 0
        source = wave_s[0, safe] * 3 + wave_s[1, safe]
        level, orient = wave_s[0, wavelet], wave_s[1, wavelet]
        key = jnp.where(live, (source * 4 + level) * 4 + orient, -1)
        twin = jnp.int32(-1)
        for q in range(p - 1, -1, -1):
            twin = jnp.where(found[q] == key, q, twin)
        found.append(key)
        info_s[p] = jnp.where(live, jnp.where(twin >= 0, 3, level), 0)
        info_s[slots + p] = source
        info_s[2 * slots + p] = orient
        info_s[3 * slots + p] = jnp.maximum(twin, 0)
        for k in range(6):
            need[k] = need[k] | (live & (source == k))
    for k in range(6):
        info_s[4 * slots + k] = need[k].astype(jnp.int32)


def needed(info_s, slots):
    return [[info_s[4 * slots + level * 3 + orient] > 0 for orient in range(3)] for level in range(2)]


def filter_rows(need, place, count, w_first, grid_ref, low_refs, low_lhs):
    @pl.when(need[0][0])
    def _():
        for r in range(count):
            high, rest = split(grid_ref[place + r])
            low_lhs[r * 16:r * 16 + 16, 0:128] = high
            low_lhs[r * 16:r * 16 + 16, 128:256] = rest
        z = dot(low_lhs[0:count * 16, :], w_first[0, :, 0:256])
        low_refs[0][pl.ds(place, count)] = (z[:, 0:128] + z[:, 128:256]).reshape(count, 16, 128)

    @pl.when(need[1][0])
    def _():
        pairs = (count + 3) // 4
        for r in range(pairs):
            even = [grid_ref[place + 4 * r + n, pl.ds(0, 8, stride=2), :] for n in (0, 2)]
            high, rest = split(jnp.concatenate(even, axis=0))
            low_lhs[r * 16:r * 16 + 16, 0:128] = high
            low_lhs[r * 16:r * 16 + 16, 128:256] = rest
        z = dot(low_lhs[0:pairs * 16, :], w_first[1, :, 0:256])
        low_refs[1][pl.ds(place // 2, 2 * pairs)] = (z[:, 0:128] + z[:, 128:256]).reshape(2 * pairs, 8, 128)


def first_rows(need, starts, edge, tile_rows, taps_ref, w_first, grid_ref, low_refs, m_ref, low_lhs, z_ref):
    rank = lax.axis_index("space")
    total = lax.axis_size("space") * tile_rows

    def x_pass(level, kind, n, start):
        taps = [taps_ref[kind, t] for t in range(TAPS)]
        skip = edge[level] if n == 0 else 0
        stride = 2 - level
        parts = []
        for h in range(2 - level):
            sums = [None] * 8
            for r in range(stride * skip, stride * 7 + TAPS):
                if level == 0:
                    ref = low_refs[0] if kind == BOTH else grid_ref
                    value = ref[2 * start + HALF + FRONT + r, 8 * h:8 * h + 8, :]
                elif kind == BOTH:
                    value = low_refs[1][start + r + FRONT // 2]
                else:
                    value = grid_ref[2 * (start + r) + FRONT, pl.ds(0, 8, stride=2), :]
                for i in range(skip, 8):
                    t = r - stride * i
                    if 0 <= t < TAPS:
                        term = taps[t] * value
                        sums[i] = term if sums[i] is None else sums[i] + term
            parts.append(sums)
        if level == 0:
            return [(i * 16, jnp.concatenate([parts[0][i], parts[1][i]], axis=0)) for i in range(skip, 8)]
        return [(i * 8, jnp.concatenate([parts[0][i], parts[0][i + 1]], axis=0)) for i in range(skip, 8, 2)]

    def finish(level, orient):
        height = 16 >> level
        taps = taps_ref.at[BOTH if orient == 1 else LOW]
        place = m_ref.at[level * 3 + orient].reshape(STORED * 8, 128)
        for n, start in enumerate(starts[level]):
            values = [z_ref[orient, pl.ds(n * 8 * height + y, 8, stride=height), :] for y in range(height)]
            i = start + rows(TILE)
            x = rank * tile_rows - 28 + 2 * i
            inside = (x >= 0) & (x < total) & (i >= 0) & (i < KEPT)
            for j in range(8):
                terms = [(y - (2 - level) * j + HALF, y) for y in range(height)]
                out = modulus(weigh(taps, values, [(t, y) for t, y in terms if 0 <= t < TAPS]))
                place[pl.ds((start + SHIFT) * 8 + j, 8, stride=8), :] = jnp.where(inside, out, 0.0)

    for level in range(2):
        per = 128 >> level
        first, size = edge[level] * (16 >> level), per * len(starts[level])

        @pl.when(need[level][1] | need[level][2])
        def _():
            for n, start in enumerate(starts[level]):
                for at, value in x_pass(level, LOW, n, start):
                    high, rest = split(value)
                    at += n * per
                    low_lhs[at:at + 16, 0:128] = high
                    low_lhs[at:at + 16, 128:256] = rest
            z = dot(low_lhs[first:size, :], w_first[level])
            z_ref[1, first:size, :] = z[:, 0:128] + z[:, 128:256]
            z_ref[2, first:size, :] = z[:, 256:384] + z[:, 384:512]

        for orient in (1, 2):
            @pl.when(need[level][orient])
            def _():
                finish(level, orient)

        @pl.when(need[level][0])
        def _():
            for n, start in enumerate(starts[level]):
                for at, value in x_pass(level, BOTH, n, start):
                    at += n * per
                    z_ref[0, at:at + 16, :] = value
            finish(level, 0)


def second_order(need, slots, info_s, taps_ref, w_second, m_ref, out_ref, lhs_second, z2_even, z2_odd, line_ref, done_ref, sems):
    left = lanes((16, 128)) < 64
    for level in range(2):
        for orient in range(3):
            @pl.when(need[level][orient])
            def _():
                source = level * 3 + orient
                for i in range(0, KEPT, 2):
                    value = jnp.concatenate([m_ref[source, i + SHIFT], m_ref[source, i + 1 + SHIFT]], axis=0)
                    high = value.astype(BF16)
                    wide = high.astype(F32)
                    pair = jnp.where(left, wide, value - wide).astype(BF16)
                    lhs_second[source, i * 8:i * 8 + 16, 0:128] = pair
                    lhs_second[source, i * 8:i * 8 + 16, 128:256] = high

    def z_pass(p, place):
        kind = 2 * (info_s[p] == 2).astype(jnp.int32) + (info_s[2 * slots + p] == 2).astype(jnp.int32)
        place[...] = dot(lhs_second[info_s[slots + p]], w_second[kind]).reshape(KEPT, 8, 128)

    def copy(p):
        return pltpu.make_async_copy(done_ref.at[p], out_ref.at[p], sems.at[p])

    def one_pair(p, here, there):
        mode, orient = info_s[p], info_s[2 * slots + p]
        following = jnp.minimum(p + 1, slots - 1)

        def work(dilation):
            z_pass(following, there)
            x_taps = taps_ref.at[jnp.where(orient == 0, BOTH, LOW)]
            y_taps = taps_ref.at[jnp.where(orient == 1, BOTH, LOW)]
            place = done_ref.at[p].reshape(done_ref.shape[1] * 8, 64)
            for c in range(0, 32, 16):
                taps = [x_taps[t] for t in range(TAPS)]
                sums = [None] * 16
                first = c + 14 - HALF * dilation
                for r in range(15 + 14 * dilation + 1):
                    value = here[first + r]
                    for i in range(16):
                        if (r - i) % dilation == 0 and 0 <= (r - i) // dilation < TAPS:
                            term = taps[(r - i) // dilation] * value
                            sums[i] = term if sums[i] is None else sums[i] + term
                for i in range(16):
                    line_ref[(c + i) * 8:(c + i) * 8 + 8, :] = sums[i]
            for c in range(4):
                lines = [line_ref[pl.ds(c * 64 + y, 8, stride=8), :] for y in range(8)]
                for j in range(8):
                    terms = [((y - j) // dilation + HALF, y) for y in range(8) if (y - j) % dilation == 0]
                    out = modulus(weigh(y_taps, lines, terms))
                    place[pl.ds(c * 64 + j, 8, stride=8), :] = out[:, 0:64]

        for dilation in (1, 2):
            @pl.when(mode == dilation)
            def _():
                work(dilation)

        @pl.when(mode == 3)
        def _():
            z_pass(following, there)
            done_ref[p] = done_ref[info_s[3 * slots + p]]

        @pl.when(mode == 0)
        def _():
            done_ref[p] = jnp.zeros(done_ref.shape[1:], F32)

        copy(p).start()

    def two_pairs(k, carry):
        one_pair(2 * k, z2_even, z2_odd)
        one_pair(2 * k + 1, z2_odd, z2_even)
        return carry

    z_pass(0, z2_even)
    lax.fori_loop(0, slots // 2, two_pairs, 0)
    for p in range(slots):
        copy(p).wait()


def inner_body(
    even_ref, odd_ref, low_ref, wave_ref, pairs_ref, own_ref,
    taps_ref, w_first, w_second, grid_ref, low_zero, low_one, m_ref, info_s,
    even_s, odd_s, low_s, wave_s, pairs_s, low_lhs, z_ref, sems, *, slots,
):
    tile_rows = own_ref.shape[0]
    moves = (
        (even_ref, even_s), (odd_ref, odd_s), (low_ref, low_s), (wave_ref, wave_s), (pairs_ref, pairs_s),
        (own_ref, grid_ref.at[pl.ds(FRONT + HALO, tile_rows)]),
    )
    copies = [pltpu.make_async_copy(source, place, sems.at[n]) for n, (source, place) in enumerate(moves)]
    for copy in copies:
        copy.start()
    for copy in copies[:-1]:
        copy.wait()
    make_filters(even_s, odd_s, low_s, taps_ref, w_first, w_second)
    read_tables(wave_s, pairs_s, lax.axis_index("wave") * slots, slots, info_s)
    copies[-1].wait()
    need = needed(info_s, slots)
    low_refs = (low_zero, low_one)
    filter_rows(need, FRONT + HALO, tile_rows, w_first, grid_ref, low_refs, low_lhs)
    first_rows(need, INNER, (0, 0), tile_rows, taps_ref, w_first, grid_ref, low_refs, m_ref, low_lhs, z_ref)


def add_side(side, info_s, halo_ref, taps_ref, w_first, grid_ref, low_refs, m_ref, low_lhs, z_ref, slots, tile_rows):
    place = FRONT + (1 - side) * (HALO + tile_rows)
    for r in range(HALO):
        grid_ref[place + r] = halo_ref[r]
    need = needed(info_s, slots)
    filter_rows(need, place, HALO, w_first, grid_ref, low_refs, low_lhs)
    starts = [[jnp.where(side == 1, x, y) for x, y in zip(*both)] for both in zip(BEFORE, AFTER)]
    first_rows(need, starts, EDGE, tile_rows, taps_ref, w_first, grid_ref, low_refs, m_ref, low_lhs, z_ref)
    return need


def side_body(
    info_s, got_ref, taps_ref, w_first, grid_in, zero_in, one_in, m_in,
    grid_ref, low_zero, low_one, m_ref, low_lhs, z_ref, *, slots, tile_rows,
):
    side = lax.axis_index("wave") % 2
    add_side(side, info_s, got_ref, taps_ref, w_first, grid_ref, (low_zero, low_one), m_ref, low_lhs, z_ref, slots, tile_rows)


def last_body(
    info_s, other_ref, taps_ref, w_first, grid_in, zero_in, one_in, m_in, w_second,
    out_ref, grid_ref, low_zero, low_one, m_ref, low_lhs, z_ref, lhs_second, z2_even, z2_odd, line_ref, done_ref, sems,
    *, slots, tile_rows,
):
    side = 1 - lax.axis_index("wave") % 2
    need = add_side(side, info_s, other_ref, taps_ref, w_first, grid_ref, (low_zero, low_one), m_ref, low_lhs, z_ref, slots, tile_rows)
    second_order(need, slots, info_s, taps_ref, w_second, m_ref, out_ref, lhs_second, z2_even, z2_odd, line_ref, done_ref, sems)


def shards(density, even_taps, odd_taps, low_taps, wavelets, pairs):
    tile_rows, ny, nz = density.shape
    count, waves = lax.axis_size("space"), lax.axis_size("wave")
    slots = pairs.shape[0] // waves
    upper = lax.axis_index("wave") % 2
    halo = lax.dynamic_slice_in_dim(density, upper * (tile_rows - HALO), HALO, 0)
    step = (-1, 1)
    moves = [
        (z * waves + w, (z + step[w % 2]) * waves + w)
        for z in range(count)
        for w in range(waves)
        if 0 <= z + step[w % 2] < count
    ]
    got = lax.ppermute(halo, ("space", "wave"), moves)

    smem = pl.BlockSpec(memory_space=pltpu.SMEM)
    vmem = pl.BlockSpec(memory_space=pltpu.VMEM)
    anywhere = pl.BlockSpec(memory_space=pl.ANY)
    params = pltpu.CompilerParams(vmem_limit_bytes=24 * 1024 * 1024)

    def held(value):
        return pltpu.with_memory_space_constraint(value, pltpu.VMEM)

    def far(value):
        return pltpu.with_memory_space_constraint(value, pltpu.HBM)

    def cost(us):
        return pl.CostEstimate(flops=us * 1000000000, bytes_accessed=us * 2500000, transcendentals=0)

    state_types = [
        pltpu.VMEM((WINDOW, ny, nz), F32),
        pltpu.VMEM((WINDOW, ny, nz), F32),
        pltpu.VMEM((WINDOW // 2, ny // 2, nz), F32),
        pltpu.VMEM((6, STORED, 8, 128), F32),
    ]
    out_shape = (slots, tile_rows // 2, ny // 2, nz // 2)
    scratch = [pltpu.VMEM((1024, 256), BF16), pltpu.VMEM((3, 384, 128), F32)]
    taps, w_first, w_second, *state, info = pl.pallas_call(
        functools.partial(inner_body, slots=slots),
        out_shape=[
            pltpu.VMEM((4, 16, 8, 128), F32),
            pltpu.VMEM((2, 256, 512), BF16),
            pltpu.VMEM((4, 256, 128), BF16),
            *state_types,
            pltpu.SMEM((4 * slots + 8,), jnp.int32),
        ],
        in_specs=[anywhere] * 6,
        out_specs=[vmem] * 7 + [smem],
        scratch_shapes=[
            pltpu.SMEM((TAPS,), F32),
            pltpu.SMEM((TAPS,), F32),
            pltpu.SMEM((TAPS,), F32),
            pltpu.SMEM(wavelets.shape[::-1], jnp.int32),
            pltpu.SMEM(pairs.shape[::-1], jnp.int32),
            *scratch,
            pltpu.SemaphoreType.DMA((6,)),
        ],
        compiler_params=params,
        cost_estimate=cost(3),
        name="inner_rows",
    )(*map(far, (even_taps, odd_taps, low_taps, wavelets.T, pairs.T, density)))
    got, state[0] = lax.optimization_barrier((got, state[0]))
    other = lax.ppermute(got, "wave", [(w, w ^ 1) for w in range(waves)])
    taps, w_first, w_second = map(held, (taps, w_first, w_second))
    info = pltpu.with_memory_space_constraint(info, pltpu.SMEM)
    state = pl.pallas_call(
        functools.partial(side_body, slots=slots, tile_rows=tile_rows),
        out_shape=state_types,
        in_specs=[smem] + [vmem] * 7,
        out_specs=[vmem] * 4,
        input_output_aliases={4: 0, 5: 1, 6: 2, 7: 3},
        scratch_shapes=scratch,
        compiler_params=params,
        cost_estimate=cost(2),
        name="side_rows",
    )(info, held(got), taps, w_first, *map(held, state))
    second, *_ = pl.pallas_call(
        functools.partial(last_body, slots=slots, tile_rows=tile_rows),
        out_shape=[jax.ShapeDtypeStruct(out_shape, F32), *state_types],
        in_specs=[smem] + [vmem] * 8,
        out_specs=[anywhere] + [vmem] * 4,
        input_output_aliases={4: 1, 5: 2, 6: 3, 7: 4},
        scratch_shapes=scratch + [
            pltpu.VMEM((6, KEPT * 8, 256), BF16),
            pltpu.VMEM((KEPT, 8, 128), F32),
            pltpu.VMEM((KEPT, 8, 128), F32),
            pltpu.VMEM((256, 128), F32),
            pltpu.VMEM(out_shape, F32),
            pltpu.SemaphoreType.DMA((slots,)),
        ],
        compiler_params=params,
        cost_estimate=cost(5),
        name="side_rows_and_pairs",
    )(info, held(other), taps, w_first, *map(held, state), w_second)
    return second


def solution(mesh):
    placed = (P(("groups", "space"), None, None), P(), P(), P(), P(), P())
    return jax.shard_map(
        shards,
        mesh=mesh,
        in_specs=placed,
        out_specs=P("wave", ("groups", "space"), None, None),
        check_vma=False,
    )
```

```python
import functools

import jax
import jax.numpy as jnp
from jax import lax
from jax.experimental import pallas as pl
from jax.experimental.pallas import tpu as pltpu
from jax.sharding import PartitionSpec as P

TAPS = 15
HALF = 7
HALO = 42
NEAR = 35
BEYOND = 4
SENT = NEAR + BEYOND // 2
FRONT = 8
WINDOW = 160
KEPT = 60
STORED = 72
SHIFT = 6
INNER = ((18, 26, 34), (21, 29))
BEFORE = ((-6, 2, 10), (-3, 5, 13))
AFTER = ((52, 42, 50), (36, 44, 52))
EDGE = (6, 0)
EPS = 1e-6
F32 = jnp.float32
BF16 = jnp.bfloat16
LOW, EVEN, ODD, BOTH = 0, 1, 2, 3
TILE = (8, 128)


def split(value):
    high = value.astype(BF16)
    return high, (value - high.astype(F32)).astype(BF16)


def dot(a, b):
    return jnp.dot(a, b, preferred_element_type=F32)


def rows(shape):
    return lax.broadcasted_iota(jnp.int32, shape, 0)


def lanes(shape):
    return lax.broadcasted_iota(jnp.int32, shape, 1)


def modulus(value):
    squares = value * value
    total = squares + pltpu.roll(squares, 64, 1) + EPS
    return total * lax.rsqrt(total)


def weigh(taps, values, pairs):
    acc = None
    for t, v in pairs:
        term = taps[t] * values[v]
        acc = term if acc is None else acc + term
    return acc


def banded(taps_ref, offset, dilation):
    low = both = jnp.zeros(offset.shape, F32)
    for t in range(TAPS):
        here = offset == (t - HALF) * dilation
        low = jnp.where(here, taps_ref[LOW, t][0:1], low)
        both = jnp.where(here, taps_ref[BOTH, t][0:1], both)
    return low, both


def make_filters(even_s, odd_s, low_s, taps_ref, w_first, w_second):
    left = lanes(TILE) < 64
    for t in range(TAPS):
        even = jnp.full(TILE, even_s[t], F32)
        odd = jnp.full(TILE, odd_s[t], F32)
        taps_ref[LOW, t] = jnp.full(TILE, low_s[t], F32)
        taps_ref[EVEN, t] = even
        taps_ref[ODD, t] = odd
        taps_ref[BOTH, t] = jnp.where(left, even, odd)
    wide = (128, 128)
    none = jnp.zeros(wide, BF16)
    for level in range(2):
        low, both = banded(taps_ref, rows(wide) - 2 * (lanes(wide) % 64), 1 << level)
        for kind, matrix in enumerate((low, both)):
            high, rest = split(matrix)
            column = 256 * kind
            w_first[level, 0:128, column:column + 128] = high
            w_first[level, 128:256, column:column + 128] = high
            w_first[level, 0:128, column + 128:column + 256] = rest
            w_first[level, 128:256, column + 128:column + 256] = none
        half = (64, 128)
        low, both = banded(taps_ref, rows(half) - lanes(half) % 64, 1 << level)
        for kind, matrix in enumerate((low, both)):
            high, rest = split(matrix)
            w_second[2 * level + kind, 0:64] = high
            w_second[2 * level + kind, 64:128] = high
            w_second[2 * level + kind, 128:192] = rest
            w_second[2 * level + kind, 192:256] = jnp.zeros(half, BF16)


def read_tables(wave_s, pairs_s, base, slots, info_s):
    found = []
    need = [False] * 6
    for p in range(slots):
        field, wavelet = pairs_s[0, base + p], pairs_s[1, base + p]
        safe = jnp.maximum(field, 0)
        live = field >= 0
        source = wave_s[0, safe] * 3 + wave_s[1, safe]
        level, orient = wave_s[0, wavelet], wave_s[1, wavelet]
        key = jnp.where(live, (source * 4 + level) * 4 + orient, -1)
        twin = jnp.int32(-1)
        for q in range(p - 1, -1, -1):
            twin = jnp.where(found[q] == key, q, twin)
        found.append(key)
        info_s[p] = jnp.where(live, jnp.where(twin >= 0, 3, level), 0)
        info_s[slots + p] = source
        info_s[2 * slots + p] = orient
        info_s[3 * slots + p] = jnp.maximum(twin, 0)
        for k in range(6):
            need[k] = need[k] | (live & (source == k))
    for k in range(6):
        info_s[4 * slots + k] = need[k].astype(jnp.int32)


def needed(info_s, slots):
    return [[info_s[4 * slots + level * 3 + orient] > 0 for orient in range(3)] for level in range(2)]


def filter_rows(need, spans, w_first, grid_ref, low_refs, low_lhs):
    @pl.when(need[0][0])
    def _():
        place, count = spans[0]
        for r in range(count):
            high, rest = split(grid_ref[place + r])
            low_lhs[r * 16:r * 16 + 16, 0:128] = high
            low_lhs[r * 16:r * 16 + 16, 128:256] = rest
        z = dot(low_lhs[0:count * 16, :], w_first[0, :, 0:256])
        low_refs[0][pl.ds(place, count)] = (z[:, 0:128] + z[:, 128:256]).reshape(count, 16, 128)

    @pl.when(need[1][0])
    def _():
        place, count = spans[1]
        pairs = (count + 3) // 4
        for r in range(pairs):
            even = [grid_ref[place + 4 * r + n, pl.ds(0, 8, stride=2), :] for n in (0, 2)]
            high, rest = split(jnp.concatenate(even, axis=0))
            low_lhs[r * 16:r * 16 + 16, 0:128] = high
            low_lhs[r * 16:r * 16 + 16, 128:256] = rest
        z = dot(low_lhs[0:pairs * 16, :], w_first[1, :, 0:256])
        low_refs[1][pl.ds(place // 2, 2 * pairs)] = (z[:, 0:128] + z[:, 128:256]).reshape(2 * pairs, 8, 128)


def first_rows(need, starts, edge, tile_rows, taps_ref, w_first, grid_ref, low_refs, m_ref, low_lhs, z_ref):
    rank = lax.axis_index("space")
    total = lax.axis_size("space") * tile_rows

    def x_pass(level, kind, n, start):
        taps = [taps_ref[kind, t] for t in range(TAPS)]
        skip = edge[level] if n == 0 else 0
        stride = 2 - level
        parts = []
        for h in range(2 - level):
            sums = [None] * 8
            for r in range(stride * skip, stride * 7 + TAPS):
                if level == 0:
                    ref = low_refs[0] if kind == BOTH else grid_ref
                    value = ref[2 * start + HALF + FRONT + r, 8 * h:8 * h + 8, :]
                elif kind == BOTH:
                    value = low_refs[1][start + r + FRONT // 2]
                else:
                    value = grid_ref[2 * (start + r) + FRONT, pl.ds(0, 8, stride=2), :]
                for i in range(skip, 8):
                    t = r - stride * i
                    if 0 <= t < TAPS:
                        term = taps[t] * value
                        sums[i] = term if sums[i] is None else sums[i] + term
            parts.append(sums)
        if level == 0:
            return [(i * 16, jnp.concatenate([parts[0][i], parts[1][i]], axis=0)) for i in range(skip, 8)]
        return [(i * 8, jnp.concatenate([parts[0][i], parts[0][i + 1]], axis=0)) for i in range(skip, 8, 2)]

    def finish(level, orient):
        height = 16 >> level
        taps = taps_ref.at[BOTH if orient == 1 else LOW]
        place = m_ref.at[level * 3 + orient].reshape(STORED * 8, 128)
        for n, start in enumerate(starts[level]):
            values = [z_ref[orient, pl.ds(n * 8 * height + y, 8, stride=height), :] for y in range(height)]
            i = start + rows(TILE)
            x = rank * tile_rows - 28 + 2 * i
            inside = (x >= 0) & (x < total) & (i >= 0) & (i < KEPT)
            for j in range(8):
                terms = [(y - (2 - level) * j + HALF, y) for y in range(height)]
                out = modulus(weigh(taps, values, [(t, y) for t, y in terms if 0 <= t < TAPS]))
                place[pl.ds((start + SHIFT) * 8 + j, 8, stride=8), :] = jnp.where(inside, out, 0.0)

    for level in range(2):
        per = 128 >> level
        first, size = edge[level] * (16 >> level), per * len(starts[level])

        @pl.when(need[level][1] | need[level][2])
        def _():
            for n, start in enumerate(starts[level]):
                for at, value in x_pass(level, LOW, n, start):
                    high, rest = split(value)
                    at += n * per
                    low_lhs[at:at + 16, 0:128] = high
                    low_lhs[at:at + 16, 128:256] = rest
            z = dot(low_lhs[first:size, :], w_first[level])
            z_ref[1, first:size, :] = z[:, 0:128] + z[:, 128:256]
            z_ref[2, first:size, :] = z[:, 256:384] + z[:, 384:512]

        for orient in (1, 2):
            @pl.when(need[level][orient])
            def _():
                finish(level, orient)

        @pl.when(need[level][0])
        def _():
            for n, start in enumerate(starts[level]):
                for at, value in x_pass(level, BOTH, n, start):
                    at += n * per
                    z_ref[0, at:at + 16, :] = value
            finish(level, 0)


def second_order(need, slots, info_s, taps_ref, w_second, m_ref, out_ref, lhs_second, z2_even, z2_odd, line_ref, done_ref, sems):
    left = lanes((16, 128)) < 64
    for level in range(2):
        for orient in range(3):
            @pl.when(need[level][orient])
            def _():
                source = level * 3 + orient
                for i in range(0, KEPT, 2):
                    value = jnp.concatenate([m_ref[source, i + SHIFT], m_ref[source, i + 1 + SHIFT]], axis=0)
                    high = value.astype(BF16)
                    wide = high.astype(F32)
                    pair = jnp.where(left, wide, value - wide).astype(BF16)
                    lhs_second[source, i * 8:i * 8 + 16, 0:128] = pair
                    lhs_second[source, i * 8:i * 8 + 16, 128:256] = high

    def z_pass(p, place):
        kind = 2 * (info_s[p] == 2).astype(jnp.int32) + (info_s[2 * slots + p] == 2).astype(jnp.int32)
        place[...] = dot(lhs_second[info_s[slots + p]], w_second[kind]).reshape(KEPT, 8, 128)

    def copy(p):
        return pltpu.make_async_copy(done_ref.at[p], out_ref.at[p], sems.at[p])

    def one_pair(p, here, there):
        mode, orient = info_s[p], info_s[2 * slots + p]
        following = jnp.minimum(p + 1, slots - 1)

        def work(dilation):
            z_pass(following, there)
            x_taps = taps_ref.at[jnp.where(orient == 0, BOTH, LOW)]
            y_taps = taps_ref.at[jnp.where(orient == 1, BOTH, LOW)]
            place = done_ref.at[p].reshape(done_ref.shape[1] * 8, 64)
            for c in range(0, 32, 16):
                taps = [x_taps[t] for t in range(TAPS)]
                sums = [None] * 16
                first = c + 14 - HALF * dilation
                for r in range(15 + 14 * dilation + 1):
                    value = here[first + r]
                    for i in range(16):
                        if (r - i) % dilation == 0 and 0 <= (r - i) // dilation < TAPS:
                            term = taps[(r - i) // dilation] * value
                            sums[i] = term if sums[i] is None else sums[i] + term
                for i in range(16):
                    line_ref[(c + i) * 8:(c + i) * 8 + 8, :] = sums[i]
            for c in range(4):
                lines = [line_ref[pl.ds(c * 64 + y, 8, stride=8), :] for y in range(8)]
                for j in range(8):
                    terms = [((y - j) // dilation + HALF, y) for y in range(8) if (y - j) % dilation == 0]
                    out = modulus(weigh(y_taps, lines, terms))
                    place[pl.ds(c * 64 + j, 8, stride=8), :] = out[:, 0:64]

        for dilation in (1, 2):
            @pl.when(mode == dilation)
            def _():
                work(dilation)

        @pl.when(mode == 3)
        def _():
            z_pass(following, there)
            done_ref[p] = done_ref[info_s[3 * slots + p]]

        @pl.when(mode == 0)
        def _():
            done_ref[p] = jnp.zeros(done_ref.shape[1:], F32)

        copy(p).start()

    def two_pairs(k, carry):
        one_pair(2 * k, z2_even, z2_odd)
        one_pair(2 * k + 1, z2_odd, z2_even)
        return carry

    z_pass(0, z2_even)
    lax.fori_loop(0, slots // 2, two_pairs, 0)
    for p in range(slots):
        copy(p).wait()


def pack_body(own_ref, sent_ref, rows_ref, sems):
    upper = lax.axis_index("wave") % 2
    tile_rows = own_ref.shape[0]
    copies = [pltpu.make_async_copy(own_ref.at[pl.ds(upper * (tile_rows - NEAR), NEAR)], sent_ref.at[0:NEAR], sems.at[0])]
    for k in range(BEYOND):
        row = jnp.where(upper == 1, tile_rows - NEAR - 1 - 2 * k, NEAR + 1 + 2 * k)
        copies.append(pltpu.make_async_copy(own_ref.at[pl.ds(row, 1)], rows_ref.at[k:k + 1], sems.at[1 + k]))
    for copy in copies:
        copy.start()
    for copy in copies[1:]:
        copy.wait()
    for k in range(BEYOND):
        sent_ref[NEAR + k // 2, 8 * (k % 2):8 * (k % 2) + 8, :] = rows_ref[k, pl.ds(0, 8, stride=2), :]
    copies[0].wait()


def inner_body(
    even_ref, odd_ref, low_ref, wave_ref, pairs_ref, own_ref,
    taps_ref, w_first, w_second, grid_ref, low_zero, low_one, m_ref, info_s,
    even_s, odd_s, low_s, wave_s, pairs_s, low_lhs, z_ref, sems, *, slots,
):
    tile_rows = own_ref.shape[0]
    moves = (
        (even_ref, even_s), (odd_ref, odd_s), (low_ref, low_s), (wave_ref, wave_s), (pairs_ref, pairs_s),
        (own_ref, grid_ref.at[pl.ds(FRONT + HALO, tile_rows)]),
    )
    copies = [pltpu.make_async_copy(source, place, sems.at[n]) for n, (source, place) in enumerate(moves)]
    for copy in copies:
        copy.start()
    for copy in copies[:-1]:
        copy.wait()
    make_filters(even_s, odd_s, low_s, taps_ref, w_first, w_second)
    read_tables(wave_s, pairs_s, lax.axis_index("wave") * slots, slots, info_s)
    copies[-1].wait()
    need = needed(info_s, slots)
    low_refs = (low_zero, low_one)
    filter_rows(need, [(FRONT + HALO, tile_rows)] * 2, w_first, grid_ref, low_refs, low_lhs)
    first_rows(need, INNER, (0, 0), tile_rows, taps_ref, w_first, grid_ref, low_refs, m_ref, low_lhs, z_ref)


def add_side(side, info_s, halo_ref, taps_ref, w_first, grid_ref, low_refs, m_ref, low_lhs, z_ref, slots, tile_rows):
    far = FRONT + HALO + tile_rows
    near = jnp.where(side == 1, FRONT + HALO - NEAR, far)
    for r in range(NEAR):
        grid_ref[near + r] = halo_ref[r]
    for k in range(BEYOND):
        row = jnp.where(side == 1, FRONT + HALO - NEAR - 1 - 2 * k, far + NEAR + 1 + 2 * k)
        grid_ref[row, pl.ds(0, 8, stride=2), :] = halo_ref[NEAR + k // 2, 8 * (k % 2):8 * (k % 2) + 8, :]
    need = needed(info_s, slots)
    spans = [(near, NEAR), (jnp.where(side == 1, FRONT, far), HALO)]
    filter_rows(need, spans, w_first, grid_ref, low_refs, low_lhs)
    starts = [[jnp.where(side == 1, x, y) for x, y in zip(*both)] for both in zip(BEFORE, AFTER)]
    first_rows(need, starts, EDGE, tile_rows, taps_ref, w_first, grid_ref, low_refs, m_ref, low_lhs, z_ref)
    return need


def side_body(
    info_s, got_ref, taps_ref, w_first, grid_in, zero_in, one_in, m_in,
    grid_ref, low_zero, low_one, m_ref, low_lhs, z_ref, *, slots, tile_rows,
):
    side = lax.axis_index("wave") % 2
    add_side(side, info_s, got_ref, taps_ref, w_first, grid_ref, (low_zero, low_one), m_ref, low_lhs, z_ref, slots, tile_rows)


def last_body(
    info_s, other_ref, taps_ref, w_first, grid_in, zero_in, one_in, m_in, w_second,
    out_ref, grid_ref, low_zero, low_one, m_ref, low_lhs, z_ref, lhs_second, z2_even, z2_odd, line_ref, done_ref, sems,
    *, slots, tile_rows,
):
    side = 1 - lax.axis_index("wave") % 2
    need = add_side(side, info_s, other_ref, taps_ref, w_first, grid_ref, (low_zero, low_one), m_ref, low_lhs, z_ref, slots, tile_rows)
    second_order(need, slots, info_s, taps_ref, w_second, m_ref, out_ref, lhs_second, z2_even, z2_odd, line_ref, done_ref, sems)


def shards(density, even_taps, odd_taps, low_taps, wavelets, pairs):
    tile_rows, ny, nz = density.shape
    count, waves = lax.axis_size("space"), lax.axis_size("wave")
    slots = pairs.shape[0] // waves
    step = (-1, 1)
    moves = [
        (z * waves + w, (z + step[w % 2]) * waves + w)
        for z in range(count)
        for w in range(waves)
        if 0 <= z + step[w % 2] < count
    ]
    smem = pl.BlockSpec(memory_space=pltpu.SMEM)
    vmem = pl.BlockSpec(memory_space=pltpu.VMEM)
    anywhere = pl.BlockSpec(memory_space=pl.ANY)
    params = pltpu.CompilerParams(vmem_limit_bytes=24 * 1024 * 1024)

    def held(value):
        return pltpu.with_memory_space_constraint(value, pltpu.VMEM)

    def far(value):
        return pltpu.with_memory_space_constraint(value, pltpu.HBM)

    def cost(us):
        return pl.CostEstimate(flops=us * 1000000000, bytes_accessed=us * 2500000, transcendentals=0)

    density = far(density)
    sent = pl.pallas_call(
        pack_body,
        out_shape=pltpu.VMEM((SENT, ny, nz), F32),
        in_specs=[anywhere],
        out_specs=vmem,
        scratch_shapes=[pltpu.VMEM((BEYOND, ny, nz), F32), pltpu.SemaphoreType.DMA((1 + BEYOND,))],
        compiler_params=params,
        name="pack_halo",
    )(density)
    got = lax.ppermute(sent, ("space", "wave"), moves)
    state_types = [
        pltpu.VMEM((WINDOW, ny, nz), F32),
        pltpu.VMEM((WINDOW, ny, nz), F32),
        pltpu.VMEM((WINDOW // 2, ny // 2, nz), F32),
        pltpu.VMEM((6, STORED, 8, 128), F32),
    ]
    out_shape = (slots, tile_rows // 2, ny // 2, nz // 2)
    scratch = [pltpu.VMEM((1024, 256), BF16), pltpu.VMEM((3, 384, 128), F32)]
    taps, w_first, w_second, *state, info = pl.pallas_call(
        functools.partial(inner_body, slots=slots),
        out_shape=[
            pltpu.VMEM((4, 16, 8, 128), F32),
            pltpu.VMEM((2, 256, 512), BF16),
            pltpu.VMEM((4, 256, 128), BF16),
            *state_types,
            pltpu.SMEM((4 * slots + 8,), jnp.int32),
        ],
        in_specs=[anywhere] * 6,
        out_specs=[vmem] * 7 + [smem],
        scratch_shapes=[
            pltpu.SMEM((TAPS,), F32),
            pltpu.SMEM((TAPS,), F32),
            pltpu.SMEM((TAPS,), F32),
            pltpu.SMEM(wavelets.shape[::-1], jnp.int32),
            pltpu.SMEM(pairs.shape[::-1], jnp.int32),
            *scratch,
            pltpu.SemaphoreType.DMA((6,)),
        ],
        compiler_params=params,
        cost_estimate=cost(3),
        name="inner_rows",
    )(*map(far, (even_taps, odd_taps, low_taps, wavelets.T, pairs.T)), density)
    got, state[0] = lax.optimization_barrier((got, state[0]))
    other = lax.ppermute(got, "wave", [(w, w ^ 1) for w in range(waves)])
    taps, w_first, w_second = map(held, (taps, w_first, w_second))
    info = pltpu.with_memory_space_constraint(info, pltpu.SMEM)
    state = pl.pallas_call(
        functools.partial(side_body, slots=slots, tile_rows=tile_rows),
        out_shape=state_types,
        in_specs=[smem] + [vmem] * 7,
        out_specs=[vmem] * 4,
        input_output_aliases={4: 0, 5: 1, 6: 2, 7: 3},
        scratch_shapes=scratch,
        compiler_params=params,
        cost_estimate=cost(2),
        name="side_rows",
    )(info, held(got), taps, w_first, *map(held, state))
    second, *_ = pl.pallas_call(
        functools.partial(last_body, slots=slots, tile_rows=tile_rows),
        out_shape=[jax.ShapeDtypeStruct(out_shape, F32), *state_types],
        in_specs=[smem] + [vmem] * 8,
        out_specs=[anywhere] + [vmem] * 4,
        input_output_aliases={4: 1, 5: 2, 6: 3, 7: 4},
        scratch_shapes=scratch + [
            pltpu.VMEM((6, KEPT * 8, 256), BF16),
            pltpu.VMEM((KEPT, 8, 128), F32),
            pltpu.VMEM((KEPT, 8, 128), F32),
            pltpu.VMEM((256, 128), F32),
            pltpu.VMEM(out_shape, F32),
            pltpu.SemaphoreType.DMA((slots,)),
        ],
        compiler_params=params,
        cost_estimate=cost(5),
        name="side_rows_and_pairs",
    )(info, held(other), taps, w_first, *map(held, state), w_second)
    return second


def solution(mesh):
    placed = (P(("groups", "space"), None, None), P(), P(), P(), P(), P())
    return jax.shard_map(
        shards,
        mesh=mesh,
        in_specs=placed,
        out_specs=P("wave", ("groups", "space"), None, None),
        check_vma=False,
    )
```

```python
import functools

import jax
import jax.numpy as jnp
from jax import lax
from jax.experimental import pallas as pl
from jax.experimental.pallas import tpu as pltpu
from jax.sharding import PartitionSpec as P

TAPS = 15
HALF = 7
HALO = 42
NEAR = 35
BEYOND = 4
SENT = NEAR + BEYOND // 2
PIECE = 5
FRONT = 8
WINDOW = 160
KEPT = 60
STORED = 72
SHIFT = 6
INNER = ((18, 26, 34), (21, 29))
BEFORE = ((-6, 2, 10), (-3, 5, 13))
AFTER = ((52, 42, 50), (36, 44, 52))
KNOWN = ((18, 42), (21, 37))
OUTER = (((0, 18), (42, 60)), ((0, 22), (36, 60)))
EDGE = (6, 0)
EPS = 1e-6
F32 = jnp.float32
BF16 = jnp.bfloat16
LOW, EVEN, ODD, BOTH = 0, 1, 2, 3
TILE = (8, 128)


def split(value):
    high = value.astype(BF16)
    return high, (value - high.astype(F32)).astype(BF16)


def dot(a, b):
    return jnp.dot(a, b, preferred_element_type=F32)


def rows(shape):
    return lax.broadcasted_iota(jnp.int32, shape, 0)


def lanes(shape):
    return lax.broadcasted_iota(jnp.int32, shape, 1)


def modulus(value):
    squares = value * value
    total = squares + pltpu.roll(squares, 64, 1) + EPS
    return total * lax.rsqrt(total)


def weigh(taps, values, pairs):
    acc = None
    for t, v in pairs:
        term = taps[t] * values[v]
        acc = term if acc is None else acc + term
    return acc


def banded(taps_ref, offset, dilation):
    low = both = jnp.zeros(offset.shape, F32)
    for t in range(TAPS):
        here = offset == (t - HALF) * dilation
        low = jnp.where(here, taps_ref[LOW, t][0:1], low)
        both = jnp.where(here, taps_ref[BOTH, t][0:1], both)
    return low, both


def make_filters(even_s, odd_s, low_s, taps_ref, w_first, w_second):
    left = lanes(TILE) < 64
    for t in range(TAPS):
        even = jnp.full(TILE, even_s[t], F32)
        odd = jnp.full(TILE, odd_s[t], F32)
        taps_ref[LOW, t] = jnp.full(TILE, low_s[t], F32)
        taps_ref[EVEN, t] = even
        taps_ref[ODD, t] = odd
        taps_ref[BOTH, t] = jnp.where(left, even, odd)
    wide = (128, 128)
    none = jnp.zeros(wide, BF16)
    for level in range(2):
        low, both = banded(taps_ref, rows(wide) - 2 * (lanes(wide) % 64), 1 << level)
        for kind, matrix in enumerate((low, both)):
            high, rest = split(matrix)
            column = 256 * kind
            w_first[level, 0:128, column:column + 128] = high
            w_first[level, 128:256, column:column + 128] = high
            w_first[level, 0:128, column + 128:column + 256] = rest
            w_first[level, 128:256, column + 128:column + 256] = none
        half = (64, 128)
        low, both = banded(taps_ref, rows(half) - lanes(half) % 64, 1 << level)
        for kind, matrix in enumerate((low, both)):
            high, rest = split(matrix)
            w_second[2 * level + kind, 0:64] = high
            w_second[2 * level + kind, 64:128] = high
            w_second[2 * level + kind, 128:192] = rest
            w_second[2 * level + kind, 192:256] = jnp.zeros(half, BF16)


def read_tables(wave_s, pairs_s, base, slots, info_s):
    found = []
    need = [False] * 6
    for p in range(slots):
        field, wavelet = pairs_s[0, base + p], pairs_s[1, base + p]
        safe = jnp.maximum(field, 0)
        live = field >= 0
        source = wave_s[0, safe] * 3 + wave_s[1, safe]
        level, orient = wave_s[0, wavelet], wave_s[1, wavelet]
        key = jnp.where(live, (source * 4 + level) * 4 + orient, -1)
        twin = jnp.int32(-1)
        for q in range(p - 1, -1, -1):
            twin = jnp.where(found[q] == key, q, twin)
        found.append(key)
        info_s[p] = jnp.where(live, jnp.where(twin >= 0, 3, level), 0)
        info_s[slots + p] = source
        info_s[2 * slots + p] = orient
        info_s[3 * slots + p] = jnp.maximum(twin, 0)
        for k in range(6):
            need[k] = need[k] | (live & (source == k))
    for k in range(6):
        info_s[4 * slots + k] = need[k].astype(jnp.int32)


def needed(info_s, slots):
    return [[info_s[4 * slots + level * 3 + orient] > 0 for orient in range(3)] for level in range(2)]


def filter_rows(need, spans, w_first, grid_ref, low_refs, low_lhs):
    @pl.when(need[0][0])
    def _():
        place, count = spans[0]
        for r in range(count):
            high, rest = split(grid_ref[place + r])
            low_lhs[r * 16:r * 16 + 16, 0:128] = high
            low_lhs[r * 16:r * 16 + 16, 128:256] = rest
        z = dot(low_lhs[0:count * 16, :], w_first[0, :, 0:256])
        low_refs[0][pl.ds(place, count)] = (z[:, 0:128] + z[:, 128:256]).reshape(count, 16, 128)

    @pl.when(need[1][0])
    def _():
        place, count = spans[1]
        pairs = (count + 3) // 4
        for r in range(pairs):
            even = [grid_ref[place + 4 * r + n, pl.ds(0, 8, stride=2), :] for n in (0, 2)]
            high, rest = split(jnp.concatenate(even, axis=0))
            low_lhs[r * 16:r * 16 + 16, 0:128] = high
            low_lhs[r * 16:r * 16 + 16, 128:256] = rest
        z = dot(low_lhs[0:pairs * 16, :], w_first[1, :, 0:256])
        low_refs[1][pl.ds(place // 2, 2 * pairs)] = (z[:, 0:128] + z[:, 128:256]).reshape(2 * pairs, 8, 128)


def first_rows(need, starts, edge, tile_rows, taps_ref, w_first, grid_ref, low_refs, m_ref, low_lhs, z_ref):
    rank = lax.axis_index("space")
    total = lax.axis_size("space") * tile_rows

    def x_pass(level, kind, n, start):
        taps = [taps_ref[kind, t] for t in range(TAPS)]
        skip = edge[level] if n == 0 else 0
        stride = 2 - level
        parts = []
        for h in range(2 - level):
            sums = [None] * 8
            for r in range(stride * skip, stride * 7 + TAPS):
                if level == 0:
                    ref = low_refs[0] if kind == BOTH else grid_ref
                    value = ref[2 * start + HALF + FRONT + r, 8 * h:8 * h + 8, :]
                elif kind == BOTH:
                    value = low_refs[1][start + r + FRONT // 2]
                else:
                    value = grid_ref[2 * (start + r) + FRONT, pl.ds(0, 8, stride=2), :]
                for i in range(skip, 8):
                    t = r - stride * i
                    if 0 <= t < TAPS:
                        term = taps[t] * value
                        sums[i] = term if sums[i] is None else sums[i] + term
            parts.append(sums)
        if level == 0:
            return [(i * 16, jnp.concatenate([parts[0][i], parts[1][i]], axis=0)) for i in range(skip, 8)]
        return [(i * 8, jnp.concatenate([parts[0][i], parts[0][i + 1]], axis=0)) for i in range(skip, 8, 2)]

    def finish(level, orient):
        height = 16 >> level
        taps = taps_ref.at[BOTH if orient == 1 else LOW]
        place = m_ref.at[level * 3 + orient].reshape(STORED * 8, 128)
        for n, start in enumerate(starts[level]):
            values = [z_ref[orient, pl.ds(n * 8 * height + y, 8, stride=height), :] for y in range(height)]
            i = start + rows(TILE)
            x = rank * tile_rows - 28 + 2 * i
            inside = (x >= 0) & (x < total) & (i >= 0) & (i < KEPT)
            for j in range(8):
                terms = [(y - (2 - level) * j + HALF, y) for y in range(height)]
                out = modulus(weigh(taps, values, [(t, y) for t, y in terms if 0 <= t < TAPS]))
                place[pl.ds((start + SHIFT) * 8 + j, 8, stride=8), :] = jnp.where(inside, out, 0.0)

    for level in range(2):
        per = 128 >> level
        first, size = edge[level] * (16 >> level), per * len(starts[level])

        @pl.when(need[level][1] | need[level][2])
        def _():
            for n, start in enumerate(starts[level]):
                for at, value in x_pass(level, LOW, n, start):
                    high, rest = split(value)
                    at += n * per
                    low_lhs[at:at + 16, 0:128] = high
                    low_lhs[at:at + 16, 128:256] = rest
            z = dot(low_lhs[first:size, :], w_first[level])
            z_ref[1, first:size, :] = z[:, 0:128] + z[:, 128:256]
            z_ref[2, first:size, :] = z[:, 256:384] + z[:, 384:512]

        for orient in (1, 2):
            @pl.when(need[level][orient])
            def _():
                finish(level, orient)

        @pl.when(need[level][0])
        def _():
            for n, start in enumerate(starts[level]):
                for at, value in x_pass(level, BOTH, n, start):
                    at += n * per
                    z_ref[0, at:at + 16, :] = value
            finish(level, 0)


def pack_rows(need, blocks, m_ref, lhs_ref):
    left = lanes((16, 128)) < 64
    for level in range(2):
        for orient in range(3):
            @pl.when(need[level][orient])
            def _():
                source = level * 3 + orient
                at = 0
                for first, end in blocks[level]:
                    for i in range(first, end, 2):
                        value = jnp.concatenate([m_ref[source, i + SHIFT], m_ref[source, i + 1 + SHIFT]], axis=0)
                        high = value.astype(BF16)
                        wide = high.astype(F32)
                        lhs_ref[source, at:at + 16, 0:128] = jnp.where(left, wide, value - wide).astype(BF16)
                        lhs_ref[source, at:at + 16, 128:256] = high
                        at += 16


def every_pair(slots, info_s, w_second, lhs_ref, z_even, z_odd, live, other):
    def z_pass(p, place):
        kind = 2 * (info_s[p] == 2).astype(jnp.int32) + (info_s[2 * slots + p] == 2).astype(jnp.int32)
        place[...] = dot(lhs_ref[info_s[slots + p]], w_second[kind]).reshape(place.shape)

    def one_pair(p, here, there):
        mode, source = info_s[p], info_s[slots + p]
        following = jnp.minimum(p + 1, slots - 1)
        for dilation, level in ((1, 0), (2, 0), (2, 1)):
            @pl.when((mode == dilation) & ((source >= 3) == (level == 1)))
            def _():
                z_pass(following, there)
                live(p, here, dilation, level)

        @pl.when(mode == 3)
        def _():
            z_pass(following, there)

        other(p, mode)

    def two_pairs(k, carry):
        one_pair(2 * k, z_even, z_odd)
        one_pair(2 * k + 1, z_odd, z_even)
        return carry

    z_pass(0, z_even)
    lax.fori_loop(0, slots // 2, two_pairs, 0)


def x_sums(taps, first, dilation, sums, have, read):
    for r in range(first, first + 16 + 14 * dilation):
        if have(r):
            value = read(r)
            for i in range(16):
                if (r - first - i) % dilation == 0 and 0 <= (r - first - i) // dilation < TAPS:
                    term = taps[(r - first - i) // dilation] * value
                    sums[i] = term if sums[i] is None else sums[i] + term
    return sums


def inner_sums(need, slots, info_s, taps_ref, w_second, m_ref, part_ref, lhs_ref, z_even, z_odd):
    pack_rows(need, [[(low, high)] for low, high in KNOWN], m_ref, lhs_ref)

    def live(p, here, dilation, level):
        taps_at = taps_ref.at[jnp.where(info_s[2 * slots + p] == 0, BOTH, LOW)]
        taps = [taps_at[t] for t in range(TAPS)]
        low, high = KNOWN[level]
        for c in range(0, 32, 16):
            sums = x_sums(taps, c + 14 - HALF * dilation, dilation, [None] * 16, lambda r: low <= r < high, lambda r: here[r - low])
            for i in range(16):
                part_ref[p, c + i] = sums[i]

    every_pair(slots, info_s, w_second, lhs_ref, z_even, z_odd, live, lambda p, mode: None)


def second_order(need, slots, info_s, taps_ref, w_second, m_ref, part_ref, out_ref, lhs_ref, z_even, z_odd, line_ref, done_ref, sems):
    pack_rows(need, OUTER, m_ref, lhs_ref)
    half = done_ref.shape[1] // 2

    def copy(p, h):
        rows_at = pl.ds(h * half, half)
        return pltpu.make_async_copy(done_ref.at[p, rows_at], out_ref.at[p, rows_at], sems.at[p, h])

    def live(p, here, dilation, level):
        orient = info_s[2 * slots + p]
        x_taps = taps_ref.at[jnp.where(orient == 0, BOTH, LOW)]
        y_taps = taps_ref.at[jnp.where(orient == 1, BOTH, LOW)]
        place = done_ref.at[p].reshape(done_ref.shape[1] * 8, 64)
        low, high = KNOWN[level]
        (_, split_at), (rest, _) = OUTER[level]
        taps = [x_taps[t] for t in range(TAPS)]
        for c in range(0, 32, 16):
            sums = x_sums(
                taps, c + 14 - HALF * dilation, dilation, [part_ref[p, c + i] for i in range(16)],
                lambda r: not low <= r < high, lambda r: here[r if r < low else r - rest + split_at],
            )
            for i in range(16):
                line_ref[(c + i) * 8:(c + i) * 8 + 8, :] = sums[i]
            for c in (c // 8, c // 8 + 1):
                lines = [line_ref[pl.ds(c * 64 + y, 8, stride=8), :] for y in range(8)]
                for j in range(8):
                    terms = [((y - j) // dilation + HALF, y) for y in range(8) if (y - j) % dilation == 0]
                    out = modulus(weigh(y_taps, lines, terms))
                    place[pl.ds(c * 64 + j, 8, stride=8), :] = out[:, 0:64]
            copy(p, c // 2).start()

    def other(p, mode):
        @pl.when((mode == 0) | (mode == 3))
        def _():
            @pl.when(mode == 3)
            def _():
                done_ref[p] = done_ref[info_s[3 * slots + p]]

            @pl.when(mode == 0)
            def _():
                done_ref[p] = jnp.zeros(done_ref.shape[1:], F32)

            for h in range(2):
                copy(p, h).start()

    every_pair(slots, info_s, w_second, lhs_ref, z_even, z_odd, live, other)
    for p in range(slots):
        for h in range(2):
            copy(p, h).wait()


def pack_body(own_ref, sent_ref, rows_ref, sems):
    upper = lax.axis_index("wave") % 2
    tile_rows = own_ref.shape[0]
    copies = []
    for n in range(0, NEAR, PIECE):
        source = own_ref.at[pl.ds(upper * (tile_rows - NEAR) + n, PIECE)]
        copies.append(pltpu.make_async_copy(source, sent_ref.at[n:n + PIECE], sems.at[BEYOND + n // PIECE]))
    for k in range(BEYOND):
        row = jnp.where(upper == 1, tile_rows - NEAR - 1 - 2 * k, NEAR + 1 + 2 * k)
        copies.append(pltpu.make_async_copy(own_ref.at[pl.ds(row, 1)], rows_ref.at[k:k + 1], sems.at[k]))
    for copy in copies:
        copy.start()
    for copy in copies[-BEYOND:]:
        copy.wait()
    for k in range(BEYOND):
        sent_ref[NEAR + k // 2, 8 * (k % 2):8 * (k % 2) + 8, :] = rows_ref[k, pl.ds(0, 8, stride=2), :]
    for copy in copies[:-BEYOND]:
        copy.wait()


def inner_body(
    even_ref, odd_ref, low_ref, wave_ref, pairs_ref, own_ref,
    taps_ref, w_first, w_second, grid_ref, low_zero, low_one, m_ref, part_ref, info_s,
    even_s, odd_s, low_s, wave_s, pairs_s, low_lhs, z_ref, lhs_second, z2_even, z2_odd, sems, *, slots,
):
    tile_rows = own_ref.shape[0]
    moves = (
        (even_ref, even_s), (odd_ref, odd_s), (low_ref, low_s), (wave_ref, wave_s), (pairs_ref, pairs_s),
        (own_ref, grid_ref.at[pl.ds(FRONT + HALO, tile_rows)]),
    )
    copies = [pltpu.make_async_copy(source, place, sems.at[n]) for n, (source, place) in enumerate(moves)]
    for copy in copies:
        copy.start()
    for copy in copies[:-1]:
        copy.wait()
    make_filters(even_s, odd_s, low_s, taps_ref, w_first, w_second)
    read_tables(wave_s, pairs_s, lax.axis_index("wave") * slots, slots, info_s)
    copies[-1].wait()
    need = needed(info_s, slots)
    low_refs = (low_zero, low_one)
    filter_rows(need, [(FRONT + HALO, tile_rows)] * 2, w_first, grid_ref, low_refs, low_lhs)
    first_rows(need, INNER, (0, 0), tile_rows, taps_ref, w_first, grid_ref, low_refs, m_ref, low_lhs, z_ref)
    inner_sums(need, slots, info_s, taps_ref, w_second, m_ref, part_ref, lhs_second, z2_even, z2_odd)


def add_side(side, info_s, halo_ref, taps_ref, w_first, grid_ref, low_refs, m_ref, low_lhs, z_ref, slots, tile_rows):
    far = FRONT + HALO + tile_rows
    near = jnp.where(side == 1, FRONT + HALO - NEAR, far)
    for r in range(NEAR):
        grid_ref[near + r] = halo_ref[r]
    for k in range(BEYOND):
        row = jnp.where(side == 1, FRONT + HALO - NEAR - 1 - 2 * k, far + NEAR + 1 + 2 * k)
        grid_ref[row, pl.ds(0, 8, stride=2), :] = halo_ref[NEAR + k // 2, 8 * (k % 2):8 * (k % 2) + 8, :]
    need = needed(info_s, slots)
    spans = [(near, NEAR), (jnp.where(side == 1, FRONT, far), HALO)]
    filter_rows(need, spans, w_first, grid_ref, low_refs, low_lhs)
    starts = [[jnp.where(side == 1, x, y) for x, y in zip(*both)] for both in zip(BEFORE, AFTER)]
    first_rows(need, starts, EDGE, tile_rows, taps_ref, w_first, grid_ref, low_refs, m_ref, low_lhs, z_ref)
    return need


def side_body(
    info_s, got_ref, taps_ref, w_first, grid_in, zero_in, one_in, m_in,
    grid_ref, low_zero, low_one, m_ref, low_lhs, z_ref, *, slots, tile_rows,
):
    side = lax.axis_index("wave") % 2
    add_side(side, info_s, got_ref, taps_ref, w_first, grid_ref, (low_zero, low_one), m_ref, low_lhs, z_ref, slots, tile_rows)


def last_body(
    info_s, other_ref, taps_ref, w_first, grid_in, zero_in, one_in, m_in, w_second, part_ref,
    out_ref, grid_ref, low_zero, low_one, m_ref, low_lhs, z_ref, lhs_second, z2_even, z2_odd, line_ref, done_ref, sems,
    *, slots, tile_rows,
):
    side = 1 - lax.axis_index("wave") % 2
    need = add_side(side, info_s, other_ref, taps_ref, w_first, grid_ref, (low_zero, low_one), m_ref, low_lhs, z_ref, slots, tile_rows)
    second_order(need, slots, info_s, taps_ref, w_second, m_ref, part_ref, out_ref, lhs_second, z2_even, z2_odd, line_ref, done_ref, sems)


def shards(density, even_taps, odd_taps, low_taps, wavelets, pairs):
    tile_rows, ny, nz = density.shape
    count, waves = lax.axis_size("space"), lax.axis_size("wave")
    slots = pairs.shape[0] // waves
    step = (-1, 1)
    moves = [
        (z * waves + w, (z + step[w % 2]) * waves + w)
        for z in range(count)
        for w in range(waves)
        if 0 <= z + step[w % 2] < count
    ]
    smem = pl.BlockSpec(memory_space=pltpu.SMEM)
    vmem = pl.BlockSpec(memory_space=pltpu.VMEM)
    anywhere = pl.BlockSpec(memory_space=pl.ANY)
    params = pltpu.CompilerParams(vmem_limit_bytes=24 * 1024 * 1024)

    def held(value):
        return pltpu.with_memory_space_constraint(value, pltpu.VMEM)

    def far(value):
        return pltpu.with_memory_space_constraint(value, pltpu.HBM)

    def cost(us):
        return pl.CostEstimate(flops=us * 1000000000, bytes_accessed=us * 2500000, transcendentals=0)

    density = far(density)
    sent = pl.pallas_call(
        pack_body,
        out_shape=pltpu.VMEM((SENT, ny, nz), F32),
        in_specs=[anywhere],
        out_specs=vmem,
        scratch_shapes=[pltpu.VMEM((BEYOND, ny, nz), F32), pltpu.SemaphoreType.DMA((BEYOND + NEAR // PIECE,))],
        compiler_params=params,
        name="pack_halo",
    )(density)
    got = lax.ppermute(sent, ("space", "wave"), moves)
    state_types = [
        pltpu.VMEM((WINDOW, ny, nz), F32),
        pltpu.VMEM((WINDOW, ny, nz), F32),
        pltpu.VMEM((WINDOW // 2, ny // 2, nz), F32),
        pltpu.VMEM((6, STORED, 8, 128), F32),
    ]
    part_type = pltpu.VMEM((slots, tile_rows // 2, 8, 128), F32)
    out_shape = (slots, tile_rows // 2, ny // 2, nz // 2)
    scratch = [pltpu.VMEM((1024, 256), BF16), pltpu.VMEM((3, 384, 128), F32)]
    taps, w_first, w_second, *state, part, info = pl.pallas_call(
        functools.partial(inner_body, slots=slots),
        out_shape=[
            pltpu.VMEM((4, 16, 8, 128), F32),
            pltpu.VMEM((2, 256, 512), BF16),
            pltpu.VMEM((4, 256, 128), BF16),
            *state_types,
            part_type,
            pltpu.SMEM((4 * slots + 8,), jnp.int32),
        ],
        in_specs=[anywhere] * 6,
        out_specs=[vmem] * 8 + [smem],
        scratch_shapes=[
            pltpu.SMEM((TAPS,), F32),
            pltpu.SMEM((TAPS,), F32),
            pltpu.SMEM((TAPS,), F32),
            pltpu.SMEM(wavelets.shape[::-1], jnp.int32),
            pltpu.SMEM(pairs.shape[::-1], jnp.int32),
            *scratch,
            pltpu.VMEM((6, 24 * 8, 256), BF16),
            pltpu.VMEM((24, 8, 128), F32),
            pltpu.VMEM((24, 8, 128), F32),
            pltpu.SemaphoreType.DMA((6,)),
        ],
        compiler_params=params,
        cost_estimate=cost(3),
        name="inner_rows",
    )(*map(far, (even_taps, odd_taps, low_taps, wavelets.T, pairs.T)), density)
    got, state[0] = lax.optimization_barrier((got, state[0]))
    other = lax.ppermute(got, "wave", [(w, w ^ 1) for w in range(waves)])
    taps, w_first, w_second = map(held, (taps, w_first, w_second))
    info = pltpu.with_memory_space_constraint(info, pltpu.SMEM)
    state = pl.pallas_call(
        functools.partial(side_body, slots=slots, tile_rows=tile_rows),
        out_shape=state_types,
        in_specs=[smem] + [vmem] * 7,
        out_specs=[vmem] * 4,
        input_output_aliases={4: 0, 5: 1, 6: 2, 7: 3},
        scratch_shapes=scratch,
        compiler_params=params,
        cost_estimate=cost(2),
        name="side_rows",
    )(info, held(got), taps, w_first, *map(held, state))
    second, *_ = pl.pallas_call(
        functools.partial(last_body, slots=slots, tile_rows=tile_rows),
        out_shape=[jax.ShapeDtypeStruct(out_shape, F32), *state_types],
        in_specs=[smem] + [vmem] * 9,
        out_specs=[anywhere] + [vmem] * 4,
        input_output_aliases={4: 1, 5: 2, 6: 3, 7: 4},
        scratch_shapes=scratch + [
            pltpu.VMEM((6, 46 * 8, 256), BF16),
            pltpu.VMEM((46, 8, 128), F32),
            pltpu.VMEM((46, 8, 128), F32),
            pltpu.VMEM((256, 128), F32),
            pltpu.VMEM(out_shape, F32),
            pltpu.SemaphoreType.DMA((slots, 2)),
        ],
        compiler_params=params,
        cost_estimate=cost(5),
        name="side_rows_and_pairs",
    )(info, held(other), taps, w_first, *map(held, state), w_second, held(part))
    return second


def solution(mesh):
    placed = (P(("groups", "space"), None, None), P(), P(), P(), P(), P())
    return jax.shard_map(
        shards,
        mesh=mesh,
        in_specs=placed,
        out_specs=P("wave", ("groups", "space"), None, None),
        check_vma=False,
    )
```

```python
import functools

import jax
import jax.numpy as jnp
from jax import lax
from jax.experimental import pallas as pl
from jax.experimental.pallas import tpu as pltpu
from jax.sharding import PartitionSpec as P

TAPS = 15
HALF = 7
HALO = 42
NEAR = 35
BEYOND = 4
SENT = NEAR + BEYOND // 2
PIECE = 5
FRONT = 8
WINDOW = 160
KEPT = 60
STORED = 72
SHIFT = 6
INNER = ((18, 26, 34), (21, 29))
BEFORE = ((-6, 2, 10), (-3, 5, 13))
AFTER = ((52, 42, 50), (36, 44, 52))
KNOWN = ((18, 42), (21, 37))
OUTER = (((0, 18), (42, 60)), ((0, 22), (36, 60)))
EDGE = (6, 0)
EPS = 1e-6
F32 = jnp.float32
BF16 = jnp.bfloat16
LOW, EVEN, ODD, BOTH = 0, 1, 2, 3
TILE = (8, 128)


def split(value):
    high = value.astype(BF16)
    return high, (value - high.astype(F32)).astype(BF16)


def dot(a, b):
    return jnp.dot(a, b, preferred_element_type=F32)


def rows(shape):
    return lax.broadcasted_iota(jnp.int32, shape, 0)


def lanes(shape):
    return lax.broadcasted_iota(jnp.int32, shape, 1)


def modulus(value):
    squares = value * value
    total = squares + pltpu.roll(squares, 64, 1) + EPS
    return total * lax.rsqrt(total)


def flip(values):
    values = list(values)
    sub = rows(TILE)
    for s in (4, 2, 1):
        kept = (sub & s) == 0
        for k in range(8):
            if k & s == 0:
                a, b = values[k], values[k + s]
                values[k] = jnp.where(kept, a, pltpu.roll(b, s, 0))
                values[k + s] = jnp.where(kept, pltpu.roll(a, 8 - s, 0), b)
    return values


def weigh(taps, values, pairs):
    acc = None
    for t, v in pairs:
        term = taps[t] * values[v]
        acc = term if acc is None else acc + term
    return acc


def banded(taps_ref, offset, dilation):
    low = both = jnp.zeros(offset.shape, F32)
    for t in range(TAPS):
        here = offset == (t - HALF) * dilation
        low = jnp.where(here, taps_ref[LOW, t][0:1], low)
        both = jnp.where(here, taps_ref[BOTH, t][0:1], both)
    return low, both


def make_filters(even_s, odd_s, low_s, taps_ref, w_first, w_second):
    left = lanes(TILE) < 64
    for t in range(TAPS):
        even = jnp.full(TILE, even_s[t], F32)
        odd = jnp.full(TILE, odd_s[t], F32)
        taps_ref[LOW, t] = jnp.full(TILE, low_s[t], F32)
        taps_ref[EVEN, t] = even
        taps_ref[ODD, t] = odd
        taps_ref[BOTH, t] = jnp.where(left, even, odd)
    wide = (128, 128)
    none = jnp.zeros(wide, BF16)
    for level in range(2):
        low, both = banded(taps_ref, rows(wide) - 2 * (lanes(wide) % 64), 1 << level)
        for kind, matrix in enumerate((low, both)):
            high, rest = split(matrix)
            column = 256 * kind
            w_first[level, 0:128, column:column + 128] = high
            w_first[level, 128:256, column:column + 128] = high
            w_first[level, 0:128, column + 128:column + 256] = rest
            w_first[level, 128:256, column + 128:column + 256] = none
        half = (64, 128)
        low, both = banded(taps_ref, rows(half) - lanes(half) % 64, 1 << level)
        for kind, matrix in enumerate((low, both)):
            high, rest = split(matrix)
            w_second[2 * level + kind, 0:64] = high
            w_second[2 * level + kind, 64:128] = high
            w_second[2 * level + kind, 128:192] = rest
            w_second[2 * level + kind, 192:256] = jnp.zeros(half, BF16)


def read_tables(wave_s, pairs_s, base, slots, info_s):
    found = []
    need = [False] * 6
    for p in range(slots):
        field, wavelet = pairs_s[0, base + p], pairs_s[1, base + p]
        safe = jnp.maximum(field, 0)
        live = field >= 0
        source = wave_s[0, safe] * 3 + wave_s[1, safe]
        level, orient = wave_s[0, wavelet], wave_s[1, wavelet]
        key = jnp.where(live, (source * 4 + level) * 4 + orient, -1)
        twin = jnp.int32(-1)
        for q in range(p - 1, -1, -1):
            twin = jnp.where(found[q] == key, q, twin)
        found.append(key)
        info_s[p] = jnp.where(live, jnp.where(twin >= 0, 3, level), 0)
        info_s[slots + p] = source
        info_s[2 * slots + p] = orient
        info_s[3 * slots + p] = jnp.maximum(twin, 0)
        for k in range(6):
            need[k] = need[k] | (live & (source == k))
    for k in range(6):
        info_s[4 * slots + k] = need[k].astype(jnp.int32)


def needed(info_s, slots):
    return [[info_s[4 * slots + level * 3 + orient] > 0 for orient in range(3)] for level in range(2)]


def filter_rows(need, spans, w_first, grid_ref, low_refs, low_lhs):
    @pl.when(need[0][0])
    def _():
        place, count = spans[0]
        for r in range(count):
            high, rest = split(grid_ref[place + r])
            low_lhs[r * 16:r * 16 + 16, 0:128] = high
            low_lhs[r * 16:r * 16 + 16, 128:256] = rest
        z = dot(low_lhs[0:count * 16, :], w_first[0, :, 0:256])
        low_refs[0][pl.ds(place, count)] = (z[:, 0:128] + z[:, 128:256]).reshape(count, 16, 128)

    @pl.when(need[1][0])
    def _():
        place, count = spans[1]
        pairs = (count + 3) // 4
        for r in range(pairs):
            even = [grid_ref[place + 4 * r + n, pl.ds(0, 8, stride=2), :] for n in (0, 2)]
            high, rest = split(jnp.concatenate(even, axis=0))
            low_lhs[r * 16:r * 16 + 16, 0:128] = high
            low_lhs[r * 16:r * 16 + 16, 128:256] = rest
        z = dot(low_lhs[0:pairs * 16, :], w_first[1, :, 0:256])
        low_refs[1][pl.ds(place // 2, 2 * pairs)] = (z[:, 0:128] + z[:, 128:256]).reshape(2 * pairs, 8, 128)


def first_rows(need, starts, edge, tile_rows, taps_ref, w_first, grid_ref, low_refs, m_ref, low_lhs, z_ref):
    rank = lax.axis_index("space")
    total = lax.axis_size("space") * tile_rows

    def x_pass(level, kind, n, start):
        taps = [taps_ref[kind, t] for t in range(TAPS)]
        skip = edge[level] if n == 0 else 0
        stride = 2 - level
        parts = []
        for h in range(2 - level):
            sums = [None] * 8
            for r in range(stride * skip, stride * 7 + TAPS):
                if level == 0:
                    ref = low_refs[0] if kind == BOTH else grid_ref
                    value = ref[2 * start + HALF + FRONT + r, 8 * h:8 * h + 8, :]
                elif kind == BOTH:
                    value = low_refs[1][start + r + FRONT // 2]
                else:
                    value = grid_ref[2 * (start + r) + FRONT, pl.ds(0, 8, stride=2), :]
                for i in range(skip, 8):
                    t = r - stride * i
                    if 0 <= t < TAPS:
                        term = taps[t] * value
                        sums[i] = term if sums[i] is None else sums[i] + term
            parts.append(sums)
        if level == 0:
            return [(i * 16, jnp.concatenate([parts[0][i], parts[1][i]], axis=0)) for i in range(skip, 8)]
        return [(i * 8, jnp.concatenate([parts[0][i], parts[0][i + 1]], axis=0)) for i in range(skip, 8, 2)]

    def finish(level, orient):
        height = 16 >> level
        taps = taps_ref.at[BOTH if orient == 1 else LOW]
        for n, start in enumerate(starts[level]):
            values = []
            for y in range(0, height, 8):
                at = [n * 8 * height + k * height + y for k in range(8)]
                values += flip(z_ref[orient, r:r + 8, :] for r in at)
            outs = []
            i = start + rows(TILE)
            x = rank * tile_rows - 28 + 2 * i
            inside = (x >= 0) & (x < total) & (i >= 0) & (i < KEPT)
            for j in range(8):
                terms = [(y - (2 - level) * j + HALF, y) for y in range(height)]
                out = modulus(weigh(taps, values, [(t, y) for t, y in terms if 0 <= t < TAPS]))
                outs.append(jnp.where(inside, out, 0.0))
            for k, out in enumerate(flip(outs)):
                m_ref[level * 3 + orient, start + SHIFT + k] = out

    for level in range(2):
        per = 128 >> level
        first, size = edge[level] * (16 >> level), per * len(starts[level])

        @pl.when(need[level][1] | need[level][2])
        def _():
            for n, start in enumerate(starts[level]):
                for at, value in x_pass(level, LOW, n, start):
                    high, rest = split(value)
                    at += n * per
                    low_lhs[at:at + 16, 0:128] = high
                    low_lhs[at:at + 16, 128:256] = rest
            z = dot(low_lhs[first:size, :], w_first[level])
            z_ref[1, first:size, :] = z[:, 0:128] + z[:, 128:256]
            z_ref[2, first:size, :] = z[:, 256:384] + z[:, 384:512]

        for orient in (1, 2):
            @pl.when(need[level][orient])
            def _():
                finish(level, orient)

        @pl.when(need[level][0])
        def _():
            for n, start in enumerate(starts[level]):
                for at, value in x_pass(level, BOTH, n, start):
                    at += n * per
                    z_ref[0, at:at + 16, :] = value
            finish(level, 0)


def pack_rows(need, blocks, m_ref, lhs_ref):
    left = lanes((16, 128)) < 64
    for level in range(2):
        for orient in range(3):
            @pl.when(need[level][orient])
            def _():
                source = level * 3 + orient
                at = 0
                for first, end in blocks[level]:
                    for i in range(first, end, 2):
                        value = jnp.concatenate([m_ref[source, i + SHIFT], m_ref[source, i + 1 + SHIFT]], axis=0)
                        high = value.astype(BF16)
                        wide = high.astype(F32)
                        lhs_ref[source, at:at + 16, 0:128] = jnp.where(left, wide, value - wide).astype(BF16)
                        lhs_ref[source, at:at + 16, 128:256] = high
                        at += 16


def every_pair(slots, info_s, w_second, lhs_ref, z_even, z_odd, live, other):
    def z_pass(p, place):
        kind = 2 * (info_s[p] == 2).astype(jnp.int32) + (info_s[2 * slots + p] == 2).astype(jnp.int32)
        place[...] = dot(lhs_ref[info_s[slots + p]], w_second[kind]).reshape(place.shape)

    def one_pair(p, here, there):
        mode, source = info_s[p], info_s[slots + p]
        following = jnp.minimum(p + 1, slots - 1)
        for dilation, level in ((1, 0), (2, 0), (2, 1)):
            @pl.when((mode == dilation) & ((source >= 3) == (level == 1)))
            def _():
                z_pass(following, there)
                live(p, here, dilation, level)

        @pl.when(mode == 3)
        def _():
            z_pass(following, there)

        other(p, mode)

    def two_pairs(k, carry):
        one_pair(2 * k, z_even, z_odd)
        one_pair(2 * k + 1, z_odd, z_even)
        return carry

    z_pass(0, z_even)
    lax.fori_loop(0, slots // 2, two_pairs, 0)


def x_sums(taps, first, dilation, sums, have, read):
    for r in range(first, first + 16 + 14 * dilation):
        if have(r):
            value = read(r)
            for i in range(16):
                if (r - first - i) % dilation == 0 and 0 <= (r - first - i) // dilation < TAPS:
                    term = taps[(r - first - i) // dilation] * value
                    sums[i] = term if sums[i] is None else sums[i] + term
    return sums


def inner_sums(need, slots, info_s, taps_ref, w_second, m_ref, part_ref, lhs_ref, z_even, z_odd):
    pack_rows(need, [[(low, high)] for low, high in KNOWN], m_ref, lhs_ref)

    def live(p, here, dilation, level):
        taps_at = taps_ref.at[jnp.where(info_s[2 * slots + p] == 0, BOTH, LOW)]
        taps = [taps_at[t] for t in range(TAPS)]
        low, high = KNOWN[level]
        for c in range(0, 32, 16):
            sums = x_sums(taps, c + 14 - HALF * dilation, dilation, [None] * 16, lambda r: low <= r < high, lambda r: here[r - low])
            for i in range(16):
                part_ref[p, c + i] = sums[i]

    every_pair(slots, info_s, w_second, lhs_ref, z_even, z_odd, live, lambda p, mode: None)


def second_order(need, slots, info_s, taps_ref, w_second, m_ref, part_ref, out_ref, lhs_ref, z_even, z_odd, done_ref, sems):
    pack_rows(need, OUTER, m_ref, lhs_ref)
    half = done_ref.shape[1] // 2

    def copy(p, h):
        rows_at = pl.ds(h * half, half)
        return pltpu.make_async_copy(done_ref.at[p, rows_at], out_ref.at[p, rows_at], sems.at[p, h])

    def live(p, here, dilation, level):
        orient = info_s[2 * slots + p]
        x_taps = taps_ref.at[jnp.where(orient == 0, BOTH, LOW)]
        y_taps = taps_ref.at[jnp.where(orient == 1, BOTH, LOW)]
        low, high = KNOWN[level]
        (_, split_at), (rest, _) = OUTER[level]
        taps = [x_taps[t] for t in range(TAPS)]
        for c in range(0, 32, 16):
            sums = x_sums(
                taps, c + 14 - HALF * dilation, dilation, [part_ref[p, c + i] for i in range(16)],
                lambda r: not low <= r < high, lambda r: here[r if r < low else r - rest + split_at],
            )
            for n in (0, 8):
                lines = flip(sums[n:n + 8])
                outs = []
                for j in range(8):
                    terms = [((y - j) // dilation + HALF, y) for y in range(8) if (y - j) % dilation == 0]
                    outs.append(modulus(weigh(y_taps, lines, terms)))
                for k, out in enumerate(flip(outs)):
                    done_ref[p, c + n + k] = out[:, 0:64]
            copy(p, c // 16).start()

    def other(p, mode):
        @pl.when((mode == 0) | (mode == 3))
        def _():
            @pl.when(mode == 3)
            def _():
                done_ref[p] = done_ref[info_s[3 * slots + p]]

            @pl.when(mode == 0)
            def _():
                done_ref[p] = jnp.zeros(done_ref.shape[1:], F32)

            for h in range(2):
                copy(p, h).start()

    every_pair(slots, info_s, w_second, lhs_ref, z_even, z_odd, live, other)
    for p in range(slots):
        for h in range(2):
            copy(p, h).wait()


def pack_body(own_ref, sent_ref, rows_ref, sems):
    upper = lax.axis_index("wave") % 2
    tile_rows = own_ref.shape[0]
    copies = []
    for n in range(0, NEAR, PIECE):
        source = own_ref.at[pl.ds(upper * (tile_rows - NEAR) + n, PIECE)]
        copies.append(pltpu.make_async_copy(source, sent_ref.at[n:n + PIECE], sems.at[BEYOND + n // PIECE]))
    for k in range(BEYOND):
        row = jnp.where(upper == 1, tile_rows - NEAR - 1 - 2 * k, NEAR + 1 + 2 * k)
        copies.append(pltpu.make_async_copy(own_ref.at[pl.ds(row, 1)], rows_ref.at[k:k + 1], sems.at[k]))
    for copy in copies:
        copy.start()
    for copy in copies[-BEYOND:]:
        copy.wait()
    for k in range(BEYOND):
        sent_ref[NEAR + k // 2, 8 * (k % 2):8 * (k % 2) + 8, :] = rows_ref[k, pl.ds(0, 8, stride=2), :]
    for copy in copies[:-BEYOND]:
        copy.wait()


def inner_body(
    even_ref, odd_ref, low_ref, wave_ref, pairs_ref, own_ref,
    taps_ref, w_first, w_second, grid_ref, low_zero, low_one, m_ref, part_ref, info_s,
    even_s, odd_s, low_s, wave_s, pairs_s, low_lhs, z_ref, lhs_second, z2_even, z2_odd, sems, *, slots,
):
    tile_rows = own_ref.shape[0]
    moves = (
        (even_ref, even_s), (odd_ref, odd_s), (low_ref, low_s), (wave_ref, wave_s), (pairs_ref, pairs_s),
        (own_ref, grid_ref.at[pl.ds(FRONT + HALO, tile_rows)]),
    )
    copies = [pltpu.make_async_copy(source, place, sems.at[n]) for n, (source, place) in enumerate(moves)]
    for copy in copies:
        copy.start()
    for copy in copies[:-1]:
        copy.wait()
    make_filters(even_s, odd_s, low_s, taps_ref, w_first, w_second)
    read_tables(wave_s, pairs_s, lax.axis_index("wave") * slots, slots, info_s)
    copies[-1].wait()
    need = needed(info_s, slots)
    low_refs = (low_zero, low_one)
    filter_rows(need, [(FRONT + HALO, tile_rows)] * 2, w_first, grid_ref, low_refs, low_lhs)
    first_rows(need, INNER, (0, 0), tile_rows, taps_ref, w_first, grid_ref, low_refs, m_ref, low_lhs, z_ref)
    inner_sums(need, slots, info_s, taps_ref, w_second, m_ref, part_ref, lhs_second, z2_even, z2_odd)


def add_side(side, info_s, halo_ref, taps_ref, w_first, grid_ref, low_refs, m_ref, low_lhs, z_ref, slots, tile_rows):
    far = FRONT + HALO + tile_rows
    near = jnp.where(side == 1, FRONT + HALO - NEAR, far)
    for r in range(NEAR):
        grid_ref[near + r] = halo_ref[r]
    for k in range(BEYOND):
        row = jnp.where(side == 1, FRONT + HALO - NEAR - 1 - 2 * k, far + NEAR + 1 + 2 * k)
        grid_ref[row, pl.ds(0, 8, stride=2), :] = halo_ref[NEAR + k // 2, 8 * (k % 2):8 * (k % 2) + 8, :]
    need = needed(info_s, slots)
    spans = [(near, NEAR), (jnp.where(side == 1, FRONT, far), HALO)]
    filter_rows(need, spans, w_first, grid_ref, low_refs, low_lhs)
    starts = [[jnp.where(side == 1, x, y) for x, y in zip(*both)] for both in zip(BEFORE, AFTER)]
    first_rows(need, starts, EDGE, tile_rows, taps_ref, w_first, grid_ref, low_refs, m_ref, low_lhs, z_ref)
    return need


def side_body(
    info_s, got_ref, taps_ref, w_first, grid_in, zero_in, one_in, m_in,
    grid_ref, low_zero, low_one, m_ref, low_lhs, z_ref, *, slots, tile_rows,
):
    side = lax.axis_index("wave") % 2
    add_side(side, info_s, got_ref, taps_ref, w_first, grid_ref, (low_zero, low_one), m_ref, low_lhs, z_ref, slots, tile_rows)


def last_body(
    info_s, other_ref, taps_ref, w_first, grid_in, zero_in, one_in, m_in, w_second, part_ref,
    out_ref, grid_ref, low_zero, low_one, m_ref, low_lhs, z_ref, lhs_second, z2_even, z2_odd, done_ref, sems,
    *, slots, tile_rows,
):
    side = 1 - lax.axis_index("wave") % 2
    need = add_side(side, info_s, other_ref, taps_ref, w_first, grid_ref, (low_zero, low_one), m_ref, low_lhs, z_ref, slots, tile_rows)
    second_order(need, slots, info_s, taps_ref, w_second, m_ref, part_ref, out_ref, lhs_second, z2_even, z2_odd, done_ref, sems)


def shards(density, even_taps, odd_taps, low_taps, wavelets, pairs):
    tile_rows, ny, nz = density.shape
    count, waves = lax.axis_size("space"), lax.axis_size("wave")
    slots = pairs.shape[0] // waves
    step = (-1, 1)
    moves = [
        (z * waves + w, (z + step[w % 2]) * waves + w)
        for z in range(count)
        for w in range(waves)
        if 0 <= z + step[w % 2] < count
    ]
    smem = pl.BlockSpec(memory_space=pltpu.SMEM)
    vmem = pl.BlockSpec(memory_space=pltpu.VMEM)
    anywhere = pl.BlockSpec(memory_space=pl.ANY)
    params = pltpu.CompilerParams(vmem_limit_bytes=24 * 1024 * 1024)

    def held(value):
        return pltpu.with_memory_space_constraint(value, pltpu.VMEM)

    def far(value):
        return pltpu.with_memory_space_constraint(value, pltpu.HBM)

    def cost(us):
        return pl.CostEstimate(flops=us * 1000000000, bytes_accessed=us * 2500000, transcendentals=0)

    density = far(density)
    sent = pl.pallas_call(
        pack_body,
        out_shape=pltpu.VMEM((SENT, ny, nz), F32),
        in_specs=[anywhere],
        out_specs=vmem,
        scratch_shapes=[pltpu.VMEM((BEYOND, ny, nz), F32), pltpu.SemaphoreType.DMA((BEYOND + NEAR // PIECE,))],
        compiler_params=params,
        name="pack_halo",
    )(density)
    got = lax.ppermute(sent, ("space", "wave"), moves)
    state_types = [
        pltpu.VMEM((WINDOW, ny, nz), F32),
        pltpu.VMEM((WINDOW, ny, nz), F32),
        pltpu.VMEM((WINDOW // 2, ny // 2, nz), F32),
        pltpu.VMEM((6, STORED, 8, 128), F32),
    ]
    part_type = pltpu.VMEM((slots, tile_rows // 2, 8, 128), F32)
    out_shape = (slots, tile_rows // 2, ny // 2, nz // 2)
    scratch = [pltpu.VMEM((1024, 256), BF16), pltpu.VMEM((3, 384, 128), F32)]
    taps, w_first, w_second, *state, part, info = pl.pallas_call(
        functools.partial(inner_body, slots=slots),
        out_shape=[
            pltpu.VMEM((4, 16, 8, 128), F32),
            pltpu.VMEM((2, 256, 512), BF16),
            pltpu.VMEM((4, 256, 128), BF16),
            *state_types,
            part_type,
            pltpu.SMEM((4 * slots + 8,), jnp.int32),
        ],
        in_specs=[anywhere] * 6,
        out_specs=[vmem] * 8 + [smem],
        scratch_shapes=[
            pltpu.SMEM((TAPS,), F32),
            pltpu.SMEM((TAPS,), F32),
            pltpu.SMEM((TAPS,), F32),
            pltpu.SMEM(wavelets.shape[::-1], jnp.int32),
            pltpu.SMEM(pairs.shape[::-1], jnp.int32),
            *scratch,
            pltpu.VMEM((6, 24 * 8, 256), BF16),
            pltpu.VMEM((24, 8, 128), F32),
            pltpu.VMEM((24, 8, 128), F32),
            pltpu.SemaphoreType.DMA((6,)),
        ],
        compiler_params=params,
        cost_estimate=cost(3),
        name="inner_rows",
    )(*map(far, (even_taps, odd_taps, low_taps, wavelets.T, pairs.T)), density)
    got, state[0] = lax.optimization_barrier((got, state[0]))
    other = lax.ppermute(got, "wave", [(w, w ^ 1) for w in range(waves)])
    taps, w_first, w_second = map(held, (taps, w_first, w_second))
    info = pltpu.with_memory_space_constraint(info, pltpu.SMEM)
    state = pl.pallas_call(
        functools.partial(side_body, slots=slots, tile_rows=tile_rows),
        out_shape=state_types,
        in_specs=[smem] + [vmem] * 7,
        out_specs=[vmem] * 4,
        input_output_aliases={4: 0, 5: 1, 6: 2, 7: 3},
        scratch_shapes=scratch,
        compiler_params=params,
        cost_estimate=cost(2),
        name="side_rows",
    )(info, held(got), taps, w_first, *map(held, state))
    second, *_ = pl.pallas_call(
        functools.partial(last_body, slots=slots, tile_rows=tile_rows),
        out_shape=[jax.ShapeDtypeStruct(out_shape, F32), *state_types],
        in_specs=[smem] + [vmem] * 9,
        out_specs=[anywhere] + [vmem] * 4,
        input_output_aliases={4: 1, 5: 2, 6: 3, 7: 4},
        scratch_shapes=scratch + [
            pltpu.VMEM((6, 46 * 8, 256), BF16),
            pltpu.VMEM((46, 8, 128), F32),
            pltpu.VMEM((46, 8, 128), F32),
            pltpu.VMEM(out_shape, F32),
            pltpu.SemaphoreType.DMA((slots, 2)),
        ],
        compiler_params=params,
        cost_estimate=cost(5),
        name="side_rows_and_pairs",
    )(info, held(other), taps, w_first, *map(held, state), w_second, held(part))
    return second


def solution(mesh):
    placed = (P(("groups", "space"), None, None), P(), P(), P(), P(), P())
    return jax.shard_map(
        shards,
        mesh=mesh,
        in_specs=placed,
        out_specs=P("wave", ("groups", "space"), None, None),
        check_vma=False,
    )
```

```python
import functools

import jax
import jax.numpy as jnp
from jax import lax
from jax.experimental import pallas as pl
from jax.experimental.pallas import tpu as pltpu
from jax.sharding import PartitionSpec as P

TAPS = 15
HALF = 7
HALO = 42
NEAR = 35
BEYOND = 4
SENT = NEAR + BEYOND // 2
PIECE = 5
FRONT = 8
WINDOW = 160
KEPT = 60
STORED = 72
SHIFT = 6
SIDE = (3, 3)
BEFORE = (-6, -3)
AFTER = (42, 36)
INNER = (3, 2)
INNER_FROM = (18, 21)
GROUP = (6, 8)
KNOWN = ((18, 42), (21, 37))
OUTER = (((0, 18), (42, 60)), ((0, 22), (36, 60)))
UNUSED = 6
EPS = 1e-6
F32 = jnp.float32
BF16 = jnp.bfloat16
LOW, EVEN, ODD, BOTH = 0, 1, 2, 3
TILE = (8, 128)


def split(value):
    high = value.astype(BF16)
    return high, (value - high.astype(F32)).astype(BF16)


def dot(a, b):
    return jnp.dot(a, b, preferred_element_type=F32)


def rows(shape):
    return lax.broadcasted_iota(jnp.int32, shape, 0)


def lanes(shape):
    return lax.broadcasted_iota(jnp.int32, shape, 1)


def modulus(value):
    squares = value * value
    total = squares + pltpu.roll(squares, 64, 1) + EPS
    return total * lax.rsqrt(total)


def weigh(taps, values, pairs):
    acc = None
    for t, v in pairs:
        term = taps[t] * values[v]
        acc = term if acc is None else acc + term
    return acc


def banded(taps_ref, offset, dilation):
    low = both = jnp.zeros(offset.shape, F32)
    for t in range(TAPS):
        here = offset == (t - HALF) * dilation
        low = jnp.where(here, taps_ref[LOW, t][0:1], low)
        both = jnp.where(here, taps_ref[BOTH, t][0:1], both)
    return low, both


def make_filters(even_s, odd_s, low_s, taps_ref, w_first, w_second):
    left = lanes(TILE) < 64
    for t in range(TAPS):
        even = jnp.full(TILE, even_s[t], F32)
        odd = jnp.full(TILE, odd_s[t], F32)
        taps_ref[LOW, t] = jnp.full(TILE, low_s[t], F32)
        taps_ref[EVEN, t] = even
        taps_ref[ODD, t] = odd
        taps_ref[BOTH, t] = jnp.where(left, even, odd)
    wide = (128, 128)
    none = jnp.zeros(wide, BF16)
    for level in range(2):
        low, both = banded(taps_ref, rows(wide) - 2 * (lanes(wide) % 64), 1 << level)
        for kind, matrix in enumerate((low, both)):
            high, rest = split(matrix)
            column = 256 * kind
            w_first[level, 0:128, column:column + 128] = high
            w_first[level, 128:256, column:column + 128] = high
            w_first[level, 0:128, column + 128:column + 256] = rest
            w_first[level, 128:256, column + 128:column + 256] = none
        half = (64, 128)
        low, both = banded(taps_ref, rows(half) - lanes(half) % 64, 1 << level)
        for kind, matrix in enumerate((low, both)):
            high, rest = split(matrix)
            w_second[2 * level + kind, 0:64] = high
            w_second[2 * level + kind, 64:128] = high
            w_second[2 * level + kind, 128:192] = rest
            w_second[2 * level + kind, 192:256] = jnp.zeros(half, BF16)


def read_tables(wave_s, pairs_s, base, slots, info_s):
    found = []
    need = [False] * 6
    for p in range(slots):
        field, wavelet = pairs_s[0, base + p], pairs_s[1, base + p]
        safe = jnp.maximum(field, 0)
        live = field >= 0
        source = wave_s[0, safe] * 3 + wave_s[1, safe]
        level, orient = wave_s[0, wavelet], wave_s[1, wavelet]
        key = jnp.where(live, (source * 4 + level) * 4 + orient, -1)
        twin = jnp.int32(-1)
        for q in range(p - 1, -1, -1):
            twin = jnp.where(found[q] == key, q, twin)
        found.append(key)
        info_s[p] = jnp.where(live, jnp.where(twin >= 0, 3, level), 0)
        info_s[slots + p] = source
        info_s[2 * slots + p] = orient
        info_s[3 * slots + p] = jnp.maximum(twin, 0)
        for k in range(6):
            need[k] = need[k] | (live & (source == k))
    for k in range(6):
        info_s[4 * slots + k] = need[k].astype(jnp.int32)


def needed(info_s, slots):
    return [[info_s[4 * slots + level * 3 + orient] > 0 for orient in range(3)] for level in range(2)]


def filter_rows(need, spans, w_first, grid_ref, low_refs, low_lhs):
    @pl.when(need[0][0])
    def _():
        place, count = spans[0]
        for r in range(count):
            high, rest = split(grid_ref[place + r])
            low_lhs[r * 16:r * 16 + 16, 0:128] = high
            low_lhs[r * 16:r * 16 + 16, 128:256] = rest
        z = dot(low_lhs[0:count * 16, :], w_first[0, :, 0:256])
        low_refs[0][pl.ds(place, count)] = (z[:, 0:128] + z[:, 128:256]).reshape(count, 16, 128)

    @pl.when(need[1][0])
    def _():
        place, count = spans[1]
        pairs = (count + 3) // 4
        for r in range(pairs):
            even = [grid_ref[place + 4 * r + n, pl.ds(0, 8, stride=2), :] for n in (0, 2)]
            high, rest = split(jnp.concatenate(even, axis=0))
            low_lhs[r * 16:r * 16 + 16, 0:128] = high
            low_lhs[r * 16:r * 16 + 16, 128:256] = rest
        z = dot(low_lhs[0:pairs * 16, :], w_first[1, :, 0:256])
        low_refs[1][pl.ds(place // 2, 2 * pairs)] = (z[:, 0:128] + z[:, 128:256]).reshape(2 * pairs, 8, 128)


def first_rows(need, chunks, starts, skips, tile_rows, taps_ref, w_first, grid_ref, low_refs, m_ref, low_lhs, z_ref):
    rank = lax.axis_index("space")
    total = lax.axis_size("space") * tile_rows

    def x_pass(level, kind, store):
        taps = [taps_ref[kind, t] for t in range(TAPS)]
        stride = 2 - level
        group = GROUP[level]
        skip, count = skips[level]

        def step(n, carry):
            start = starts[level] + skip + group * n
            parts = []
            for h in range(2 - level):
                sums = [None] * group
                for r in range(stride * (group - 1) + TAPS):
                    if level == 0:
                        ref = low_refs[0] if kind == BOTH else grid_ref
                        value = ref[2 * start + HALF + FRONT + r, 8 * h:8 * h + 8, :]
                    elif kind == BOTH:
                        value = low_refs[1][start + r + FRONT // 2]
                    else:
                        value = grid_ref[2 * (start + r) + FRONT, pl.ds(0, 8, stride=2), :]
                    for i in range(group):
                        t = r - stride * i
                        if 0 <= t < TAPS:
                            term = taps[t] * value
                            sums[i] = term if sums[i] is None else sums[i] + term
                parts.append(sums)
            at = (skip + group * n) * (16 >> level)
            for i in range(0, group, 1 + level):
                second = parts[1][i] if level == 0 else parts[0][i + 1]
                store(pl.multiple_of(at + i * (16 >> level), 16), jnp.concatenate([parts[0][i], second], axis=0))
            return carry

        lax.fori_loop(0, count, step, 0)

    def finish(level, orient):
        height = 16 >> level
        taps = taps_ref.at[BOTH if orient == 1 else LOW]
        place = m_ref.at[level * 3 + orient].reshape(STORED * 8, 128)

        def step(n, carry):
            start = starts[level] + 8 * n
            at = pl.multiple_of(n * 8 * height, 8)
            values = [z_ref[orient, pl.ds(at + y, 8, stride=height), :] for y in range(height)]
            i = start + rows(TILE)
            x = rank * tile_rows - 28 + 2 * i
            inside = (x >= 0) & (x < total) & (i >= 0) & (i < KEPT)
            for j in range(8):
                terms = [(y - (2 - level) * j + HALF, y) for y in range(height)]
                out = modulus(weigh(taps, values, [(t, y) for t, y in terms if 0 <= t < TAPS]))
                place[pl.ds((start + SHIFT) * 8 + j, 8, stride=8), :] = jnp.where(inside, out, 0.0)
            return carry

        lax.fori_loop(0, chunks[level], step, 0)

    for level in range(2):
        size = (128 >> level) * chunks[level]

        @pl.when(need[level][1] | need[level][2])
        def _():
            def store(at, value):
                high, rest = split(value)
                low_lhs[pl.ds(at, 16), 0:128] = high
                low_lhs[pl.ds(at, 16), 128:256] = rest

            x_pass(level, LOW, store)
            z = dot(low_lhs[0:size, :], w_first[level])
            z_ref[1, 0:size, :] = z[:, 0:128] + z[:, 128:256]
            z_ref[2, 0:size, :] = z[:, 256:384] + z[:, 384:512]

        for orient in (1, 2):
            @pl.when(need[level][orient])
            def _():
                finish(level, orient)

        @pl.when(need[level][0])
        def _():
            def store(at, value):
                z_ref[0, pl.ds(at, 16), :] = value

            x_pass(level, BOTH, store)
            finish(level, 0)


def pack_rows(need, blocks, m_ref, lhs_ref):
    left = lanes((16, 128)) < 64
    for level in range(2):
        for orient in range(3):
            @pl.when(need[level][orient])
            def _():
                source = level * 3 + orient
                at = 0
                for first, end in blocks[level]:
                    for i in range(first, end, 2):
                        value = jnp.concatenate([m_ref[source, i + SHIFT], m_ref[source, i + 1 + SHIFT]], axis=0)
                        high = value.astype(BF16)
                        wide = high.astype(F32)
                        lhs_ref[source, at:at + 16, 0:128] = jnp.where(left, wide, value - wide).astype(BF16)
                        lhs_ref[source, at:at + 16, 128:256] = high
                        at += 16


def every_pair(slots, info_s, w_second, lhs_ref, z2_ref, sums, rest, other):
    def z_pass(p):
        kind = 2 * (info_s[p] == 2).astype(jnp.int32) + (info_s[2 * slots + p] == 2).astype(jnp.int32)
        z2_ref[...] = dot(lhs_ref[info_s[slots + p]], w_second[kind]).reshape(z2_ref.shape)

    def one_pair(p, carry):
        mode, source = info_s[p], info_s[slots + p]
        following = jnp.minimum(p + 1, slots - 1)
        for dilation, level in ((1, 0), (2, 0), (2, 1)):
            @pl.when((mode == dilation) & ((source >= 3) == (level == 1)))
            def _():
                sums(p, dilation, level)
                z_pass(following)
                rest(p, dilation)

        @pl.when(mode == 3)
        def _():
            z_pass(following)

        other(p, mode)
        return carry

    z_pass(0)
    lax.fori_loop(0, slots, one_pair, 0)


def x_sums(taps, first, dilation, sums, have, read):
    for r in range(first, first + 16 + 14 * dilation):
        if have(r):
            value = read(r)
            for i in range(16):
                if (r - first - i) % dilation == 0 and 0 <= (r - first - i) // dilation < TAPS:
                    term = taps[(r - first - i) // dilation] * value
                    sums[i] = term if sums[i] is None else sums[i] + term
    return sums


def inner_sums(need, slots, info_s, taps_ref, w_second, m_ref, part_ref, lhs_ref, z2_ref):
    pack_rows(need, [[(low, high)] for low, high in KNOWN], m_ref, lhs_ref)

    def inner(p, dilation, level):
        taps_at = taps_ref.at[jnp.where(info_s[2 * slots + p] == 0, BOTH, LOW)]
        taps = [taps_at[t] for t in range(TAPS)]
        low, high = KNOWN[level]
        for c in range(0, 32, 16):
            sums = x_sums(taps, c + 14 - HALF * dilation, dilation, [None] * 16, lambda r: low <= r < high, lambda r: z2_ref[r - low])
            for i in range(16):
                part_ref[p, c + i] = sums[i]

    every_pair(slots, info_s, w_second, lhs_ref, z2_ref, inner, lambda p, dilation: None, lambda p, mode: None)


def second_order(need, slots, info_s, taps_ref, w_second, m_ref, part_ref, out_ref, lhs_ref, z2_ref, line_ref, done_ref, sems):
    pack_rows(need, OUTER, m_ref, lhs_ref)
    half = done_ref.shape[1] // 2

    def copy(p, h):
        rows_at = pl.ds(h * half, half)
        return pltpu.make_async_copy(done_ref.at[p, rows_at], out_ref.at[p, rows_at], sems.at[p, h])

    def outer(p, dilation, level):
        taps_at = taps_ref.at[jnp.where(info_s[2 * slots + p] == 0, BOTH, LOW)]
        taps = [taps_at[t] for t in range(TAPS)]
        low, high = KNOWN[level]
        (_, split_at), (rest, _) = OUTER[level]
        for c in range(0, 32, 16):
            sums = x_sums(
                taps, c + 14 - HALF * dilation, dilation, [part_ref[p, c + i] for i in range(16)],
                lambda r: not low <= r < high, lambda r: z2_ref[r if r < low else r - rest + split_at],
            )
            for i in range(16):
                line_ref[(c + i) * 8:(c + i) * 8 + 8, :] = sums[i]

    def finish(p, dilation):
        taps = taps_ref.at[jnp.where(info_s[2 * slots + p] == 1, BOTH, LOW)]
        place = done_ref.at[p].reshape(done_ref.shape[1] * 8, 64)
        for c in range(4):
            lines = [line_ref[pl.ds(c * 64 + y, 8, stride=8), :] for y in range(8)]
            for j in range(8):
                terms = [((y - j) // dilation + HALF, y) for y in range(8) if (y - j) % dilation == 0]
                out = modulus(weigh(taps, lines, terms))
                place[pl.ds(c * 64 + j, 8, stride=8), :] = out[:, 0:64]
            if c % 2:
                copy(p, c // 2).start()

    def other(p, mode):
        @pl.when((mode == 0) | (mode == 3))
        def _():
            @pl.when(mode == 3)
            def _():
                done_ref[p] = done_ref[info_s[3 * slots + p]]

            @pl.when(mode == 0)
            def _():
                done_ref[p] = jnp.zeros(done_ref.shape[1:], F32)

            for h in range(2):
                copy(p, h).start()

    every_pair(slots, info_s, w_second, lhs_ref, z2_ref, outer, finish, other)
    for p in range(slots):
        for h in range(2):
            copy(p, h).wait()


def pack_body(own_ref, sent_ref, rows_ref, sems):
    upper = lax.axis_index("wave") % 2
    tile_rows = own_ref.shape[0]
    copies = []
    for n in range(0, NEAR, PIECE):
        source = own_ref.at[pl.ds(upper * (tile_rows - NEAR) + n, PIECE)]
        copies.append(pltpu.make_async_copy(source, sent_ref.at[n:n + PIECE], sems.at[BEYOND + n // PIECE]))
    for k in range(BEYOND):
        row = jnp.where(upper == 1, tile_rows - NEAR - 1 - 2 * k, NEAR + 1 + 2 * k)
        copies.append(pltpu.make_async_copy(own_ref.at[pl.ds(row, 1)], rows_ref.at[k:k + 1], sems.at[k]))
    for copy in copies:
        copy.start()
    for copy in copies[-BEYOND:]:
        copy.wait()
    for k in range(BEYOND):
        sent_ref[NEAR + k // 2, 8 * (k % 2):8 * (k % 2) + 8, :] = rows_ref[k, pl.ds(0, 8, stride=2), :]
    for copy in copies[:-BEYOND]:
        copy.wait()


def inner_body(
    even_ref, odd_ref, low_ref, wave_ref, pairs_ref, own_ref,
    taps_ref, w_first, w_second, grid_ref, low_zero, low_one, m_ref, part_ref, info_s,
    even_s, odd_s, low_s, wave_s, pairs_s, low_lhs, z_ref, lhs_second, z2_ref, sems, *, slots,
):
    tile_rows = own_ref.shape[0]
    moves = (
        (even_ref, even_s), (odd_ref, odd_s), (low_ref, low_s), (wave_ref, wave_s), (pairs_ref, pairs_s),
        (own_ref, grid_ref.at[pl.ds(FRONT + HALO, tile_rows)]),
    )
    copies = [pltpu.make_async_copy(source, place, sems.at[n]) for n, (source, place) in enumerate(moves)]
    for copy in copies:
        copy.start()
    for copy in copies[:-1]:
        copy.wait()
    make_filters(even_s, odd_s, low_s, taps_ref, w_first, w_second)
    read_tables(wave_s, pairs_s, lax.axis_index("wave") * slots, slots, info_s)
    copies[-1].wait()
    need = needed(info_s, slots)
    low_refs = (low_zero, low_one)
    filter_rows(need, [(FRONT + HALO, tile_rows)] * 2, w_first, grid_ref, low_refs, low_lhs)
    first_rows(need, INNER, INNER_FROM, ((0, 4), (0, 2)), tile_rows, taps_ref, w_first, grid_ref, low_refs, m_ref, low_lhs, z_ref)
    inner_sums(need, slots, info_s, taps_ref, w_second, m_ref, part_ref, lhs_second, z2_ref)


def add_side(side, info_s, halo_ref, taps_ref, w_first, grid_ref, low_refs, m_ref, low_lhs, z_ref, slots, tile_rows):
    far = FRONT + HALO + tile_rows
    near = jnp.where(side == 1, FRONT + HALO - NEAR, far)
    for r in range(NEAR):
        grid_ref[near + r] = halo_ref[r]
    for k in range(BEYOND):
        row = jnp.where(side == 1, FRONT + HALO - NEAR - 1 - 2 * k, far + NEAR + 1 + 2 * k)
        grid_ref[row, pl.ds(0, 8, stride=2), :] = halo_ref[NEAR + k // 2, 8 * (k % 2):8 * (k % 2) + 8, :]
    need = needed(info_s, slots)
    spans = [(near, NEAR), (jnp.where(side == 1, FRONT, far), HALO)]
    filter_rows(need, spans, w_first, grid_ref, low_refs, low_lhs)
    starts = [jnp.where(side == 1, x, y) for x, y in zip(BEFORE, AFTER)]
    skips = ((jnp.where(side == 1, UNUSED, 0), 3), (0, 3))
    first_rows(need, SIDE, starts, skips, tile_rows, taps_ref, w_first, grid_ref, low_refs, m_ref, low_lhs, z_ref)
    return need


def side_body(
    info_s, got_ref, taps_ref, w_first, grid_in, zero_in, one_in, m_in,
    grid_ref, low_zero, low_one, m_ref, low_lhs, z_ref, *, slots, tile_rows,
):
    side = lax.axis_index("wave") % 2
    add_side(side, info_s, got_ref, taps_ref, w_first, grid_ref, (low_zero, low_one), m_ref, low_lhs, z_ref, slots, tile_rows)


def last_body(
    info_s, other_ref, taps_ref, w_first, grid_in, zero_in, one_in, m_in, w_second, part_ref,
    out_ref, grid_ref, low_zero, low_one, m_ref, low_lhs, z_ref, lhs_second, z2_ref, line_ref, done_ref, sems,
    *, slots, tile_rows,
):
    side = 1 - lax.axis_index("wave") % 2
    need = add_side(side, info_s, other_ref, taps_ref, w_first, grid_ref, (low_zero, low_one), m_ref, low_lhs, z_ref, slots, tile_rows)
    second_order(need, slots, info_s, taps_ref, w_second, m_ref, part_ref, out_ref, lhs_second, z2_ref, line_ref, done_ref, sems)


def shards(density, even_taps, odd_taps, low_taps, wavelets, pairs):
    tile_rows, ny, nz = density.shape
    count, waves = lax.axis_size("space"), lax.axis_size("wave")
    slots = pairs.shape[0] // waves
    step = (-1, 1)
    moves = [
        (z * waves + w, (z + step[w % 2]) * waves + w)
        for z in range(count)
        for w in range(waves)
        if 0 <= z + step[w % 2] < count
    ]
    smem = pl.BlockSpec(memory_space=pltpu.SMEM)
    vmem = pl.BlockSpec(memory_space=pltpu.VMEM)
    anywhere = pl.BlockSpec(memory_space=pl.ANY)
    params = pltpu.CompilerParams(vmem_limit_bytes=24 * 1024 * 1024)

    def held(value):
        return pltpu.with_memory_space_constraint(value, pltpu.VMEM)

    def far(value):
        return pltpu.with_memory_space_constraint(value, pltpu.HBM)

    def cost(us):
        return pl.CostEstimate(flops=us * 1000000000, bytes_accessed=us * 2500000, transcendentals=0)

    density = far(density)
    sent = pl.pallas_call(
        pack_body,
        out_shape=pltpu.VMEM((SENT, ny, nz), F32),
        in_specs=[anywhere],
        out_specs=vmem,
        scratch_shapes=[pltpu.VMEM((BEYOND, ny, nz), F32), pltpu.SemaphoreType.DMA((BEYOND + NEAR // PIECE,))],
        compiler_params=params,
        name="pack_halo",
    )(density)
    got = lax.ppermute(sent, ("space", "wave"), moves)
    state_types = [
        pltpu.VMEM((WINDOW, ny, nz), F32),
        pltpu.VMEM((WINDOW, ny, nz), F32),
        pltpu.VMEM((WINDOW // 2, ny // 2, nz), F32),
        pltpu.VMEM((6, STORED, 8, 128), F32),
    ]
    part_type = pltpu.VMEM((slots, tile_rows // 2, 8, 128), F32)
    out_shape = (slots, tile_rows // 2, ny // 2, nz // 2)
    scratch = [pltpu.VMEM((1024, 256), BF16), pltpu.VMEM((3, 384, 128), F32)]
    taps, w_first, w_second, *state, part, info = pl.pallas_call(
        functools.partial(inner_body, slots=slots),
        out_shape=[
            pltpu.VMEM((4, 16, 8, 128), F32),
            pltpu.VMEM((2, 256, 512), BF16),
            pltpu.VMEM((4, 256, 128), BF16),
            *state_types,
            part_type,
            pltpu.SMEM((4 * slots + 8,), jnp.int32),
        ],
        in_specs=[anywhere] * 6,
        out_specs=[vmem] * 8 + [smem],
        scratch_shapes=[
            pltpu.SMEM((TAPS,), F32),
            pltpu.SMEM((TAPS,), F32),
            pltpu.SMEM((TAPS,), F32),
            pltpu.SMEM(wavelets.shape[::-1], jnp.int32),
            pltpu.SMEM(pairs.shape[::-1], jnp.int32),
            *scratch,
            pltpu.VMEM((6, 24 * 8, 256), BF16),
            pltpu.VMEM((24, 8, 128), F32),
            pltpu.SemaphoreType.DMA((6,)),
        ],
        compiler_params=params,
        cost_estimate=cost(3),
        name="inner_rows",
    )(*map(far, (even_taps, odd_taps, low_taps, wavelets.T, pairs.T)), density)
    got, state[0] = lax.optimization_barrier((got, state[0]))
    other = lax.ppermute(got, "wave", [(w, w ^ 1) for w in range(waves)])
    taps, w_first, w_second = map(held, (taps, w_first, w_second))
    info = pltpu.with_memory_space_constraint(info, pltpu.SMEM)
    state = pl.pallas_call(
        functools.partial(side_body, slots=slots, tile_rows=tile_rows),
        out_shape=state_types,
        in_specs=[smem] + [vmem] * 7,
        out_specs=[vmem] * 4,
        input_output_aliases={4: 0, 5: 1, 6: 2, 7: 3},
        scratch_shapes=scratch,
        compiler_params=params,
        cost_estimate=cost(2),
        name="side_rows",
    )(info, held(got), taps, w_first, *map(held, state))
    second, *_ = pl.pallas_call(
        functools.partial(last_body, slots=slots, tile_rows=tile_rows),
        out_shape=[jax.ShapeDtypeStruct(out_shape, F32), *state_types],
        in_specs=[smem] + [vmem] * 9,
        out_specs=[anywhere] + [vmem] * 4,
        input_output_aliases={4: 1, 5: 2, 6: 3, 7: 4},
        scratch_shapes=scratch + [
            pltpu.VMEM((6, 46 * 8, 256), BF16),
            pltpu.VMEM((46, 8, 128), F32),
            pltpu.VMEM((256, 128), F32),
            pltpu.VMEM(out_shape, F32),
            pltpu.SemaphoreType.DMA((slots, 2)),
        ],
        compiler_params=params,
        cost_estimate=cost(5),
        name="side_rows_and_pairs",
    )(info, held(other), taps, w_first, *map(held, state), w_second, held(part))
    return second


def solution(mesh):
    placed = (P(("groups", "space"), None, None), P(), P(), P(), P(), P())
    return jax.shard_map(
        shards,
        mesh=mesh,
        in_specs=placed,
        out_specs=P("wave", ("groups", "space"), None, None),
        check_vma=False,
    )
```

```python
import functools

import jax
import jax.numpy as jnp
from jax import lax
from jax.experimental import pallas as pl
from jax.experimental.pallas import tpu as pltpu
from jax.sharding import PartitionSpec as P

TAPS = 15
HALF = 7
HALO = 42
NEAR = 35
BEYOND = 4
SENT = NEAR + BEYOND // 2
PIECE = 5
FRONT = 8
WINDOW = 160
KEPT = 60
STORED = 72
SHIFT = 6
INNER = ((18, 26, 34), (21, 29))
BEFORE = ((-6, 2, 10), (-3, 5, 13))
AFTER = ((52, 42, 50), (36, 44, 52))
KNOWN = ((18, 42), (21, 37))
OUTER = (((0, 18), (42, 60)), ((0, 22), (36, 60)))
EDGE = (6, 0)
EPS = 1e-6
F32 = jnp.float32
BF16 = jnp.bfloat16
LOW, EVEN, ODD, BOTH = 0, 1, 2, 3
TILE = (8, 128)


def split(value):
    high = value.astype(BF16)
    return high, (value - high.astype(F32)).astype(BF16)


def dot(a, b):
    return jnp.dot(a, b, preferred_element_type=F32)


def rows(shape):
    return lax.broadcasted_iota(jnp.int32, shape, 0)


def lanes(shape):
    return lax.broadcasted_iota(jnp.int32, shape, 1)


def modulus(value):
    squares = value * value
    total = squares + pltpu.roll(squares, 64, 1) + EPS
    return total * lax.rsqrt(total)


def weigh(taps, values, pairs):
    acc = None
    for t, v in pairs:
        term = taps[t] * values[v]
        acc = term if acc is None else acc + term
    return acc


def banded(taps_ref, offset, dilation):
    low = both = jnp.zeros(offset.shape, F32)
    for t in range(TAPS):
        here = offset == (t - HALF) * dilation
        low = jnp.where(here, taps_ref[LOW, t][0:1], low)
        both = jnp.where(here, taps_ref[BOTH, t][0:1], both)
    return low, both


def make_filters(even_s, odd_s, low_s, taps_ref, w_first, w_second):
    left = lanes(TILE) < 64
    for t in range(TAPS):
        even = jnp.full(TILE, even_s[t], F32)
        odd = jnp.full(TILE, odd_s[t], F32)
        taps_ref[LOW, t] = jnp.full(TILE, low_s[t], F32)
        taps_ref[EVEN, t] = even
        taps_ref[ODD, t] = odd
        taps_ref[BOTH, t] = jnp.where(left, even, odd)
    wide = (128, 128)
    none = jnp.zeros(wide, BF16)
    for level in range(2):
        low, both = banded(taps_ref, rows(wide) - 2 * (lanes(wide) % 64), 1 << level)
        for kind, matrix in enumerate((low, both)):
            high, rest = split(matrix)
            column = 256 * kind
            w_first[level, 0:128, column:column + 128] = high
            w_first[level, 128:256, column:column + 128] = high
            w_first[level, 0:128, column + 128:column + 256] = rest
            w_first[level, 128:256, column + 128:column + 256] = none
        half = (64, 128)
        low, both = banded(taps_ref, rows(half) - lanes(half) % 64, 1 << level)
        for kind, matrix in enumerate((low, both)):
            high, rest = split(matrix)
            w_second[2 * level + kind, 0:64] = high
            w_second[2 * level + kind, 64:128] = high
            w_second[2 * level + kind, 128:192] = rest
            w_second[2 * level + kind, 192:256] = jnp.zeros(half, BF16)


def read_tables(wave_s, pairs_s, base, slots, info_s):
    found = []
    need = [False] * 6
    for p in range(slots):
        field, wavelet = pairs_s[0, base + p], pairs_s[1, base + p]
        safe = jnp.maximum(field, 0)
        live = field >= 0
        source = wave_s[0, safe] * 3 + wave_s[1, safe]
        level, orient = wave_s[0, wavelet], wave_s[1, wavelet]
        key = jnp.where(live, (source * 4 + level) * 4 + orient, -1)
        twin = jnp.int32(-1)
        for q in range(p - 1, -1, -1):
            twin = jnp.where(found[q] == key, q, twin)
        found.append(key)
        info_s[p] = jnp.where(live, jnp.where(twin >= 0, 3, level), 0)
        info_s[slots + p] = source
        info_s[2 * slots + p] = orient
        info_s[3 * slots + p] = jnp.maximum(twin, 0)
        for k in range(6):
            need[k] = need[k] | (live & (source == k))
    for k in range(6):
        info_s[4 * slots + k] = need[k].astype(jnp.int32)


def needed(info_s, slots):
    return [[info_s[4 * slots + level * 3 + orient] > 0 for orient in range(3)] for level in range(2)]


def filter_rows(level, span, w_first, grid_ref, low_ref, low_lhs):
    place, count = span
    tiles = count if level == 0 else (count + 3) // 4
    for r in range(tiles):
        if level == 0:
            value = grid_ref[place + r]
        else:
            value = jnp.concatenate([grid_ref[place + 4 * r + n, pl.ds(0, 8, stride=2), :] for n in (0, 2)], axis=0)
        high, rest = split(value)
        low_lhs[r * 16:r * 16 + 16, 0:128] = high
        low_lhs[r * 16:r * 16 + 16, 128:256] = rest
    z = dot(low_lhs[0:tiles * 16, :], w_first[level, :, 0:256])
    z = z[:, 0:128] + z[:, 128:256]
    if level == 0:
        low_ref[pl.ds(place, tiles)] = z.reshape(tiles, 16, 128)
    else:
        low_ref[pl.ds(place // 2, 2 * tiles)] = z.reshape(2 * tiles, 8, 128)


def first_rows(need, spans, starts, edge, tile_rows, taps_ref, w_first, grid_ref, low_refs, m_ref, low_lhs, z_ref):
    rank = lax.axis_index("space")
    total = lax.axis_size("space") * tile_rows

    def x_pass(level, kind, n, start):
        taps = [taps_ref[kind, t] for t in range(TAPS)]
        skip = edge[level] if n == 0 else 0
        stride = 2 - level
        parts = []
        for h in range(2 - level):
            sums = [None] * 8
            for r in range(stride * skip, stride * 7 + TAPS):
                if level == 0:
                    ref = low_refs[0] if kind == BOTH else grid_ref
                    value = ref[2 * start + HALF + FRONT + r, 8 * h:8 * h + 8, :]
                elif kind == BOTH:
                    value = low_refs[1][start + r + FRONT // 2]
                else:
                    value = grid_ref[2 * (start + r) + FRONT, pl.ds(0, 8, stride=2), :]
                for i in range(skip, 8):
                    t = r - stride * i
                    if 0 <= t < TAPS:
                        term = taps[t] * value
                        sums[i] = term if sums[i] is None else sums[i] + term
            parts.append(sums)
        if level == 0:
            return [(i * 16, jnp.concatenate([parts[0][i], parts[1][i]], axis=0)) for i in range(skip, 8)]
        return [(i * 8, jnp.concatenate([parts[0][i], parts[0][i + 1]], axis=0)) for i in range(skip, 8, 2)]

    def finish(level, orient, n):
        height = 16 >> level
        start = starts[level][n]
        taps = taps_ref.at[BOTH if orient == 1 else LOW]
        place = m_ref.at[level * 3 + orient].reshape(STORED * 8, 128)
        values = [z_ref[orient, pl.ds(n * 8 * height + y, 8, stride=height), :] for y in range(height)]
        i = start + rows(TILE)
        x = rank * tile_rows - 28 + 2 * i
        inside = (x >= 0) & (x < total) & (i >= 0) & (i < KEPT)
        for j in range(8):
            terms = [(y - (2 - level) * j + HALF, y) for y in range(height)]
            out = modulus(weigh(taps, values, [(t, y) for t, y in terms if 0 <= t < TAPS]))
            place[pl.ds((start + SHIFT) * 8 + j, 8, stride=8), :] = jnp.where(inside, out, 0.0)

    def chunk_by_chunk(level, orients, begin):
        count = len(starts[level])
        for n in range(count + 1):
            if n < count:
                begin(n)
            if n > 0:
                for orient in orients:
                    finish(level, orient, n - 1)

    for level in range(2):
        per = 128 >> level
        one, two = need[level][1], need[level][2]

        def filtered(orients):
            columns = slice(256 * (orients[0] - 1), 256 * orients[-1])

            def begin(n):
                for at, value in x_pass(level, LOW, n, starts[level][n]):
                    high, rest = split(value)
                    at += n * per
                    low_lhs[at:at + 16, 0:128] = high
                    low_lhs[at:at + 16, 128:256] = rest
                first, end = n * per + (edge[level] * (16 >> level) if n == 0 else 0), (n + 1) * per
                z = dot(low_lhs[first:end, :], w_first[level, :, columns])
                for k, orient in enumerate(orients):
                    z_ref[orient, first:end, :] = z[:, 256 * k:256 * k + 128] + z[:, 256 * k + 128:256 * k + 256]

            chunk_by_chunk(level, orients, begin)

        @pl.when(one & two)
        def _():
            filtered((1, 2))

        @pl.when(one & jnp.logical_not(two))
        def _():
            filtered((1,))

        @pl.when(two & jnp.logical_not(one))
        def _():
            filtered((2,))

        @pl.when(need[level][0])
        def _():
            def begin(n):
                for at, value in x_pass(level, BOTH, n, starts[level][n]):
                    z_ref[0, n * per + at:n * per + at + 16, :] = value

            filter_rows(level, spans[level], w_first, grid_ref, low_refs[level], low_lhs)
            chunk_by_chunk(level, (0,), begin)


def pack_rows(need, blocks, m_ref, lhs_ref):
    left = lanes((16, 128)) < 64
    for level in range(2):
        for orient in range(3):
            @pl.when(need[level][orient])
            def _():
                source = level * 3 + orient
                at = 0
                for first, end in blocks[level]:
                    for i in range(first, end, 2):
                        value = jnp.concatenate([m_ref[source, i + SHIFT], m_ref[source, i + 1 + SHIFT]], axis=0)
                        high = value.astype(BF16)
                        wide = high.astype(F32)
                        lhs_ref[source, at:at + 16, 0:128] = jnp.where(left, wide, value - wide).astype(BF16)
                        lhs_ref[source, at:at + 16, 128:256] = high
                        at += 16


def every_pair(slots, info_s, w_second, lhs_ref, z_even, z_odd, live, other):
    def z_pass(p, place):
        kind = 2 * (info_s[p] == 2).astype(jnp.int32) + (info_s[2 * slots + p] == 2).astype(jnp.int32)
        place[...] = dot(lhs_ref[info_s[slots + p]], w_second[kind]).reshape(place.shape)

    def one_pair(p, here, there):
        mode, source = info_s[p], info_s[slots + p]
        following = jnp.minimum(p + 1, slots - 1)
        for dilation, level in ((1, 0), (2, 0), (2, 1)):
            @pl.when((mode == dilation) & ((source >= 3) == (level == 1)))
            def _():
                z_pass(following, there)
                live(p, here, dilation, level)

        @pl.when(mode == 3)
        def _():
            z_pass(following, there)

        other(p, mode)

    def two_pairs(k, carry):
        one_pair(2 * k, z_even, z_odd)
        one_pair(2 * k + 1, z_odd, z_even)
        return carry

    z_pass(0, z_even)
    lax.fori_loop(0, slots // 2, two_pairs, 0)


def x_sums(taps, first, dilation, sums, have, read):
    for r in range(first, first + 16 + 14 * dilation):
        if have(r):
            value = read(r)
            for i in range(16):
                if (r - first - i) % dilation == 0 and 0 <= (r - first - i) // dilation < TAPS:
                    term = taps[(r - first - i) // dilation] * value
                    sums[i] = term if sums[i] is None else sums[i] + term
    return sums


def inner_sums(need, slots, info_s, taps_ref, w_second, m_ref, part_ref, lhs_ref, z_even, z_odd):
    pack_rows(need, [[(low, high)] for low, high in KNOWN], m_ref, lhs_ref)

    def live(p, here, dilation, level):
        taps_at = taps_ref.at[jnp.where(info_s[2 * slots + p] == 0, BOTH, LOW)]
        taps = [taps_at[t] for t in range(TAPS)]
        low, high = KNOWN[level]
        for c in range(0, 32, 16):
            sums = x_sums(taps, c + 14 - HALF * dilation, dilation, [None] * 16, lambda r: low <= r < high, lambda r: here[r - low])
            for i in range(16):
                part_ref[p, c + i] = sums[i]

    every_pair(slots, info_s, w_second, lhs_ref, z_even, z_odd, live, lambda p, mode: None)


def second_order(need, slots, info_s, taps_ref, w_second, m_ref, part_ref, out_ref, lhs_ref, z_even, z_odd, line_ref, done_ref, sems):
    pack_rows(need, OUTER, m_ref, lhs_ref)
    half = done_ref.shape[1] // 2

    def copy(p, h):
        rows_at = pl.ds(h * half, half)
        return pltpu.make_async_copy(done_ref.at[p, rows_at], out_ref.at[p, rows_at], sems.at[p, h])

    def live(p, here, dilation, level):
        orient = info_s[2 * slots + p]
        x_taps = taps_ref.at[jnp.where(orient == 0, BOTH, LOW)]
        y_taps = taps_ref.at[jnp.where(orient == 1, BOTH, LOW)]
        place = done_ref.at[p].reshape(done_ref.shape[1] * 8, 64)
        low, high = KNOWN[level]
        (_, split_at), (rest, _) = OUTER[level]
        taps = [x_taps[t] for t in range(TAPS)]
        for c in range(0, 32, 16):
            sums = x_sums(
                taps, c + 14 - HALF * dilation, dilation, [part_ref[p, c + i] for i in range(16)],
                lambda r: not low <= r < high, lambda r: here[r if r < low else r - rest + split_at],
            )
            for i in range(16):
                line_ref[(c + i) * 8:(c + i) * 8 + 8, :] = sums[i]
            for c in (c // 8, c // 8 + 1):
                lines = [line_ref[pl.ds(c * 64 + y, 8, stride=8), :] for y in range(8)]
                for j in range(8):
                    terms = [((y - j) // dilation + HALF, y) for y in range(8) if (y - j) % dilation == 0]
                    out = modulus(weigh(y_taps, lines, terms))
                    place[pl.ds(c * 64 + j, 8, stride=8), :] = out[:, 0:64]
            copy(p, c // 2).start()

    def other(p, mode):
        @pl.when((mode == 0) | (mode == 3))
        def _():
            @pl.when(mode == 3)
            def _():
                done_ref[p] = done_ref[info_s[3 * slots + p]]

            @pl.when(mode == 0)
            def _():
                done_ref[p] = jnp.zeros(done_ref.shape[1:], F32)

            for h in range(2):
                copy(p, h).start()

    every_pair(slots, info_s, w_second, lhs_ref, z_even, z_odd, live, other)
    for p in range(slots):
        for h in range(2):
            copy(p, h).wait()


def pack_body(own_ref, sent_ref, rows_ref, sems):
    upper = lax.axis_index("wave") % 2
    tile_rows = own_ref.shape[0]
    copies = []
    for n in range(0, NEAR, PIECE):
        source = own_ref.at[pl.ds(upper * (tile_rows - NEAR) + n, PIECE)]
        copies.append(pltpu.make_async_copy(source, sent_ref.at[n:n + PIECE], sems.at[BEYOND + n // PIECE]))
    for k in range(BEYOND):
        row = jnp.where(upper == 1, tile_rows - NEAR - 1 - 2 * k, NEAR + 1 + 2 * k)
        copies.append(pltpu.make_async_copy(own_ref.at[pl.ds(row, 1)], rows_ref.at[k:k + 1], sems.at[k]))
    for copy in copies:
        copy.start()
    for copy in copies[-BEYOND:]:
        copy.wait()
    for k in range(BEYOND):
        sent_ref[NEAR + k // 2, 8 * (k % 2):8 * (k % 2) + 8, :] = rows_ref[k, pl.ds(0, 8, stride=2), :]
    for copy in copies[:-BEYOND]:
        copy.wait()


def inner_body(
    even_ref, odd_ref, low_ref, wave_ref, pairs_ref, own_ref,
    taps_ref, w_first, w_second, grid_ref, low_zero, low_one, m_ref, part_ref, info_s,
    even_s, odd_s, low_s, wave_s, pairs_s, low_lhs, z_ref, lhs_second, z2_even, z2_odd, sems, *, slots,
):
    tile_rows = own_ref.shape[0]
    moves = (
        (even_ref, even_s), (odd_ref, odd_s), (low_ref, low_s), (wave_ref, wave_s), (pairs_ref, pairs_s),
        (own_ref, grid_ref.at[pl.ds(FRONT + HALO, tile_rows)]),
    )
    copies = [pltpu.make_async_copy(source, place, sems.at[n]) for n, (source, place) in enumerate(moves)]
    for copy in copies:
        copy.start()
    for copy in copies[:-1]:
        copy.wait()
    make_filters(even_s, odd_s, low_s, taps_ref, w_first, w_second)
    read_tables(wave_s, pairs_s, lax.axis_index("wave") * slots, slots, info_s)
    copies[-1].wait()
    need = needed(info_s, slots)
    low_refs = (low_zero, low_one)
    spans = [(FRONT + HALO, tile_rows)] * 2
    first_rows(need, spans, INNER, (0, 0), tile_rows, taps_ref, w_first, grid_ref, low_refs, m_ref, low_lhs, z_ref)
    inner_sums(need, slots, info_s, taps_ref, w_second, m_ref, part_ref, lhs_second, z2_even, z2_odd)


def add_side(side, info_s, halo_ref, taps_ref, w_first, grid_ref, low_refs, m_ref, low_lhs, z_ref, slots, tile_rows):
    far = FRONT + HALO + tile_rows
    near = jnp.where(side == 1, FRONT + HALO - NEAR, far)
    for r in range(NEAR):
        grid_ref[near + r] = halo_ref[r]
    for k in range(BEYOND):
        row = jnp.where(side == 1, FRONT + HALO - NEAR - 1 - 2 * k, far + NEAR + 1 + 2 * k)
        grid_ref[row, pl.ds(0, 8, stride=2), :] = halo_ref[NEAR + k // 2, 8 * (k % 2):8 * (k % 2) + 8, :]
    need = needed(info_s, slots)
    spans = [(near, NEAR), (jnp.where(side == 1, FRONT, far), HALO)]
    starts = [[jnp.where(side == 1, x, y) for x, y in zip(*both)] for both in zip(BEFORE, AFTER)]
    first_rows(need, spans, starts, EDGE, tile_rows, taps_ref, w_first, grid_ref, low_refs, m_ref, low_lhs, z_ref)
    return need


def side_body(
    info_s, got_ref, taps_ref, w_first, grid_in, zero_in, one_in, m_in,
    grid_ref, low_zero, low_one, m_ref, low_lhs, z_ref, *, slots, tile_rows,
):
    side = lax.axis_index("wave") % 2
    add_side(side, info_s, got_ref, taps_ref, w_first, grid_ref, (low_zero, low_one), m_ref, low_lhs, z_ref, slots, tile_rows)


def last_body(
    info_s, other_ref, taps_ref, w_first, grid_in, zero_in, one_in, m_in, w_second, part_ref,
    out_ref, grid_ref, low_zero, low_one, m_ref, low_lhs, z_ref, lhs_second, z2_even, z2_odd, line_ref, done_ref, sems,
    *, slots, tile_rows,
):
    side = 1 - lax.axis_index("wave") % 2
    need = add_side(side, info_s, other_ref, taps_ref, w_first, grid_ref, (low_zero, low_one), m_ref, low_lhs, z_ref, slots, tile_rows)
    second_order(need, slots, info_s, taps_ref, w_second, m_ref, part_ref, out_ref, lhs_second, z2_even, z2_odd, line_ref, done_ref, sems)


def shards(density, even_taps, odd_taps, low_taps, wavelets, pairs):
    tile_rows, ny, nz = density.shape
    count, waves = lax.axis_size("space"), lax.axis_size("wave")
    slots = pairs.shape[0] // waves
    step = (-1, 1)
    moves = [
        (z * waves + w, (z + step[w % 2]) * waves + w)
        for z in range(count)
        for w in range(waves)
        if 0 <= z + step[w % 2] < count
    ]
    smem = pl.BlockSpec(memory_space=pltpu.SMEM)
    vmem = pl.BlockSpec(memory_space=pltpu.VMEM)
    anywhere = pl.BlockSpec(memory_space=pl.ANY)
    params = pltpu.CompilerParams(vmem_limit_bytes=24 * 1024 * 1024)

    def held(value):
        return pltpu.with_memory_space_constraint(value, pltpu.VMEM)

    def far(value):
        return pltpu.with_memory_space_constraint(value, pltpu.HBM)

    def cost(us):
        return pl.CostEstimate(flops=us * 1000000000, bytes_accessed=us * 2500000, transcendentals=0)

    density = far(density)
    sent = pl.pallas_call(
        pack_body,
        out_shape=pltpu.VMEM((SENT, ny, nz), F32),
        in_specs=[anywhere],
        out_specs=vmem,
        scratch_shapes=[pltpu.VMEM((BEYOND, ny, nz), F32), pltpu.SemaphoreType.DMA((BEYOND + NEAR // PIECE,))],
        compiler_params=params,
        name="pack_halo",
    )(density)
    got = lax.ppermute(sent, ("space", "wave"), moves)
    state_types = [
        pltpu.VMEM((WINDOW, ny, nz), F32),
        pltpu.VMEM((WINDOW, ny, nz), F32),
        pltpu.VMEM((WINDOW // 2, ny // 2, nz), F32),
        pltpu.VMEM((6, STORED, 8, 128), F32),
    ]
    part_type = pltpu.VMEM((slots, tile_rows // 2, 8, 128), F32)
    out_shape = (slots, tile_rows // 2, ny // 2, nz // 2)
    scratch = [pltpu.VMEM((1024, 256), BF16), pltpu.VMEM((3, 384, 128), F32)]
    taps, w_first, w_second, *state, part, info = pl.pallas_call(
        functools.partial(inner_body, slots=slots),
        out_shape=[
            pltpu.VMEM((4, 16, 8, 128), F32),
            pltpu.VMEM((2, 256, 512), BF16),
            pltpu.VMEM((4, 256, 128), BF16),
            *state_types,
            part_type,
            pltpu.SMEM((4 * slots + 8,), jnp.int32),
        ],
        in_specs=[anywhere] * 6,
        out_specs=[vmem] * 8 + [smem],
        scratch_shapes=[
            pltpu.SMEM((TAPS,), F32),
            pltpu.SMEM((TAPS,), F32),
            pltpu.SMEM((TAPS,), F32),
            pltpu.SMEM(wavelets.shape[::-1], jnp.int32),
            pltpu.SMEM(pairs.shape[::-1], jnp.int32),
            *scratch,
            pltpu.VMEM((6, 24 * 8, 256), BF16),
            pltpu.VMEM((24, 8, 128), F32),
            pltpu.VMEM((24, 8, 128), F32),
            pltpu.SemaphoreType.DMA((6,)),
        ],
        compiler_params=params,
        cost_estimate=cost(3),
        name="inner_rows",
    )(*map(far, (even_taps, odd_taps, low_taps, wavelets.T, pairs.T)), density)
    got, state[0] = lax.optimization_barrier((got, state[0]))
    other = lax.ppermute(got, "wave", [(w, w ^ 1) for w in range(waves)])
    taps, w_first, w_second = map(held, (taps, w_first, w_second))
    info = pltpu.with_memory_space_constraint(info, pltpu.SMEM)
    state = pl.pallas_call(
        functools.partial(side_body, slots=slots, tile_rows=tile_rows),
        out_shape=state_types,
        in_specs=[smem] + [vmem] * 7,
        out_specs=[vmem] * 4,
        input_output_aliases={4: 0, 5: 1, 6: 2, 7: 3},
        scratch_shapes=scratch,
        compiler_params=params,
        cost_estimate=cost(2),
        name="side_rows",
    )(info, held(got), taps, w_first, *map(held, state))
    second, *_ = pl.pallas_call(
        functools.partial(last_body, slots=slots, tile_rows=tile_rows),
        out_shape=[jax.ShapeDtypeStruct(out_shape, F32), *state_types],
        in_specs=[smem] + [vmem] * 9,
        out_specs=[anywhere] + [vmem] * 4,
        input_output_aliases={4: 1, 5: 2, 6: 3, 7: 4},
        scratch_shapes=scratch + [
            pltpu.VMEM((6, 46 * 8, 256), BF16),
            pltpu.VMEM((46, 8, 128), F32),
            pltpu.VMEM((46, 8, 128), F32),
            pltpu.VMEM((256, 128), F32),
            pltpu.VMEM(out_shape, F32),
            pltpu.SemaphoreType.DMA((slots, 2)),
        ],
        compiler_params=params,
        cost_estimate=cost(5),
        name="side_rows_and_pairs",
    )(info, held(other), taps, w_first, *map(held, state), w_second, held(part))
    return second


def solution(mesh):
    placed = (P(("groups", "space"), None, None), P(), P(), P(), P(), P())
    return jax.shard_map(
        shards,
        mesh=mesh,
        in_specs=placed,
        out_specs=P("wave", ("groups", "space"), None, None),
        check_vma=False,
    )
```

```python
import functools

import jax
import jax.numpy as jnp
from jax import lax
from jax.experimental import pallas as pl
from jax.experimental.pallas import tpu as pltpu
from jax.sharding import PartitionSpec as P

TAPS = 15
HALF = 7
HALO = 42
NEAR = 35
BEYOND = 4
SENT = NEAR + BEYOND // 2
PIECE = 5
FRONT = 8
WINDOW = 160
KEPT = 60
STORED = 72
SHIFT = 6
INNER = ((18, 26, 34), (21, 29))
BEFORE = ((-6, 2, 10), (-3, 5, 13))
AFTER = ((52, 42, 50), (36, 44, 52))
KNOWN = ((18, 42), (21, 37))
OUTER = (((0, 18), (42, 60)), ((0, 22), (36, 60)))
EDGE = (6, 0)
EPS = 1e-6
F32 = jnp.float32
BF16 = jnp.bfloat16
LOW, EVEN, ODD, BOTH = 0, 1, 2, 3
TILE = (8, 128)


def split(value):
    high = value.astype(BF16)
    return high, (value - high.astype(F32)).astype(BF16)


def dot(a, b):
    return jnp.dot(a, b, preferred_element_type=F32)


def rows(shape):
    return lax.broadcasted_iota(jnp.int32, shape, 0)


def lanes(shape):
    return lax.broadcasted_iota(jnp.int32, shape, 1)


def modulus(value):
    squares = value * value
    total = squares + pltpu.roll(squares, 64, 1) + EPS
    return total * lax.rsqrt(total)


def weigh(taps, values, pairs):
    acc = None
    for t, v in pairs:
        term = taps[t] * values[v]
        acc = term if acc is None else acc + term
    return acc


def banded(taps_ref, offset, dilation):
    low = both = jnp.zeros(offset.shape, F32)
    for t in range(TAPS):
        here = offset == (t - HALF) * dilation
        low = jnp.where(here, taps_ref[LOW, t][0:1], low)
        both = jnp.where(here, taps_ref[BOTH, t][0:1], both)
    return low, both


def make_filters(even_s, odd_s, low_s, taps_ref, w_first, w_second):
    left = lanes(TILE) < 64
    for t in range(TAPS):
        even = jnp.full(TILE, even_s[t], F32)
        odd = jnp.full(TILE, odd_s[t], F32)
        taps_ref[LOW, t] = jnp.full(TILE, low_s[t], F32)
        taps_ref[EVEN, t] = even
        taps_ref[ODD, t] = odd
        taps_ref[BOTH, t] = jnp.where(left, even, odd)
    wide = (128, 128)
    none = jnp.zeros(wide, BF16)
    for level in range(2):
        low, both = banded(taps_ref, rows(wide) - 2 * (lanes(wide) % 64), 1 << level)
        for kind, matrix in enumerate((low, both)):
            high, rest = split(matrix)
            column = 256 * kind
            w_first[level, 0:128, column:column + 128] = high
            w_first[level, 128:256, column:column + 128] = high
            w_first[level, 0:128, column + 128:column + 256] = rest
            w_first[level, 128:256, column + 128:column + 256] = none
        half = (64, 128)
        low, both = banded(taps_ref, rows(half) - lanes(half) % 64, 1 << level)
        for kind, matrix in enumerate((low, both)):
            high, rest = split(matrix)
            w_second[2 * level + kind, 0:64] = high
            w_second[2 * level + kind, 64:128] = high
            w_second[2 * level + kind, 128:192] = rest
            w_second[2 * level + kind, 192:256] = jnp.zeros(half, BF16)


def read_tables(wave_s, pairs_s, base, slots, info_s):
    found = []
    need = [False] * 6
    for p in range(slots):
        field, wavelet = pairs_s[0, base + p], pairs_s[1, base + p]
        safe = jnp.maximum(field, 0)
        live = field >= 0
        source = wave_s[0, safe] * 3 + wave_s[1, safe]
        level, orient = wave_s[0, wavelet], wave_s[1, wavelet]
        key = jnp.where(live, (source * 4 + level) * 4 + orient, -1)
        twin = jnp.int32(-1)
        for q in range(p - 1, -1, -1):
            twin = jnp.where(found[q] == key, q, twin)
        found.append(key)
        info_s[p] = jnp.where(live, jnp.where(twin >= 0, 3, level), 0)
        info_s[slots + p] = source
        info_s[2 * slots + p] = orient
        info_s[3 * slots + p] = jnp.maximum(twin, 0)
        for k in range(6):
            need[k] = need[k] | (live & (source == k))
    for k in range(6):
        info_s[4 * slots + k] = need[k].astype(jnp.int32)


def needed(info_s, slots):
    return [[info_s[4 * slots + level * 3 + orient] > 0 for orient in range(3)] for level in range(2)]


def filter_rows(level, span, w_first, grid_ref, low_ref, low_lhs):
    place, count = span
    tiles = count if level == 0 else (count + 3) // 4
    for r in range(tiles):
        if level == 0:
            value = grid_ref[place + r]
        else:
            value = jnp.concatenate([grid_ref[place + 4 * r + n, pl.ds(0, 8, stride=2), :] for n in (0, 2)], axis=0)
        high, rest = split(value)
        low_lhs[r * 16:r * 16 + 16, 0:128] = high
        low_lhs[r * 16:r * 16 + 16, 128:256] = rest
    z = dot(low_lhs[0:tiles * 16, :], w_first[level, :, 0:256])
    z = z[:, 0:128] + z[:, 128:256]
    if level == 0:
        low_ref[pl.ds(place, tiles)] = z.reshape(tiles, 16, 128)
    else:
        low_ref[pl.ds(place // 2, 2 * tiles)] = z.reshape(2 * tiles, 8, 128)


def first_rows(need, spans, starts, edge, tile_rows, taps_ref, w_first, grid_ref, low_refs, m_ref, low_lhs, z_ref):
    rank = lax.axis_index("space")
    total = lax.axis_size("space") * tile_rows

    def x_pass(level, kind, n, start):
        taps = [taps_ref[kind, t] for t in range(TAPS)]
        skip = edge[level] if n == 0 else 0
        stride = 2 - level
        parts = []
        for h in range(2 - level):
            sums = [None] * 8
            for r in range(stride * skip, stride * 7 + TAPS):
                if level == 0:
                    ref = low_refs[0] if kind == BOTH else grid_ref
                    value = ref[2 * start + HALF + FRONT + r, 8 * h:8 * h + 8, :]
                elif kind == BOTH:
                    value = low_refs[1][start + r + FRONT // 2]
                else:
                    value = grid_ref[2 * (start + r) + FRONT, pl.ds(0, 8, stride=2), :]
                for i in range(skip, 8):
                    t = r - stride * i
                    if 0 <= t < TAPS:
                        term = taps[t] * value
                        sums[i] = term if sums[i] is None else sums[i] + term
            parts.append(sums)
        if level == 0:
            return [(i * 16, jnp.concatenate([parts[0][i], parts[1][i]], axis=0)) for i in range(skip, 8)]
        return [(i * 8, jnp.concatenate([parts[0][i], parts[0][i + 1]], axis=0)) for i in range(skip, 8, 2)]

    def finish(level, orient, n):
        height = 16 >> level
        start = starts[level][n]
        taps = taps_ref.at[BOTH if orient == 1 else LOW]
        place = m_ref.at[level * 3 + orient].reshape(STORED * 8, 128)
        values = [z_ref[orient, pl.ds(n * 8 * height + y, 8, stride=height), :] for y in range(height)]
        i = start + rows(TILE)
        x = rank * tile_rows - 28 + 2 * i
        inside = (x >= 0) & (x < total) & (i >= 0) & (i < KEPT)
        for j in range(8):
            terms = [(y - (2 - level) * j + HALF, y) for y in range(height)]
            out = modulus(weigh(taps, values, [(t, y) for t, y in terms if 0 <= t < TAPS]))
            place[pl.ds((start + SHIFT) * 8 + j, 8, stride=8), :] = jnp.where(inside, out, 0.0)

    def chunk_by_chunk(level, orients, begin):
        count = len(starts[level])
        for n in range(count + 1):
            if n < count:
                begin(n)
            if n > 0:
                for orient in orients:
                    finish(level, orient, n - 1)

    for level in range(2):
        per = 128 >> level
        one, two = need[level][1], need[level][2]

        def filtered(orients):
            columns = slice(256 * (orients[0] - 1), 256 * orients[-1])

            def begin(n):
                for at, value in x_pass(level, LOW, n, starts[level][n]):
                    high, rest = split(value)
                    at += n * per
                    low_lhs[at:at + 16, 0:128] = high
                    low_lhs[at:at + 16, 128:256] = rest
                first, end = n * per + (edge[level] * (16 >> level) if n == 0 else 0), (n + 1) * per
                z = dot(low_lhs[first:end, :], w_first[level, :, columns])
                for k, orient in enumerate(orients):
                    z_ref[orient, first:end, :] = z[:, 256 * k:256 * k + 128] + z[:, 256 * k + 128:256 * k + 256]

            chunk_by_chunk(level, orients, begin)

        @pl.when(one & two)
        def _():
            filtered((1, 2))

        @pl.when(one & jnp.logical_not(two))
        def _():
            filtered((1,))

        @pl.when(two & jnp.logical_not(one))
        def _():
            filtered((2,))

        @pl.when(need[level][0])
        def _():
            def begin(n):
                for at, value in x_pass(level, BOTH, n, starts[level][n]):
                    z_ref[0, n * per + at:n * per + at + 16, :] = value

            filter_rows(level, spans[level], w_first, grid_ref, low_refs[level], low_lhs)
            chunk_by_chunk(level, (0,), begin)


def pack_rows(need, blocks, m_ref, lhs_ref):
    left = lanes((16, 128)) < 64
    for level in range(2):
        for orient in range(3):
            @pl.when(need[level][orient])
            def _():
                source = level * 3 + orient
                at = 0
                for first, end in blocks[level]:
                    for i in range(first, end, 2):
                        value = jnp.concatenate([m_ref[source, i + SHIFT], m_ref[source, i + 1 + SHIFT]], axis=0)
                        high = value.astype(BF16)
                        wide = high.astype(F32)
                        lhs_ref[source, at:at + 16, 0:128] = jnp.where(left, wide, value - wide).astype(BF16)
                        lhs_ref[source, at:at + 16, 128:256] = high
                        at += 16


def every_pair(slots, info_s, w_second, lhs_ref, z_even, z_odd, live, other):
    def z_pass(p, place):
        kind = 2 * (info_s[p] == 2).astype(jnp.int32) + (info_s[2 * slots + p] == 2).astype(jnp.int32)
        place[...] = dot(lhs_ref[info_s[slots + p]], w_second[kind]).reshape(place.shape)

    def one_pair(p, here, there):
        mode, source = info_s[p], info_s[slots + p]
        following = jnp.minimum(p + 1, slots - 1)
        for dilation, level in ((1, 0), (2, 0), (2, 1)):
            @pl.when((mode == dilation) & ((source >= 3) == (level == 1)))
            def _():
                z_pass(following, there)
                live(p, here, dilation, level)

        @pl.when(mode == 3)
        def _():
            z_pass(following, there)

        other(p, mode)

    def two_pairs(k, carry):
        one_pair(2 * k, z_even, z_odd)
        one_pair(2 * k + 1, z_odd, z_even)
        return carry

    z_pass(0, z_even)
    lax.fori_loop(0, slots // 2, two_pairs, 0)


def x_sums(taps, first, dilation, sums, have, read):
    for r in range(first, first + 16 + 14 * dilation):
        if have(r):
            value = read(r)
            for i in range(16):
                if (r - first - i) % dilation == 0 and 0 <= (r - first - i) // dilation < TAPS:
                    term = taps[(r - first - i) // dilation] * value
                    sums[i] = term if sums[i] is None else sums[i] + term
    return sums


def inner_sums(need, slots, info_s, taps_ref, w_second, m_ref, part_ref, lhs_ref, z_even, z_odd):
    pack_rows(need, [[(low, high)] for low, high in KNOWN], m_ref, lhs_ref)

    def live(p, here, dilation, level):
        taps_at = taps_ref.at[jnp.where(info_s[2 * slots + p] == 0, BOTH, LOW)]
        taps = [taps_at[t] for t in range(TAPS)]
        low, high = KNOWN[level]
        for c in range(0, 32, 16):
            sums = x_sums(taps, c + 14 - HALF * dilation, dilation, [None] * 16, lambda r: low <= r < high, lambda r: here[r - low])
            for i in range(16):
                part_ref[p, c + i] = sums[i]

    every_pair(slots, info_s, w_second, lhs_ref, z_even, z_odd, live, lambda p, mode: None)


def second_order(need, slots, info_s, taps_ref, w_second, m_ref, part_ref, out_ref, lhs_ref, z_even, z_odd, line_ref, done_ref, sems):
    pack_rows(need, OUTER, m_ref, lhs_ref)
    half = done_ref.shape[1] // 2

    def copy(p, h):
        rows_at = pl.ds(h * half, half)
        return pltpu.make_async_copy(done_ref.at[p, rows_at], out_ref.at[p, rows_at], sems.at[p, h])

    def live(p, here, dilation, level):
        orient = info_s[2 * slots + p]
        x_taps = taps_ref.at[jnp.where(orient == 0, BOTH, LOW)]
        y_taps = taps_ref.at[jnp.where(orient == 1, BOTH, LOW)]
        place = done_ref.at[p].reshape(done_ref.shape[1] * 8, 64)
        low, high = KNOWN[level]
        (_, split_at), (rest, _) = OUTER[level]
        taps = [x_taps[t] for t in range(TAPS)]
        for c in range(0, 32, 16):
            sums = x_sums(
                taps, c + 14 - HALF * dilation, dilation, [part_ref[p, c + i] for i in range(16)],
                lambda r: not low <= r < high, lambda r: here[r if r < low else r - rest + split_at],
            )
            for i in range(16):
                line_ref[(c + i) * 8:(c + i) * 8 + 8, :] = sums[i]
        for c in range(4):
            lines = [line_ref[pl.ds(c * 64 + y, 8, stride=8), :] for y in range(8)]
            for j in range(8):
                terms = [((y - j) // dilation + HALF, y) for y in range(8) if (y - j) % dilation == 0]
                out = modulus(weigh(y_taps, lines, terms))
                place[pl.ds(c * 64 + j, 8, stride=8), :] = out[:, 0:64]
            if c % 2:
                copy(p, c // 2).start()

    def other(p, mode):
        @pl.when((mode == 0) | (mode == 3))
        def _():
            @pl.when(mode == 3)
            def _():
                done_ref[p] = done_ref[info_s[3 * slots + p]]

            @pl.when(mode == 0)
            def _():
                done_ref[p] = jnp.zeros(done_ref.shape[1:], F32)

            for h in range(2):
                copy(p, h).start()

    every_pair(slots, info_s, w_second, lhs_ref, z_even, z_odd, live, other)
    for p in range(slots):
        for h in range(2):
            copy(p, h).wait()


def pack_body(own_ref, sent_ref, rows_ref, sems):
    upper = lax.axis_index("wave") % 2
    tile_rows = own_ref.shape[0]
    copies = []
    for n in range(0, NEAR, PIECE):
        source = own_ref.at[pl.ds(upper * (tile_rows - NEAR) + n, PIECE)]
        copies.append(pltpu.make_async_copy(source, sent_ref.at[n:n + PIECE], sems.at[BEYOND + n // PIECE]))
    for k in range(BEYOND):
        row = jnp.where(upper == 1, tile_rows - NEAR - 1 - 2 * k, NEAR + 1 + 2 * k)
        copies.append(pltpu.make_async_copy(own_ref.at[pl.ds(row, 1)], rows_ref.at[k:k + 1], sems.at[k]))
    for copy in copies:
        copy.start()
    for copy in copies[-BEYOND:]:
        copy.wait()
    for k in range(BEYOND):
        sent_ref[NEAR + k // 2, 8 * (k % 2):8 * (k % 2) + 8, :] = rows_ref[k, pl.ds(0, 8, stride=2), :]
    for copy in copies[:-BEYOND]:
        copy.wait()


def inner_body(
    even_ref, odd_ref, low_ref, wave_ref, pairs_ref, own_ref,
    taps_ref, w_first, w_second, grid_ref, low_zero, low_one, m_ref, part_ref, info_s,
    even_s, odd_s, low_s, wave_s, pairs_s, low_lhs, z_ref, lhs_second, z2_even, z2_odd, sems, *, slots,
):
    tile_rows = own_ref.shape[0]
    moves = (
        (even_ref, even_s), (odd_ref, odd_s), (low_ref, low_s), (wave_ref, wave_s), (pairs_ref, pairs_s),
        (own_ref, grid_ref.at[pl.ds(FRONT + HALO, tile_rows)]),
    )
    copies = [pltpu.make_async_copy(source, place, sems.at[n]) for n, (source, place) in enumerate(moves)]
    for copy in copies:
        copy.start()
    for copy in copies[:-1]:
        copy.wait()
    make_filters(even_s, odd_s, low_s, taps_ref, w_first, w_second)
    read_tables(wave_s, pairs_s, lax.axis_index("wave") * slots, slots, info_s)
    copies[-1].wait()
    need = needed(info_s, slots)
    low_refs = (low_zero, low_one)
    spans = [(FRONT + HALO, tile_rows)] * 2
    first_rows(need, spans, INNER, (0, 0), tile_rows, taps_ref, w_first, grid_ref, low_refs, m_ref, low_lhs, z_ref)
    inner_sums(need, slots, info_s, taps_ref, w_second, m_ref, part_ref, lhs_second, z2_even, z2_odd)


def add_side(side, info_s, halo_ref, taps_ref, w_first, grid_ref, low_refs, m_ref, low_lhs, z_ref, slots, tile_rows):
    far = FRONT + HALO + tile_rows
    near = jnp.where(side == 1, FRONT + HALO - NEAR, far)
    for r in range(NEAR):
        grid_ref[near + r] = halo_ref[r]
    for k in range(BEYOND):
        row = jnp.where(side == 1, FRONT + HALO - NEAR - 1 - 2 * k, far + NEAR + 1 + 2 * k)
        grid_ref[row, pl.ds(0, 8, stride=2), :] = halo_ref[NEAR + k // 2, 8 * (k % 2):8 * (k % 2) + 8, :]
    need = needed(info_s, slots)
    spans = [(near, NEAR), (jnp.where(side == 1, FRONT, far), HALO)]
    starts = [[jnp.where(side == 1, x, y) for x, y in zip(*both)] for both in zip(BEFORE, AFTER)]
    first_rows(need, spans, starts, EDGE, tile_rows, taps_ref, w_first, grid_ref, low_refs, m_ref, low_lhs, z_ref)
    return need


def side_body(
    info_s, got_ref, taps_ref, w_first, grid_in, zero_in, one_in, m_in,
    grid_ref, low_zero, low_one, m_ref, low_lhs, z_ref, *, slots, tile_rows,
):
    side = lax.axis_index("wave") % 2
    add_side(side, info_s, got_ref, taps_ref, w_first, grid_ref, (low_zero, low_one), m_ref, low_lhs, z_ref, slots, tile_rows)


def last_body(
    info_s, other_ref, taps_ref, w_first, grid_in, zero_in, one_in, m_in, w_second, part_ref,
    out_ref, grid_ref, low_zero, low_one, m_ref, low_lhs, z_ref, lhs_second, z2_even, z2_odd, line_ref, done_ref, sems,
    *, slots, tile_rows,
):
    side = 1 - lax.axis_index("wave") % 2
    need = add_side(side, info_s, other_ref, taps_ref, w_first, grid_ref, (low_zero, low_one), m_ref, low_lhs, z_ref, slots, tile_rows)
    second_order(need, slots, info_s, taps_ref, w_second, m_ref, part_ref, out_ref, lhs_second, z2_even, z2_odd, line_ref, done_ref, sems)


def shards(density, even_taps, odd_taps, low_taps, wavelets, pairs):
    tile_rows, ny, nz = density.shape
    count, waves = lax.axis_size("space"), lax.axis_size("wave")
    slots = pairs.shape[0] // waves
    step = (-1, 1)
    moves = [
        (z * waves + w, (z + step[w % 2]) * waves + w)
        for z in range(count)
        for w in range(waves)
        if 0 <= z + step[w % 2] < count
    ]
    smem = pl.BlockSpec(memory_space=pltpu.SMEM)
    vmem = pl.BlockSpec(memory_space=pltpu.VMEM)
    anywhere = pl.BlockSpec(memory_space=pl.ANY)
    params = pltpu.CompilerParams(vmem_limit_bytes=24 * 1024 * 1024)

    def held(value):
        return pltpu.with_memory_space_constraint(value, pltpu.VMEM)

    def far(value):
        return pltpu.with_memory_space_constraint(value, pltpu.HBM)

    def cost(us):
        return pl.CostEstimate(flops=us * 1000000000, bytes_accessed=us * 2500000, transcendentals=0)

    density = far(density)
    sent = pl.pallas_call(
        pack_body,
        out_shape=pltpu.VMEM((SENT, ny, nz), F32),
        in_specs=[anywhere],
        out_specs=vmem,
        scratch_shapes=[pltpu.VMEM((BEYOND, ny, nz), F32), pltpu.SemaphoreType.DMA((BEYOND + NEAR // PIECE,))],
        compiler_params=params,
        name="pack_halo",
    )(density)
    got = lax.ppermute(sent, ("space", "wave"), moves)
    state_types = [
        pltpu.VMEM((WINDOW, ny, nz), F32),
        pltpu.VMEM((WINDOW, ny, nz), F32),
        pltpu.VMEM((WINDOW // 2, ny // 2, nz), F32),
        pltpu.VMEM((6, STORED, 8, 128), F32),
    ]
    part_type = pltpu.VMEM((slots, tile_rows // 2, 8, 128), F32)
    out_shape = (slots, tile_rows // 2, ny // 2, nz // 2)
    scratch = [pltpu.VMEM((1024, 256), BF16), pltpu.VMEM((3, 384, 128), F32)]
    taps, w_first, w_second, *state, part, info = pl.pallas_call(
        functools.partial(inner_body, slots=slots),
        out_shape=[
            pltpu.VMEM((4, 16, 8, 128), F32),
            pltpu.VMEM((2, 256, 512), BF16),
            pltpu.VMEM((4, 256, 128), BF16),
            *state_types,
            part_type,
            pltpu.SMEM((4 * slots + 8,), jnp.int32),
        ],
        in_specs=[anywhere] * 6,
        out_specs=[vmem] * 8 + [smem],
        scratch_shapes=[
            pltpu.SMEM((TAPS,), F32),
            pltpu.SMEM((TAPS,), F32),
            pltpu.SMEM((TAPS,), F32),
            pltpu.SMEM(wavelets.shape[::-1], jnp.int32),
            pltpu.SMEM(pairs.shape[::-1], jnp.int32),
            *scratch,
            pltpu.VMEM((6, 24 * 8, 256), BF16),
            pltpu.VMEM((24, 8, 128), F32),
            pltpu.VMEM((24, 8, 128), F32),
            pltpu.SemaphoreType.DMA((6,)),
        ],
        compiler_params=params,
        cost_estimate=cost(3),
        name="inner_rows",
    )(*map(far, (even_taps, odd_taps, low_taps, wavelets.T, pairs.T)), density)
    got, state[0] = lax.optimization_barrier((got, state[0]))
    other = lax.ppermute(got, "wave", [(w, w ^ 1) for w in range(waves)])
    taps, w_first, w_second = map(held, (taps, w_first, w_second))
    info = pltpu.with_memory_space_constraint(info, pltpu.SMEM)
    state = pl.pallas_call(
        functools.partial(side_body, slots=slots, tile_rows=tile_rows),
        out_shape=state_types,
        in_specs=[smem] + [vmem] * 7,
        out_specs=[vmem] * 4,
        input_output_aliases={4: 0, 5: 1, 6: 2, 7: 3},
        scratch_shapes=scratch,
        compiler_params=params,
        cost_estimate=cost(2),
        name="side_rows",
    )(info, held(got), taps, w_first, *map(held, state))
    second, *_ = pl.pallas_call(
        functools.partial(last_body, slots=slots, tile_rows=tile_rows),
        out_shape=[jax.ShapeDtypeStruct(out_shape, F32), *state_types],
        in_specs=[smem] + [vmem] * 9,
        out_specs=[anywhere] + [vmem] * 4,
        input_output_aliases={4: 1, 5: 2, 6: 3, 7: 4},
        scratch_shapes=scratch + [
            pltpu.VMEM((6, 46 * 8, 256), BF16),
            pltpu.VMEM((46, 8, 128), F32),
            pltpu.VMEM((46, 8, 128), F32),
            pltpu.VMEM((256, 128), F32),
            pltpu.VMEM(out_shape, F32),
            pltpu.SemaphoreType.DMA((slots, 2)),
        ],
        compiler_params=params,
        cost_estimate=cost(5),
        name="side_rows_and_pairs",
    )(info, held(other), taps, w_first, *map(held, state), w_second, held(part))
    return second


def solution(mesh):
    placed = (P(("groups", "space"), None, None), P(), P(), P(), P(), P())
    return jax.shard_map(
        shards,
        mesh=mesh,
        in_specs=placed,
        out_specs=P("wave", ("groups", "space"), None, None),
        check_vma=False,
    )
```
